32 devices in a mesh: section: 4 (over x, core), dp: 8 (over z, y).
Axes of the slice: x: 2, y: 2, z: 4, core: 2. Of those that a mesh axis runs over, the one named last changes fastest.
Arguments:
- tokens: bfloat16 [2, 8, 1024, 768], P(None, 'dp'), may hold values from -6 to 6
- episodes: int32 [2, 8, 1024], P(None, 'dp'), may hold values from 0 to 7, never falling along the last dimension, each value on 1 to 512 neighbouring positions
- attn_gain: float32 [2, 768], replicated, may hold values from 0.5 to 1.5
- attn_shift: float32 [2, 768], replicated, may hold values from -2 to 2
- qkv_weight: bfloat16 [2, 768, 2304], replicated, may hold values from -0.21875 to 0.21875
- out_weight: bfloat16 [2, 768, 768], replicated, may hold values from -1.75 to 1.75
- out_bias: float32 [2, 768], replicated, may hold values from -2 to 2
- ffn_gain: float32 [2, 768], replicated, may hold values from 0.5 to 1.5
- ffn_shift: float32 [2, 768], replicated, may hold values from -2 to 2
- up_weight: bfloat16 [2, 768, 3072], replicated, may hold values from -0.21875 to 0.21875
- up_bias: float32 [2, 3072], replicated, may hold values from -2 to 2
- down_weight: bfloat16 [2, 3072, 768], replicated, may hold values from -0.109375 to 0.109375
- down_bias: float32 [2, 768], replicated, may hold values from -2 to 2
- cotangent: bfloat16 [2, 8, 1024, 768], P(None, 'dp'), may hold values from -6 to 6
Outputs:
- final_activations: float32 [2, 8, 1024, 768], P(None, 'dp', 'section')
- input_gradient: float32 [2, 8, 1024, 768], P(None, 'dp', 'section')
- grad_attn_gain: float32 [2, 768], P(None, 'dp')
- grad_attn_shift: float32 [2, 768], P(None, 'dp')
- grad_qkv: float32 [2, 768, 2304], P(None, 'dp')
- grad_out: float32 [2, 768, 768], P(None, 'dp')
- grad_out_bias: float32 [2, 768], P(None, 'dp')
- grad_ffn_gain: float32 [2, 768], P(None, 'dp')
- grad_ffn_shift: float32 [2, 768], P(None, 'dp')
- grad_up: float32 [2, 768, 3072], P(None, 'dp')
- grad_up_bias: float32 [2, 3072], P(None, 'dp')
- grad_down: float32 [2, 3072, 768], P(None, 'dp')
- grad_down_bias: float32 [2, 768], P(None, 'dp')
The draws below stay inside these ranges and needn't reach their ends.
Inputs may be any that keep to these rules, and one draw needn't show every extreme that they name: `episodes`: in each window the ids never fall and each id covers 1 to 512 consecutive positions.
All inputs are finite; a program needn't handle non-finite values.
Results may differ from the reference program's by a relative error of at most 0.015.
Values may be sent and summed in bfloat16 or wider, within the bound.
No kernel may reach another device: no remote copies, remote signals or barrier semaphores. Data moves between devices by JAX's collectives and lax.ppermute only.
A program may use at most 640 MiB of HBM per device.

```python
import math
import jax
import jax.numpy as jnp
import numpy as np
from jax import lax

D = 768
HEADS = 12
HEAD_DIM = 64
FF = 3072
SEQ = 1024
MICRO = 2
WINDOWS = 8


def levels(stream_key, shape, cuts, least, largest):
    level = 1.0
    for position, shards_of in cuts:
        draws = jax.random.uniform(jax.random.fold_in(jax.random.fold_in(stream_key, 6), position), (shards_of,), jnp.float32, least / len(cuts), largest / len(cuts))
        level = level * jnp.repeat(jnp.exp(draws), shape[position] // shards_of).reshape((-1,) + (1,) * (len(shape) - 1 - position))
    return level


def profile(number_of, total, reach, skew):
    weights = [(1 << 20) // math.isqrt(grade ** skew) + 1 for grade in range(2, number_of + 1)]
    spare, counts = total - reach - (number_of - 1), [1] * (number_of - 1)
    while spare > 0:
        free = [i for i in range(number_of - 1) if counts[i] < reach]
        pool, left = sum([weights[i] for i in free]), spare
        for i in free:
            addition = min(reach - counts[i], max(1, left * weights[i] // pool), spare)
            counts[i] = counts[i] + addition
            spare = spare - addition
    return np.array([reach] + counts)


def ragged_sizes(own_key, number_of, total, most, slope):
    if number_of == 2:
        one = jax.random.randint(own_key, (), max(1, total - most), min(most, total - 1) + 1)
        return jnp.stack([one, total - one])
    lengths = jnp.asarray(profile(number_of, total, most, slope), jnp.int32)
    pairs = (number_of - 1) // 2
    giver, taker = lengths[1:1 + 2 * pairs:2], lengths[2:2 + 2 * pairs:2]
    margin = jnp.minimum(giver - 1, most - taker)
    shifted = jax.random.randint(jax.random.fold_in(own_key, 1), (pairs,), 0, 1 << 20) % (margin + 1)
    lengths = lengths.at[1:1 + 2 * pairs:2].set(giver - shifted).at[2:2 + 2 * pairs:2].set(taker + shifted)
    return lengths[jax.random.permutation(jax.random.fold_in(own_key, 2), number_of)]


def centred(stream_key, dims, width, bound, pieces=(), held_as=jnp.bfloat16):
    result = width * jax.random.normal(stream_key, dims, jnp.float32)
    if pieces:
        result = result * levels(stream_key, dims, pieces, -0.22, 0.18)
    return jnp.clip(result, -bound, bound).astype(held_as)


def setup_inputs(seed: int = 0) -> dict:
    seeds = jax.random.split(jax.random.key(seed), 15)
    return {
        "tokens": centred(seeds[0], (MICRO, WINDOWS, SEQ, D), 1.0, 6.0, ((1, 8),)),
        "episodes": jax.vmap(lambda own: jnp.searchsorted(jnp.cumsum(ragged_sizes(own, max(4, SEQ // 128), SEQ, SEQ // 2, 1)), jnp.arange(SEQ), side="right"))(jax.random.split(seeds[1], MICRO * WINDOWS)).reshape((MICRO, WINDOWS, SEQ)).astype(jnp.int32),
        "attn_gain": jnp.clip(1.0 + 0.1 * jax.random.normal(seeds[2], (2, D), jnp.float32), 0.5, 1.5),
        "attn_shift": centred(seeds[3], (2, D), 0.3, 2.0, (), jnp.float32),
        "qkv_weight": centred(seeds[4], (2, D, 3 * D), D ** -0.5, 0.21875),
        "out_weight": centred(seeds[5], (2, D, D), (max(8, D // 64)) ** -0.5, 1.75),
        "out_bias": centred(seeds[6], (2, D), 0.3, 2.0, (), jnp.float32),
        "ffn_gain": jnp.clip(1.0 + 0.1 * jax.random.normal(seeds[7], (2, D), jnp.float32), 0.5, 1.5),
        "ffn_shift": centred(seeds[8], (2, D), 0.3, 2.0, (), jnp.float32),
        "up_weight": centred(seeds[9], (2, D, FF), D ** -0.5, 0.21875),
        "up_bias": centred(seeds[10], (2, FF), 0.3, 2.0, (), jnp.float32),
        "down_weight": centred(seeds[11], (2, FF, D), FF ** -0.5, 0.109375),
        "down_bias": centred(seeds[12], (2, D), 0.3, 2.0, (), jnp.float32),
        "cotangent": centred(seeds[13], (MICRO, WINDOWS, SEQ, D), 1.0, 6.0, ((1, 8),)),
    }


PRECISE = lax.Precision.HIGHEST
EPS = 1e-05
MASKED = -1e+30

@jax.custom_vjp
def low(v):
    return lax.optimization_barrier(v.astype(jnp.bfloat16)).astype(jnp.float32)

@jax.custom_vjp
def low_back(v):
    return v

def low_keep(v):
    return (low(v), None)

def low_pass(kept, grad):
    return (grad,)

def back_keep(v):
    return (v, None)

def back_low(kept, grad):
    return (low(grad),)
low.defvjp(low_keep, low_pass)
low_back.defvjp(back_keep, back_low)

def layer_norm(inputs, gain, shift):
    center = inputs - lax.optimization_barrier(jnp.mean(inputs, -1, keepdims=True))
    return center * lax.rsqrt(lax.optimization_barrier(jnp.mean(center * center, -1, keepdims=True)) + EPS) * gain + shift

def boundary(value):
    return low_back(low(value))

def attention_block(inputs, episode, gain, shift, w_qkv, w_out, b_out):
    length = inputs.shape[0]
    normed = low(layer_norm(inputs, gain, shift))
    qkv_rows = low_back(low(jnp.dot(normed, w_qkv, precision=PRECISE)))
    qkv_split = qkv_rows.reshape(length, 3, HEADS, HEAD_DIM)
    places = jnp.arange(length)
    allowed = (places[:, None] >= places[None, :]) & (episode[:, None] == episode[None, :])
    scores = low_back(HEAD_DIM ** (-0.5) * jnp.einsum('qhd,khd->hqk', qkv_split[:, 0], qkv_split[:, 1], precision=PRECISE))
    scores = jnp.where(allowed[None], scores, MASKED)
    row_max = lax.optimization_barrier(jnp.max(scores, -1, keepdims=True))
    exp_scores = jnp.exp(scores - row_max)
    weights = low(exp_scores / lax.optimization_barrier(jnp.sum(exp_scores, -1, keepdims=True)))
    context = jnp.einsum('hqk,khd->qhd', weights, qkv_split[:, 2], precision=PRECISE)
    context = low_back(low(context.reshape(length, HEADS * HEAD_DIM)))
    return inputs + low_back(jnp.dot(context, w_out, precision=PRECISE) + b_out)

def ffn_block(inputs, gain, shift, w_up, b_up, w_down, b_down):
    normed = low(layer_norm(inputs, gain, shift))
    hidden = low_back(jnp.dot(normed, w_up, precision=PRECISE) + b_up)
    active = low(jax.nn.gelu(hidden, approximate=True))
    return inputs + low_back(jnp.dot(active, w_down, precision=PRECISE) + b_down)

def window_pass(params, inputs, episode):
    a_gain, a_shift, w_qkv, w_out, b_out, f_gain, f_shift, w_up, b_up, w_down, b_down = params
    stream = inputs
    for layer_index in range(2):
        stream = attention_block(stream, episode, a_gain[layer_index], a_shift[layer_index], w_qkv[layer_index], w_out[layer_index], b_out[layer_index])
        stream = boundary(stream)
        stream = ffn_block(stream, f_gain[layer_index], f_shift[layer_index], w_up[layer_index], b_up[layer_index], w_down[layer_index], b_down[layer_index])
        if layer_index == 0:
            stream = boundary(stream)
    return stream

def reference(tokens, episodes, attn_gain, attn_shift, qkv_weight, out_weight, out_bias, ffn_gain, ffn_shift, up_weight, up_bias, down_weight, down_bias, cotangent):
    params = tuple((weight.astype(jnp.float32) for weight in (attn_gain, attn_shift, qkv_weight, out_weight, out_bias, ffn_gain, ffn_shift, up_weight, up_bias, down_weight, down_bias)))
    flat_inputs = tokens.astype(jnp.float32).reshape(-1, SEQ, D)
    flat_episodes = episodes.reshape(-1, SEQ)

    def whole(weights_now, inputs_now):

        def window_fn(window_item):
            return window_pass(weights_now, window_item[0], window_item[1])
        return lax.map(jax.checkpoint(window_fn), (inputs_now, flat_episodes))
    outputs, pullback = jax.vjp(whole, params, flat_inputs)
    grads, d_inputs = pullback(cotangent.astype(jnp.float32).reshape(-1, SEQ, D))
    return (outputs.reshape(tokens.shape), d_inputs.reshape(tokens.shape), grads[0], grads[1], grads[2], grads[3], grads[4], grads[5], grads[6], grads[7], grads[8], grads[9], grads[10])
```

```python
from functools import partial

import jax
import jax.numpy as jnp
from jax import lax
from jax.experimental import pallas as pl
from jax.experimental.pallas import tpu as pltpu
from jax.sharding import PartitionSpec as P

BF = jnp.bfloat16
F32 = jnp.float32
EPS = 1e-05
MASKED = -1e30
D = 768
HALF = 384
PAIR = 128
HEAD_DIM = 64
FF = 3072
LENGTH = 1024
BLOCK = 256
ROWS = 512
PART = 96
GELU_A = 0.7978845608028654
GELU_B = GELU_A * 0.044715


def dot(a, b):
    return jnp.dot(a, b, preferred_element_type=F32)


def dot_nt(a, b):
    return lax.dot_general(a, b, (((1,), (1,)), ((), ())), preferred_element_type=F32)


def dot_tn(a, b):
    return lax.dot_general(a, b, (((0,), (0,)), ((), ())), preferred_element_type=F32)


def normalise(rows):
    center = rows - jnp.mean(rows, -1, keepdims=True)
    spread = lax.rsqrt(jnp.mean(center * center, -1, keepdims=True) + EPS)
    return center * spread, spread


def norm_low(rows, gain, shift):
    unit, _ = normalise(rows.astype(F32))
    return (unit * gain + shift).astype(BF)


def call(body, grid, in_specs, out_specs, out_shape, scratch, cost=None):
    return pl.pallas_call(
        body,
        grid_spec=pltpu.PrefetchScalarGridSpec(
            num_scalar_prefetch=1,
            grid=grid,
            in_specs=in_specs,
            out_specs=out_specs,
            scratch_shapes=scratch,
        ),
        out_shape=out_shape,
        compiler_params=pltpu.CompilerParams(vmem_limit_bytes=56 * 1024 * 1024),
        cost_estimate=None
        if cost is None
        else pl.CostEstimate(flops=int(cost[0]), bytes_accessed=int(cost[1]), transcendentals=0),
    )


def shape(dims, dtype):
    return jax.ShapeDtypeStruct(dims, dtype)


def whole(dims):
    count = len(dims)
    return pl.BlockSpec(dims, lambda i, sc: (0,) * count)


def at_layer(dims, layer):
    count = len(dims) - 1
    return pl.BlockSpec(dims, lambda i, sc: (layer,) + (0,) * count)


X, C, Y, Z = 0, 1, 2, 3


def in_order(own, other, block, core):
    return jnp.where(core == block % 2, own[block // 2], other[block // 2])


def episode_columns(ep_ref):
    row = jnp.broadcast_to(ep_ref[...].reshape(1, LENGTH).astype(F32), (PAIR, LENGTH))
    return row, row.T


def first_key(i):
    return max(0, i - 2) * BLOCK


def attn_fwd_body(sc, own, other, ep, gain, shift, wq, wk, wv, qkv, ctx, ctx_own, ctx_oth, lse, bias, vext, lse_cols):
    core = sc[C]
    own, other = own.at[0, :, 0], other.at[0, :, 0]
    for b in range(4):
        rows = slice(b * BLOCK, (b + 1) * BLOCK)
        normed = norm_low(in_order(own, other, b, core), gain[0], shift[0])
        qkv[rows, 0:HALF] = (dot(normed, wq[0]).astype(BF) * 0.125).astype(BF)
        qkv[rows, HALF : 2 * HALF] = dot(normed, wk[0]).astype(BF)
        qkv[rows, 2 * HALF : 3 * HALF] = dot(normed, wv[0]).astype(BF)
    ep_row, ep_col = episode_columns(ep)
    for i in range(4):
        lo, hi = first_key(i), (i + 1) * BLOCK
        key_at = lo + lax.broadcasted_iota(jnp.int32, (BLOCK, hi - lo), 1)
        row_at = i * BLOCK + lax.broadcasted_iota(jnp.int32, (BLOCK, hi - lo), 0)
        same = ep_col[i * BLOCK : hi, 0:1] == ep_row[0:1, lo:hi]
        bias[i, :, 0 : hi - lo] = jnp.where((key_at <= row_at) & same, 0.0, MASKED)
    vext[:, PAIR:] = jnp.ones((LENGTH, PAIR), BF)
    lane = lax.broadcasted_iota(jnp.int32, (BLOCK, PAIR), 1)

    @pl.loop(0, 3)
    def _(p):
        at = pl.multiple_of(p * PAIR, PAIR)
        vext[:, 0:PAIR] = qkv[:, pl.ds(2 * HALF + at, PAIR)]
        for i in range(4):
            lo, hi = first_key(i), (i + 1) * BLOCK
            rows = slice(i * BLOCK, hi)
            q = qkv[rows, pl.ds(at, PAIR)]
            k = qkv[lo:hi, pl.ds(HALF + at, PAIR)]
            outs = []
            for h in range(2):
                mine = (lane >= HEAD_DIM) if h else (lane < HEAD_DIM)
                s = dot_nt(jnp.where(mine, q, jnp.zeros_like(q)), k) + bias[i, :, 0 : hi - lo]
                top = jnp.max(s, -1, keepdims=True)
                prob = jnp.exp(s - top).astype(BF)
                o = dot(prob, vext[lo:hi, :])
                total = o[:, PAIR : PAIR + 1]
                outs.append(o[:, 0:PAIR] / total)
                lse_cols[rows, :] = jnp.where(lane == 2 * p + h, top + jnp.log(total), lse_cols[rows, :])
            ctx[rows, pl.ds(at, PAIR)] = jnp.where(lane < HEAD_DIM, outs[0], outs[1]).astype(BF)

    lse[...] = lse_cols[...].T[0:8]
    for b in range(4):
        piece = ctx[b * BLOCK : (b + 1) * BLOCK]

        @pl.when(core == b % 2)
        def _():
            ctx_own[b // 2] = piece

        @pl.when(core != b % 2)
        def _():
            ctx_oth[b // 2] = piece


def attention_forward(scalars, layer, own, own_spec, other, other_spec, episodes, ep_spec, gain, shift, w_qkv):
    columns = [pl.BlockSpec((1, D, HALF), partial(lambda j, i, sc: (layer, 0, 2 * j + sc[C]), j)) for j in range(3)]
    return call(
        attn_fwd_body,
        (1,),
        [own_spec, other_spec, ep_spec, at_layer((1, 1, D), layer), at_layer((1, 1, D), layer)] + columns,
        [
            whole((LENGTH, 3 * HALF)),
            whole((LENGTH, HALF)),
            whole((2, BLOCK, HALF)),
            whole((2, BLOCK, HALF)),
            whole((8, LENGTH)),
        ],
        [
            shape((LENGTH, 3 * HALF), BF),
            shape((LENGTH, HALF), BF),
            shape((2, BLOCK, HALF), BF),
            shape((2, BLOCK, HALF), BF),
            shape((8, LENGTH), F32),
        ],
        [
            pltpu.VMEM((4, BLOCK, 3 * BLOCK), F32),
            pltpu.VMEM((LENGTH, 2 * PAIR), BF),
            pltpu.VMEM((LENGTH, PAIR), F32),
        ],
        (1.8e9 + 2.4e9, 8e6),
    )(scalars, own, other, episodes, gain, shift, w_qkv, w_qkv, w_qkv)


def gelu_parts(u):
    cubic = GELU_B * (u * u)
    t = jnp.tanh(u * (GELU_A + cubic))
    half = 0.5 * t + 0.5
    active = u * half
    slope = half + (active * (1.0 - half)) * (6.0 * cubic + 2.0 * GELU_A)
    return active, slope


FT = 512


def ffn_fwd_body(last, sc, ctx_own, ctx_rcv, own, w_out, b_out, gain, shift, w_up, b_up, w_down, b_down, *rest):
    if last:
        s2, ctx_full, act, slope, keep, send, normed, acc = rest
    else:
        s2, ctx_full, act, slope, s3, normed, acc = rest
    t = pl.program_id(0)
    core = sc[C]

    @pl.when(t == 0)
    def _():
        a, b = ctx_own[...].reshape(ROWS, HALF), ctx_rcv[...].reshape(ROWS, HALF)
        both = jnp.concatenate([jnp.where(core == 0, a, b), jnp.where(core == 0, b, a)], 1)
        ctx_full[...] = both
        stream = own[0, :, 0].reshape(ROWS, D).astype(F32) + dot(both, w_out[0]) + b_out[0]
        low = stream.astype(BF)
        s2[...] = low
        normed[...] = norm_low(low, gain[0], shift[0])
        acc[...] = low.astype(F32) + b_down[0]

    u = dot(normed[...], w_up[0]) + b_up[0]
    a, d = gelu_parts(u)
    a = a.astype(BF)
    act[...] = a
    slope[...] = d.astype(BF)
    acc[...] += dot(a, w_down[0])

    @pl.when(t == FF // FT - 1)
    def _():
        if last:
            x = sc[X]
            keep[...] = acc[pl.ds(pl.multiple_of(x * BLOCK, BLOCK), BLOCK)]
            send[...] = acc[pl.ds(pl.multiple_of((1 - x) * BLOCK, BLOCK), BLOCK)].astype(BF)
        else:
            s3[...] = acc[...].reshape(2, BLOCK, D).astype(BF)


def ffn_forward(scalars, layer, last, ctx_own, ctx_rcv, own, own_spec, weights):
    w_out, b_out, gain, shift, w_up, b_up, w_down, b_down = weights
    vector = at_layer((1, 1, D), layer)
    out_specs = [
        whole((ROWS, D)),
        whole((ROWS, D)),
        pl.BlockSpec((ROWS, FT), lambda i, sc: (0, i)),
        pl.BlockSpec((ROWS, FT), lambda i, sc: (0, i)),
    ]
    out_shape = [shape((ROWS, D), BF), shape((ROWS, D), BF), shape((ROWS, FF), BF), shape((ROWS, FF), BF)]
    if last:
        out_specs += [whole((BLOCK, D)), whole((BLOCK, D))]
        out_shape += [shape((BLOCK, D), F32), shape((BLOCK, D), BF)]
    else:
        out_specs += [whole((2, BLOCK, D))]
        out_shape += [shape((2, BLOCK, D), BF)]
    return call(
        partial(ffn_fwd_body, last),
        (FF // FT,),
        [
            whole((2, BLOCK, HALF)),
            whole((2, BLOCK, HALF)),
            own_spec,
            at_layer((1, D, D), layer),
            vector,
            vector,
            vector,
            pl.BlockSpec((1, D, FT), lambda i, sc: (layer, 0, i)),
            pl.BlockSpec((1, 1, FT), lambda i, sc: (layer, 0, i)),
            pl.BlockSpec((1, FT, D), lambda i, sc: (layer, i, 0)),
            vector,
        ],
        out_specs,
        out_shape,
        [pltpu.VMEM((ROWS, D), BF), pltpu.VMEM((ROWS, D), F32)],
        (5.4e9, 20e6),
    )(scalars, ctx_own, ctx_rcv, own, w_out, b_out, gain, shift, w_up, b_up, w_down, b_down)


def norm_back(d_normed, rows, gain):
    unit, spread = normalise(rows)
    d_unit = d_normed * gain
    first = jnp.mean(d_unit, -1, keepdims=True)
    second = jnp.mean(d_unit * unit, -1, keepdims=True)
    d_rows = spread * (d_unit - first - unit * second)
    return d_rows, jnp.sum(d_normed * unit, 0, keepdims=True), jnp.sum(d_normed, 0, keepdims=True)


def attn_norm_body(last, sc, grad, part, part_rcv, own, gain, *outs):
    grad_rows = grad[...].reshape(ROWS, D).astype(F32)
    d_normed = part[...].reshape(ROWS, D) + part_rcv[...].reshape(ROWS, D).astype(F32)
    d_rows, g_gain, g_shift = norm_back(d_normed, own[0, :, 0].reshape(ROWS, D).astype(F32), gain[0])
    total = grad_rows + d_rows
    small = outs[-1]
    small[0:1] = g_gain
    small[1:2] = g_shift
    small[2:3] = jnp.sum(grad_rows, 0, keepdims=True)
    if last:
        keep, send = outs[0:2]
        keep[...] = jnp.where(sc[X] == 0, total[0:BLOCK], total[BLOCK:ROWS])
        send[...] = jnp.where(sc[X] == 0, total[BLOCK:ROWS], total[0:BLOCK]).astype(BF)
    else:
        outs[0][...] = total.astype(BF).reshape(2, BLOCK, D)


def attention_norm_back(scalars, layer, last, grad, part, part_rcv, own, own_spec, gain):
    block = whole((2, BLOCK, D))
    if last:
        out_specs = [whole((BLOCK, D)), whole((BLOCK, D))]
        out_shape = [shape((BLOCK, D), F32), shape((BLOCK, D), BF)]
    else:
        out_specs, out_shape = [block], [shape((2, BLOCK, D), BF)]
    return call(
        partial(attn_norm_body, last),
        (1,),
        [block, block, block, own_spec, at_layer((1, 1, D), layer)],
        out_specs + [whole((3, D))],
        out_shape + [shape((3, D), F32)],
        [],
        (2e8, 5e6),
    )(scalars, grad, part, part_rcv, own, gain)


BT = 768


def ffn_back_body(sc, grad, s2, gain, w_up, w_down, slope, dh, ds, small, bias, acc):
    t = pl.program_id(0)
    low = grad[0, :, 0].reshape(ROWS, D)
    d_act = dot_nt(low, w_down[0])
    d_hidden = d_act * slope[...].astype(F32)
    d_low = d_hidden.astype(BF)
    dh[...] = d_low
    bias[...] = jnp.sum(d_low.astype(F32), 0, keepdims=True)
    part = dot_nt(d_low, w_up[0])

    @pl.when(t == 0)
    def _():
        acc[...] = part

    @pl.when(t > 0)
    def _():
        acc[...] += part

    @pl.when(t == FF // BT - 1)
    def _():
        rows = low.astype(F32)
        d_rows, g_gain, g_shift = norm_back(acc[...], s2[...].astype(F32), gain[0])
        ds[...] = (rows + d_rows).astype(BF).reshape(2, BLOCK, D)
        small[0:1] = g_gain
        small[1:2] = g_shift
        small[2:3] = jnp.sum(rows, 0, keepdims=True)


def ffn_backward(scalars, layer, grad, grad_spec, s2, slope, weights):
    gain, w_up, w_down = weights
    return call(
        ffn_back_body,
        (FF // BT,),
        [
            grad_spec,
            whole((ROWS, D)),
            at_layer((1, 1, D), layer),
            pl.BlockSpec((1, D, BT), lambda i, sc: (layer, 0, i)),
            pl.BlockSpec((1, BT, D), lambda i, sc: (layer, i, 0)),
            pl.BlockSpec((ROWS, BT), lambda i, sc: (0, i)),
        ],
        [
            pl.BlockSpec((ROWS, BT), lambda i, sc: (0, i)),
            whole((2, BLOCK, D)),
            whole((3, D)),
            pl.BlockSpec((1, BT), lambda i, sc: (0, i)),
        ],
        [shape((ROWS, FF), BF), shape((2, BLOCK, D), BF), shape((3, D), F32), shape((1, FF), F32)],
        [pltpu.VMEM((ROWS, D), F32)],
        (4.9e9, 18e6),
    )(scalars, grad, s2, gain, w_up, w_down, slope)


def place(sc, piece):
    return (piece % 2) ^ sc[Y], (piece // 2) ^ sc[Z]


def ffn_weight_body(
    sc, grad, grad_o, s2, s2_o, gain, shift, act, dh, w_up, b_up, w_down, keep, send, n_t, n_o, n_t_o, g_t, g_t_o
):
    t = pl.program_id(0)
    core = sc[C]
    low, low_o = grad[0, :, 0].reshape(ROWS, D), grad_o[0, :, 0].reshape(ROWS, D)

    @pl.when(t == 0)
    def _():
        n_t[...] = norm_low(s2[...], gain[0], shift[0]).T
        other = norm_low(s2_o[...], gain[0], shift[0])
        n_o[...] = other
        n_t_o[...] = other.T
        x = sc[X]
        g_t[...] = jnp.where(x == 0, low[:, 0:HALF], low[:, HALF:D]).T
        g_t_o[...] = jnp.where(x == 0, low_o[:, 0:HALF], low_o[:, HALF:D]).T

    u = dot(n_o[...], w_up[0]) + b_up[0]
    active_o, slope_o = gelu_parts(u)

    @pl.when(t < 2)
    def _():
        dh_o = (dot_nt(low_o, w_down[0]) * slope_o).astype(BF)
        g_up = (dot(n_t[...], dh[...]) + dot(n_t_o[...], dh_o)).astype(BF)
        for ref, when in ((send, 0), (keep, 1)):

            @pl.when(t == when)
            def _():
                for piece in range(8):
                    py, pz = place(sc, piece)
                    for j in range(2):
                        ref[py, pz, j] = g_up[piece * PART : (piece + 1) * PART, j * HALF : (j + 1) * HALF]

    g_down = (dot(g_t[...], act[...]) + dot(g_t_o[...], active_o.astype(BF))).astype(BF).T
    tile = ffn_tile(t, sc)
    for half in range(2):
        py, pz = place(sc, 2 * tile + half)
        for j in range(2):
            first = g_down[half * HALF + j * PART : half * HALF + (j + 1) * PART]
            second = g_down[half * HALF + (j + 2) * PART : half * HALF + (j + 3) * PART]
            keep[py, pz, 2 + j] = jnp.where(core == 0, first, second)
            send[py, pz, 2 + j] = jnp.where(core == 0, second, first)


def ffn_tile(step, sc):
    mine = 2 * sc[X]
    rest = 2 - mine
    return jnp.where(step == 0, mine + 1 - sc[C], jnp.where(step == 1, mine + sc[C], rest + step - 2))


def ffn_weights(scalars, layer, grad, grad_spec, grad_o, grad_o_spec, s2, s2_o, act, dh, weights):
    gain, shift, w_up, b_up, w_down = weights
    packed = (2, 4, 4, PART, HALF)
    return call(
        ffn_weight_body,
        (FF // BT,),
        [
            grad_spec,
            grad_o_spec,
            whole((ROWS, D)),
            whole((ROWS, D)),
            at_layer((1, 1, D), layer),
            at_layer((1, 1, D), layer),
            pl.BlockSpec((ROWS, BT), lambda i, sc: (0, ffn_tile(i, sc))),
            pl.BlockSpec((ROWS, BT), lambda i, sc: (0, ffn_tile(jnp.minimum(i, 1), sc))),
            pl.BlockSpec((1, D, BT), lambda i, sc: (layer, 0, ffn_tile(i, sc))),
            pl.BlockSpec((1, 1, BT), lambda i, sc: (layer, 0, ffn_tile(i, sc))),
            pl.BlockSpec((1, BT, D), lambda i, sc: (layer, ffn_tile(jnp.minimum(i, 1), sc), 0)),
        ],
        [whole(packed), whole(packed)],
        [shape(packed, BF), shape(packed, BF)],
        [
            pltpu.VMEM((D, ROWS), BF),
            pltpu.VMEM((ROWS, D), BF),
            pltpu.VMEM((D, ROWS), BF),
            pltpu.VMEM((HALF, ROWS), BF),
            pltpu.VMEM((HALF, ROWS), BF),
        ],
        (8.6e9, 22e6),
    )(scalars, grad, grad_o, s2, s2_o, gain, shift, act, dh, w_up, b_up, w_down)


def attn_back_body(
    sc, gr_own, gr_rcv, qkv, ctx, lse, ep, w_out, wq, wk, wv, d_qkv, part_own, part_oth, bias, d_ctx, delta, d_k, d_v
):
    core = sc[C]
    for b in range(4):
        rows = slice(b * BLOCK, (b + 1) * BLOCK)
        d_ctx[rows] = dot_nt(in_order(gr_own, gr_rcv, b, core), w_out[0]).astype(BF)
    product = d_ctx[...].astype(F32) * ctx[...].astype(F32)
    high = product.astype(BF)
    rest = (product - high.astype(F32)).astype(BF)
    picks = (
        lax.broadcasted_iota(jnp.int32, (8, HALF), 0) == lax.broadcasted_iota(jnp.int32, (8, HALF), 1) // HEAD_DIM
    ).astype(BF)
    delta[...] = dot_nt(picks, high) + dot_nt(picks, rest)
    ep_row, ep_col = episode_columns(ep)
    for i in range(4):
        lo, hi = first_key(i), (i + 1) * BLOCK
        key_at = lo + lax.broadcasted_iota(jnp.int32, (hi - lo, BLOCK), 0)
        row_at = i * BLOCK + lax.broadcasted_iota(jnp.int32, (hi - lo, BLOCK), 1)
        same = ep_col[lo:hi, 0:1] == ep_row[0:1, i * BLOCK : hi]
        bias[i, 0 : hi - lo, :] = jnp.where((key_at <= row_at) & same, 0.0, MASKED)

    @pl.loop(0, 3)
    def _(p):
        at = pl.multiple_of(p * PAIR, PAIR)
        d_k[...] = jnp.zeros_like(d_k)
        d_v[...] = jnp.zeros_like(d_v)
        for i in range(4):
            lo, hi = first_key(i), (i + 1) * BLOCK
            rows = slice(i * BLOCK, hi)
            q = qkv[rows, pl.ds(at, PAIR)]
            k = qkv[lo:hi, pl.ds(HALF + at, PAIR)]
            v = qkv[lo:hi, pl.ds(2 * HALF + at, PAIR)]
            dc = d_ctx[rows, pl.ds(at, PAIR)]
            d_q = jnp.zeros((BLOCK, PAIR), F32)
            for h in range(2):

                def only(array):
                    lane = lax.broadcasted_iota(jnp.int32, array.shape, 1)
                    mine = (lane >= HEAD_DIM) if h else (lane < HEAD_DIM)
                    return jnp.where(mine, array, jnp.zeros_like(array))

                q_h, dc_h = only(q), only(dc)
                s = dot_nt(k, q_h) + bias[i, 0 : hi - lo, :]
                prob = jnp.exp(s - lse[pl.ds(2 * p + h, 1), rows])
                d_p = dot_nt(v, dc_h)
                d_s = (prob * (d_p - delta[pl.ds(2 * p + h, 1), rows])).astype(BF)
                d_v[lo:hi] += dot(prob.astype(BF), dc_h)
                d_k[lo:hi] += dot(d_s, q_h)
                d_q += dot_tn(d_s, only(k))
            d_qkv[rows, pl.ds(at, PAIR)] = (d_q * 0.125).astype(BF)
        d_qkv[:, pl.ds(HALF + at, PAIR)] = d_k[...].astype(BF)
        d_qkv[:, pl.ds(2 * HALF + at, PAIR)] = d_v[...].astype(BF)

    for b in range(4):
        rows = slice(b * BLOCK, (b + 1) * BLOCK)
        part = dot_nt(d_qkv[rows, 0:HALF], wq[0])
        part += dot_nt(d_qkv[rows, HALF : 2 * HALF], wk[0])
        part += dot_nt(d_qkv[rows, 2 * HALF : 3 * HALF], wv[0])

        @pl.when(core == b % 2)
        def _():
            part_own[b // 2] = part

        @pl.when(core != b % 2)
        def _():
            part_oth[b // 2] = part.astype(BF)


def attention_backward(scalars, layer, gr_own, gr_rcv, qkv, ctx, lse, episodes, ep_spec, w_out, w_qkv):
    columns = [pl.BlockSpec((1, D, HALF), partial(lambda j, i, sc: (layer, 0, 2 * j + sc[C]), j)) for j in range(3)]
    block = whole((2, BLOCK, D))
    return call(
        attn_back_body,
        (1,),
        [
            block,
            block,
            whole((LENGTH, 3 * HALF)),
            whole((LENGTH, HALF)),
            whole((8, LENGTH)),
            ep_spec,
            pl.BlockSpec((1, HALF, D), lambda i, sc: (layer, sc[C], 0)),
        ]
        + columns,
        [whole((LENGTH, 3 * HALF)), block, block],
        [shape((LENGTH, 3 * HALF), BF), shape((2, BLOCK, D), F32), shape((2, BLOCK, D), BF)],
        [
            pltpu.VMEM((4, 3 * BLOCK, BLOCK), F32),
            pltpu.VMEM((LENGTH, HALF), BF),
            pltpu.VMEM((8, LENGTH), F32),
            pltpu.VMEM((LENGTH, PAIR), F32),
            pltpu.VMEM((LENGTH, PAIR), F32),
        ],
        (2.5e9 + 6e9, 12e6),
    )(scalars, gr_own, gr_rcv, qkv, ctx, lse, episodes, w_out, w_qkv, w_qkv, w_qkv)


def attn_weight_body(
    sc, own, other, gain, shift, d_qkv, gr_own, gr_rcv, ctx_full, ctx_oth, ctx_rcv, keep, send, n_t, late
):
    core, x = sc[C], sc[X]
    own, other = own.at[0, :, 0], other.at[0, :, 0]
    for b in range(4):
        rows = slice(b * BLOCK, (b + 1) * BLOCK)
        n_t[:, rows] = norm_low(in_order(own, other, b, core), gain[0], shift[0]).T

    def columns(ref):
        rows = ref[...].reshape(ROWS, D)
        return jnp.where(core == 0, rows[:, 0:HALF], rows[:, HALF:D]).T

    a, b = ctx_oth[...].reshape(ROWS, HALF), ctx_rcv[...].reshape(ROWS, HALF)
    far = jnp.concatenate([jnp.where(core == 0, a, b), jnp.where(core == 0, b, a)], 1)
    g_out = (dot(columns(gr_own), ctx_full[...]) + dot(columns(gr_rcv), far)).astype(BF).T

    def grad(j):
        if j == 3:
            return g_out
        return dot(n_t[...], d_qkv[:, j * HALF : (j + 1) * HALF]).astype(BF)

    for j in range(2):
        first, second = grad(j), grad(j + 2)
        mine, yours = jnp.where(x == 0, first, second), jnp.where(x == 0, second, first)
        for piece in range(8):
            py, pz = place(sc, piece)
            keep[py, pz, j] = mine[piece * PART : (piece + 1) * PART]
            send[py, pz, j] = yours[piece * PART : (piece + 1) * PART]


def attention_weights(
    scalars, layer, own, own_spec, other, other_spec, gain, shift, d_qkv, gr_own, gr_rcv, ctx_full, ctx_oth, ctx_rcv
):
    packed = (2, 4, 2, PART, HALF)
    block = whole((2, BLOCK, D))
    return call(
        attn_weight_body,
        (1,),
        [
            own_spec,
            other_spec,
            at_layer((1, 1, D), layer),
            at_layer((1, 1, D), layer),
            whole((LENGTH, 3 * HALF)),
            block,
            block,
            whole((ROWS, D)),
            whole((2, BLOCK, HALF)),
            whole((2, BLOCK, HALF)),
        ],
        [whole(packed), whole(packed)],
        [shape(packed, BF), shape(packed, BF)],
        [pltpu.VMEM((D, LENGTH), BF), pltpu.VMEM((8, PAIR), F32)],
        (2.5e9, 12e6),
    )(scalars, own, other, gain, shift, d_qkv, gr_own, gr_rcv, ctx_full, ctx_oth, ctx_rcv)


def to_core(value):
    return lax.ppermute(value, "section", [(0, 1), (1, 0), (2, 3), (3, 2)])


def to_chip(value):
    return lax.ppermute(value, "section", [(0, 2), (2, 0), (1, 3), (3, 1)])


def to_dp(value, distance):
    return lax.ppermute(value, "dp", [(i, i ^ distance) for i in range(8)])


def total(*terms):
    out = terms[0].astype(F32)
    for term in terms[1:]:
        out = out + term.astype(F32)
    return out.astype(BF)


def reduced(keep, send, first):
    got = first(send)
    y_got = to_dp(total(keep[1], got[1]), 1)
    z_got = [to_dp(total(keep[0, k], got[0, k], y_got[k]), 2 * k) for k in (1, 2, 3)]
    return total(keep[0, 0], got[0, 0], y_got[0], *z_got)


def reduced_any(keep, send, first):
    both = total(keep, first(send))
    count = both.shape[2]
    return jnp.moveaxis(both, 0, 1).reshape(8, count, PART, HALF)


def gathered(share):
    core = lax.axis_index("section") % 2
    chip = lax.axis_index("section") // 2
    far = to_chip(share)
    pair = jnp.stack([jnp.where(chip == 0, share, far), jnp.where(chip == 0, far, share)])
    other = to_core(pair)
    return jnp.stack([jnp.where(core == 0, pair, other), jnp.where(core == 0, other, pair)], 1)


def on_device(
    tokens,
    episodes,
    attn_gain,
    attn_shift,
    qkv_weight,
    out_weight,
    out_bias,
    ffn_gain,
    ffn_shift,
    up_weight,
    up_bias,
    down_weight,
    down_bias,
    cotangent,
):
    replicas = lax.axis_size("dp")
    section = lax.axis_index("section")
    replica = lax.axis_index("dp")
    chip, core = section // 2, section % 2
    direct = replicas == 8
    y, z = (replica % 2, replica // 2) if direct else (0, 0)
    scalars = jnp.stack([jnp.asarray(v, jnp.int32) for v in (chip, core, y, z)])

    stream = tokens.reshape(2, 2, 2, BLOCK, D)
    cot = cotangent.reshape(2, 2, 2, BLOCK, D)
    eps = episodes.reshape(2, 1, LENGTH)
    ep_spec = pl.BlockSpec((1, 1, LENGTH), lambda i, sc: (sc[X], 0, 0))

    def input_spec(micro, side):
        return pl.BlockSpec((1, 2, 1, BLOCK, D), lambda i, sc: (micro(sc[X]), 0, side(sc[C]), 0, 0))

    same, flip = (lambda v: v), (lambda v: 1 - v)
    own_in, other_in, far_in = input_spec(same, same), input_spec(same, flip), input_spec(flip, same)
    local = pl.BlockSpec((1, 2, 1, BLOCK, D), lambda i, sc: (0, 0, 0, 0, 0))

    def rows5(value):
        return value.reshape(1, 2, 1, BLOCK, D)

    def vec(array):
        return array.reshape(2, 1, -1)

    a_gain, a_shift, b_out = vec(attn_gain), vec(attn_shift), vec(out_bias)
    f_gain, f_shift, b_up, b_down = vec(ffn_gain), vec(ffn_shift), vec(up_bias), vec(down_bias)

    kept = []
    own, own_spec, other, other_spec = stream, own_in, stream, other_in
    for layer in range(2):
        qkv, ctx, ctx_own, ctx_oth, lse = attention_forward(
            scalars, layer, own, own_spec, other, other_spec, eps, ep_spec, a_gain, a_shift, qkv_weight
        )
        ctx_rcv = to_core(ctx_oth)
        ctx_far = to_core(ctx_own)
        s2, ctx_full, act, slope, *result = ffn_forward(
            scalars,
            layer,
            layer == 1,
            ctx_own,
            ctx_rcv,
            own,
            own_spec,
            (out_weight, b_out, f_gain, f_shift, up_weight, b_up, down_weight, b_down),
        )
        s2_o = to_chip(s2)
        kept.append((own, own_spec, other, other_spec, qkv, ctx, ctx_oth, ctx_far, ctx_full, lse, s2, s2_o, act, slope))
        if layer == 0:
            s3 = result[0]
            own, own_spec, other, other_spec = rows5(s3), local, rows5(to_core(s3)), local
    final_keep, final_send = result

    smalls = [None, None]
    shares = [None, None]
    grad, grad_spec, grad_o, grad_o_spec = cot, own_in, cot, far_in
    for layer in (1, 0):
        own, own_spec, other, other_spec, qkv, ctx, ctx_oth, ctx_far, ctx_full, lse, s2, s2_o, act, slope = kept[layer]
        dh, ds, f_small, g_up_bias = ffn_backward(
            scalars, layer, grad, grad_spec, s2, slope, (f_gain, up_weight, down_weight)
        )
        ds_rcv = to_core(ds)
        f_keep, f_send = ffn_weights(
            scalars,
            layer,
            grad,
            grad_spec,
            grad_o,
            grad_o_spec,
            s2,
            s2_o,
            act,
            dh,
            (f_gain, f_shift, up_weight, b_up, down_weight),
        )
        d_qkv, part_own, part_oth = attention_backward(
            scalars, layer, ds, ds_rcv, qkv, ctx, lse, eps, ep_spec, out_weight, qkv_weight
        )
        part_rcv = to_core(part_oth)
        a_keep, a_send = attention_weights(
            scalars,
            layer,
            own,
            own_spec,
            other,
            other_spec,
            a_gain,
            a_shift,
            d_qkv,
            ds,
            ds_rcv,
            ctx_full,
            ctx_oth,
            ctx_far,
        )
        *result, a_small = attention_norm_back(
            scalars, layer, layer == 0, ds, part_own, part_rcv, own, own_spec, a_gain
        )
        if layer == 1:
            grad, grad_spec = rows5(result[0]), local
            grad_o, grad_o_spec = rows5(to_chip(result[0])), local
        reduce = reduced if direct else reduced_any
        shares[layer] = (reduce(f_keep, f_send, to_core), reduce(a_keep, a_send, to_chip))
        smalls[layer] = jnp.concatenate([a_small, f_small, g_up_bias.reshape(4, D)])
    input_keep, input_send = result

    def placed(keep, send):
        got = to_chip(send).astype(F32)
        return jnp.stack([jnp.where(chip == 0, keep, got), jnp.where(chip == 0, got, keep)])[:, None]

    final_out, input_out = placed(final_keep, final_send), placed(input_keep, input_send)

    small = lax.psum(jnp.stack(smalls), ("section", "dp"))
    ups, downs, qkvs, outs = [], [], [], []
    for layer in range(2):
        f_all, a_all = (gathered(share).astype(F32) for share in shares[layer])
        if direct:
            ups.append(jnp.moveaxis(f_all[:, :, 0:2], 3, 0).reshape(PART, FF))
            downs.append(f_all[:, :, 2:4].transpose(1, 2, 3, 0, 4).reshape(4 * PART, D))
            qkvs.append(
                jnp.concatenate([a_all[0, c, j] for j in range(2) for c in range(2)] + [a_all[1, 0, 0], a_all[1, 1, 0]], 1)
            )
            outs.append(jnp.concatenate([a_all[1, 0, 1], a_all[1, 1, 1]], 1))
        else:
            up = f_all[:, :, :, 0:2].transpose(2, 4, 0, 1, 3, 5).reshape(D, FF)
            down = f_all[:, :, :, 2:4].transpose(2, 1, 3, 4, 0, 5).reshape(FF, D)
            q_k = a_all[0].transpose(1, 3, 2, 0, 4).reshape(D, 2 * D)
            v = a_all[1, :, :, 0].transpose(1, 2, 0, 3).reshape(D, D)
            out = a_all[1, :, :, 1].transpose(1, 2, 0, 3).reshape(D, D)
            for found, array in ((ups, up), (downs, down), (qkvs, jnp.concatenate([q_k, v], 1)), (outs, out)):
                found.append(lax.psum_scatter(array, "dp", scatter_dimension=0, tiled=True))

    def piece(rows):
        width = rows.shape[-1] // replicas
        return lax.dynamic_slice_in_dim(rows, replica * width, width, 1)

    return (
        final_out,
        input_out,
        piece(small[:, 0]),
        piece(small[:, 1]),
        jnp.stack(qkvs),
        jnp.stack(outs),
        piece(small[:, 2]),
        piece(small[:, 3]),
        piece(small[:, 4]),
        jnp.stack(ups),
        piece(small[:, 6:10].reshape(2, FF)),
        jnp.stack(downs),
        piece(small[:, 5]),
    )


def solution(mesh):
    split = P(None, "dp", None, None)
    placed = (split, P(None, "dp", None)) + (P(),) * 11 + (split,)
    rows = P(None, "dp", "section", None)
    vector, matrix = P(None, "dp"), P(None, "dp", None)
    return jax.shard_map(
        on_device,
        mesh=mesh,
        in_specs=placed,
        out_specs=(
            rows,
            rows,
            vector,
            vector,
            matrix,
            matrix,
            vector,
            vector,
            vector,
            matrix,
            vector,
            matrix,
            vector,
        ),
        check_vma=False,
    )
```

```python
from functools import partial

import jax
import jax.numpy as jnp
from jax import lax
from jax.experimental import pallas as pl
from jax.experimental.pallas import tpu as pltpu
from jax.sharding import PartitionSpec as P

BF = jnp.bfloat16
F32 = jnp.float32
EPS = 1e-05
MASKED = -1e30
D = 768
HALF = 384
PAIR = 128
HEAD_DIM = 64
FF = 3072
LENGTH = 1024
BLOCK = 256
ROWS = 512
PART = 96
GELU_A = 0.7978845608028654
GELU_B = GELU_A * 0.044715


def dot(a, b):
    return jnp.dot(a, b, preferred_element_type=F32)


def dot_nt(a, b):
    return lax.dot_general(a, b, (((1,), (1,)), ((), ())), preferred_element_type=F32)


def dot_tn(a, b):
    return lax.dot_general(a, b, (((0,), (0,)), ((), ())), preferred_element_type=F32)


def normalise(rows):
    center = rows - jnp.mean(rows, -1, keepdims=True)
    spread = lax.rsqrt(jnp.mean(center * center, -1, keepdims=True) + EPS)
    return center * spread, spread


def norm_low(rows, gain, shift):
    unit, _ = normalise(rows.astype(F32))
    return (unit * gain + shift).astype(BF)


def call(body, grid, in_specs, out_specs, out_shape, scratch, cost=None, deps=()):
    count = len(in_specs)

    def with_deps(sc, *refs):
        return body(sc, *refs[:count], *refs[count + len(deps) :])

    kernel = pl.pallas_call(
        with_deps,
        grid_spec=pltpu.PrefetchScalarGridSpec(
            num_scalar_prefetch=1,
            grid=grid,
            in_specs=list(in_specs) + [pl.BlockSpec(memory_space=pl.ANY)] * len(deps),
            out_specs=out_specs,
            scratch_shapes=scratch,
        ),
        out_shape=out_shape,
        compiler_params=pltpu.CompilerParams(vmem_limit_bytes=56 * 1024 * 1024),
        cost_estimate=None
        if cost is None
        else pl.CostEstimate(flops=int(cost[0]), bytes_accessed=int(cost[1]), transcendentals=0),
    )
    return lambda *args: kernel(*args, *deps)


def shape(dims, dtype):
    return jax.ShapeDtypeStruct(dims, dtype)


def whole(dims):
    count = len(dims)
    return pl.BlockSpec(dims, lambda i, sc: (0,) * count)


def at_layer(dims, layer):
    count = len(dims) - 1
    return pl.BlockSpec(dims, lambda i, sc: (layer,) + (0,) * count)


X, C, Y, Z = 0, 1, 2, 3


def in_order(own, other, block, core):
    return jnp.where(core == block % 2, own[block // 2], other[block // 2])


def episode_columns(ep_ref):
    row = jnp.broadcast_to(ep_ref[...].reshape(1, LENGTH).astype(F32), (PAIR, LENGTH))
    return row, row.T


def first_key(i):
    return max(0, i - 2) * BLOCK


def attn_fwd_body(sc, own, other, ep, gain, shift, wq, wk, wv, qkv, ctx, ctx_own, ctx_oth, lse, bias, vext, lse_cols):
    core = sc[C]
    own, other = own.at[0, :, 0], other.at[0, :, 0]
    for b in range(4):
        rows = slice(b * BLOCK, (b + 1) * BLOCK)
        normed = norm_low(in_order(own, other, b, core), gain[0], shift[0])
        qkv[rows, 0:HALF] = (dot(normed, wq[0]).astype(BF) * 0.125).astype(BF)
        qkv[rows, HALF : 2 * HALF] = dot(normed, wk[0]).astype(BF)
        qkv[rows, 2 * HALF : 3 * HALF] = dot(normed, wv[0]).astype(BF)
    ep_row, ep_col = episode_columns(ep)
    for i in range(4):
        lo, hi = first_key(i), (i + 1) * BLOCK
        key_at = lo + lax.broadcasted_iota(jnp.int32, (BLOCK, hi - lo), 1)
        row_at = i * BLOCK + lax.broadcasted_iota(jnp.int32, (BLOCK, hi - lo), 0)
        same = ep_col[i * BLOCK : hi, 0:1] == ep_row[0:1, lo:hi]
        bias[i, :, 0 : hi - lo] = jnp.where((key_at <= row_at) & same, 0.0, MASKED)
    vext[:, PAIR:] = jnp.ones((LENGTH, PAIR), BF)
    lane = lax.broadcasted_iota(jnp.int32, (BLOCK, PAIR), 1)

    @pl.loop(0, 3)
    def _(p):
        at = pl.multiple_of(p * PAIR, PAIR)
        vext[:, 0:PAIR] = qkv[:, pl.ds(2 * HALF + at, PAIR)]
        for i in range(4):
            lo, hi = first_key(i), (i + 1) * BLOCK
            rows = slice(i * BLOCK, hi)
            q = qkv[rows, pl.ds(at, PAIR)]
            k = qkv[lo:hi, pl.ds(HALF + at, PAIR)]
            outs = []
            for h in range(2):
                mine = (lane >= HEAD_DIM) if h else (lane < HEAD_DIM)
                s = dot_nt(jnp.where(mine, q, jnp.zeros_like(q)), k) + bias[i, :, 0 : hi - lo]
                top = jnp.max(s, -1, keepdims=True)
                prob = jnp.exp(s - top).astype(BF)
                o = dot(prob, vext[lo:hi, :])
                total = o[:, PAIR : PAIR + 1]
                outs.append(o[:, 0:PAIR] / total)
                lse_cols[rows, :] = jnp.where(lane == 2 * p + h, top + jnp.log(total), lse_cols[rows, :])
            ctx[rows, pl.ds(at, PAIR)] = jnp.where(lane < HEAD_DIM, outs[0], outs[1]).astype(BF)

    lse[...] = lse_cols[...].T[0:8]
    for b in range(4):
        piece = ctx[b * BLOCK : (b + 1) * BLOCK]

        @pl.when(core == b % 2)
        def _():
            ctx_own[b // 2] = piece

        @pl.when(core != b % 2)
        def _():
            ctx_oth[b // 2] = piece


def attention_forward(scalars, layer, own, own_spec, other, other_spec, episodes, ep_spec, gain, shift, w_qkv):
    columns = [pl.BlockSpec((1, D, HALF), partial(lambda j, i, sc: (layer, 0, 2 * j + sc[C]), j)) for j in range(3)]
    return call(
        attn_fwd_body,
        (1,),
        [own_spec, other_spec, ep_spec, at_layer((1, 1, D), layer), at_layer((1, 1, D), layer)] + columns,
        [
            whole((LENGTH, 3 * HALF)),
            whole((LENGTH, HALF)),
            whole((2, BLOCK, HALF)),
            whole((2, BLOCK, HALF)),
            whole((8, LENGTH)),
        ],
        [
            shape((LENGTH, 3 * HALF), BF),
            shape((LENGTH, HALF), BF),
            shape((2, BLOCK, HALF), BF),
            shape((2, BLOCK, HALF), BF),
            shape((8, LENGTH), F32),
        ],
        [
            pltpu.VMEM((4, BLOCK, 3 * BLOCK), F32),
            pltpu.VMEM((LENGTH, 2 * PAIR), BF),
            pltpu.VMEM((LENGTH, PAIR), F32),
        ],
        (1.8e9 + 2.4e9, 8e6),
    )(scalars, own, other, episodes, gain, shift, w_qkv, w_qkv, w_qkv)


def gelu_parts(u):
    cubic = GELU_B * (u * u)
    t = jnp.tanh(u * (GELU_A + cubic))
    half = 0.5 * t + 0.5
    active = u * half
    slope = half + (active * (1.0 - half)) * (6.0 * cubic + 2.0 * GELU_A)
    return active, slope


FT = 512


def ffn_fwd_body(last, sc, ctx_own, ctx_rcv, own, w_out, b_out, gain, shift, w_up, b_up, w_down, b_down, *rest):
    if last:
        s2, ctx_full, act, slope, keep, send, normed, acc = rest
    else:
        s2, ctx_full, act, slope, s3, normed, acc = rest
    t = pl.program_id(0)
    core = sc[C]

    @pl.when(t == 0)
    def _():
        a, b = ctx_own[...].reshape(ROWS, HALF), ctx_rcv[...].reshape(ROWS, HALF)
        both = jnp.concatenate([jnp.where(core == 0, a, b), jnp.where(core == 0, b, a)], 1)
        ctx_full[...] = both
        stream = own[0, :, 0].reshape(ROWS, D).astype(F32) + dot(both, w_out[0]) + b_out[0]
        low = stream.astype(BF)
        s2[...] = low
        normed[...] = norm_low(low, gain[0], shift[0])
        acc[...] = low.astype(F32) + b_down[0]

    u = dot(normed[...], w_up[0]) + b_up[0]
    a, d = gelu_parts(u)
    a = a.astype(BF)
    act[...] = a
    slope[...] = d.astype(BF)
    acc[...] += dot(a, w_down[0])

    @pl.when(t == FF // FT - 1)
    def _():
        if last:
            x = sc[X]
            keep[...] = acc[pl.ds(pl.multiple_of(x * BLOCK, BLOCK), BLOCK)]
            send[...] = acc[pl.ds(pl.multiple_of((1 - x) * BLOCK, BLOCK), BLOCK)].astype(BF)
        else:
            s3[...] = acc[...].reshape(2, BLOCK, D).astype(BF)


def ffn_forward(scalars, layer, last, ctx_own, ctx_rcv, own, own_spec, weights):
    w_out, b_out, gain, shift, w_up, b_up, w_down, b_down = weights
    vector = at_layer((1, 1, D), layer)
    out_specs = [
        whole((ROWS, D)),
        whole((ROWS, D)),
        pl.BlockSpec((ROWS, FT), lambda i, sc: (0, i)),
        pl.BlockSpec((ROWS, FT), lambda i, sc: (0, i)),
    ]
    out_shape = [shape((ROWS, D), BF), shape((ROWS, D), BF), shape((ROWS, FF), BF), shape((ROWS, FF), BF)]
    if last:
        out_specs += [whole((BLOCK, D)), whole((BLOCK, D))]
        out_shape += [shape((BLOCK, D), F32), shape((BLOCK, D), BF)]
    else:
        out_specs += [whole((2, BLOCK, D))]
        out_shape += [shape((2, BLOCK, D), BF)]
    return call(
        partial(ffn_fwd_body, last),
        (FF // FT,),
        [
            whole((2, BLOCK, HALF)),
            whole((2, BLOCK, HALF)),
            own_spec,
            at_layer((1, D, D), layer),
            vector,
            vector,
            vector,
            pl.BlockSpec((1, D, FT), lambda i, sc: (layer, 0, i)),
            pl.BlockSpec((1, 1, FT), lambda i, sc: (layer, 0, i)),
            pl.BlockSpec((1, FT, D), lambda i, sc: (layer, i, 0)),
            vector,
        ],
        out_specs,
        out_shape,
        [pltpu.VMEM((ROWS, D), BF), pltpu.VMEM((ROWS, D), F32)],
        (5.4e9, 20e6),
    )(scalars, ctx_own, ctx_rcv, own, w_out, b_out, gain, shift, w_up, b_up, w_down, b_down)


def norm_back(d_normed, rows, gain):
    unit, spread = normalise(rows)
    d_unit = d_normed * gain
    first = jnp.mean(d_unit, -1, keepdims=True)
    second = jnp.mean(d_unit * unit, -1, keepdims=True)
    d_rows = spread * (d_unit - first - unit * second)
    return d_rows, jnp.sum(d_normed * unit, 0, keepdims=True), jnp.sum(d_normed, 0, keepdims=True)


def attn_norm_body(last, sc, grad, part, part_rcv, own, gain, *outs):
    grad_rows = grad[...].reshape(ROWS, D).astype(F32)
    d_normed = part[...].reshape(ROWS, D) + part_rcv[...].reshape(ROWS, D).astype(F32)
    d_rows, g_gain, g_shift = norm_back(d_normed, own[0, :, 0].reshape(ROWS, D).astype(F32), gain[0])
    total = grad_rows + d_rows
    small = outs[-1]
    small[0:1] = g_gain
    small[1:2] = g_shift
    small[2:3] = jnp.sum(grad_rows, 0, keepdims=True)
    if last:
        keep, send = outs[0:2]
        keep[...] = jnp.where(sc[X] == 0, total[0:BLOCK], total[BLOCK:ROWS])
        send[...] = jnp.where(sc[X] == 0, total[BLOCK:ROWS], total[0:BLOCK]).astype(BF)
    else:
        outs[0][...] = total.astype(BF).reshape(2, BLOCK, D)


def attention_norm_back(scalars, layer, last, grad, part, part_rcv, own, own_spec, gain, deps=()):
    block = whole((2, BLOCK, D))
    if last:
        out_specs = [whole((BLOCK, D)), whole((BLOCK, D))]
        out_shape = [shape((BLOCK, D), F32), shape((BLOCK, D), BF)]
    else:
        out_specs, out_shape = [block], [shape((2, BLOCK, D), BF)]
    return call(
        partial(attn_norm_body, last),
        (1,),
        [block, block, block, own_spec, at_layer((1, 1, D), layer)],
        out_specs + [whole((3, D))],
        out_shape + [shape((3, D), F32)],
        [],
        (2e8, 5e6),
        deps,
    )(scalars, grad, part, part_rcv, own, gain)


BT = 768


def ffn_back_body(sc, grad, s2, gain, w_up, w_down, slope, dh, ds, small, bias, acc):
    t = pl.program_id(0)
    low = grad[0, :, 0].reshape(ROWS, D)
    d_act = dot_nt(low, w_down[0])
    d_hidden = d_act * slope[...].astype(F32)
    d_low = d_hidden.astype(BF)
    dh[...] = d_low
    bias[...] = jnp.sum(d_low.astype(F32), 0, keepdims=True)
    part = dot_nt(d_low, w_up[0])

    @pl.when(t == 0)
    def _():
        acc[...] = part

    @pl.when(t > 0)
    def _():
        acc[...] += part

    @pl.when(t == FF // BT - 1)
    def _():
        rows = low.astype(F32)
        d_rows, g_gain, g_shift = norm_back(acc[...], s2[...].astype(F32), gain[0])
        ds[...] = (rows + d_rows).astype(BF).reshape(2, BLOCK, D)
        small[0:1] = g_gain
        small[1:2] = g_shift
        small[2:3] = jnp.sum(rows, 0, keepdims=True)


def ffn_backward(scalars, layer, grad, grad_spec, s2, slope, weights, deps=()):
    gain, w_up, w_down = weights
    return call(
        ffn_back_body,
        (FF // BT,),
        [
            grad_spec,
            whole((ROWS, D)),
            at_layer((1, 1, D), layer),
            pl.BlockSpec((1, D, BT), lambda i, sc: (layer, 0, i)),
            pl.BlockSpec((1, BT, D), lambda i, sc: (layer, i, 0)),
            pl.BlockSpec((ROWS, BT), lambda i, sc: (0, i)),
        ],
        [
            pl.BlockSpec((ROWS, BT), lambda i, sc: (0, i)),
            whole((2, BLOCK, D)),
            whole((3, D)),
            pl.BlockSpec((1, BT), lambda i, sc: (0, i)),
        ],
        [shape((ROWS, FF), BF), shape((2, BLOCK, D), BF), shape((3, D), F32), shape((1, FF), F32)],
        [pltpu.VMEM((ROWS, D), F32)],
        (4.9e9, 18e6),
        deps,
    )(scalars, grad, s2, gain, w_up, w_down, slope)


def place(sc, piece):
    return (piece % 2) ^ sc[Y], (piece // 2) ^ sc[Z]


def ffn_weight_body(
    sc, grad, grad_o, s2, s2_o, gain, shift, act, dh, w_up, b_up, w_down, keep, send, n_t, n_o, n_t_o, g_t, g_t_o
):
    t = pl.program_id(0)
    core = sc[C]
    low, low_o = grad[0, :, 0].reshape(ROWS, D), grad_o[0, :, 0].reshape(ROWS, D)

    @pl.when(t == 0)
    def _():
        n_t[...] = norm_low(s2[...], gain[0], shift[0]).T
        other = norm_low(s2_o[...], gain[0], shift[0])
        n_o[...] = other
        n_t_o[...] = other.T
        x = sc[X]
        g_t[...] = jnp.where(x == 0, low[:, 0:HALF], low[:, HALF:D]).T
        g_t_o[...] = jnp.where(x == 0, low_o[:, 0:HALF], low_o[:, HALF:D]).T

    u = dot(n_o[...], w_up[0]) + b_up[0]
    active_o, slope_o = gelu_parts(u)

    @pl.when(t < 2)
    def _():
        dh_o = (dot_nt(low_o, w_down[0]) * slope_o).astype(BF)
        g_up = (dot(n_t[...], dh[...]) + dot(n_t_o[...], dh_o)).astype(BF)
        for ref, when in ((send, 0), (keep, 1)):

            @pl.when(t == when)
            def _():
                for piece in range(8):
                    py, pz = place(sc, piece)
                    for j in range(2):
                        ref[py, pz, j] = g_up[piece * PART : (piece + 1) * PART, j * HALF : (j + 1) * HALF]

    g_down = (dot(g_t[...], act[...]) + dot(g_t_o[...], active_o.astype(BF))).astype(BF).T
    tile = ffn_tile(t, sc)
    for half in range(2):
        py, pz = place(sc, 2 * tile + half)
        for j in range(2):
            first = g_down[half * HALF + j * PART : half * HALF + (j + 1) * PART]
            second = g_down[half * HALF + (j + 2) * PART : half * HALF + (j + 3) * PART]
            keep[py, pz, 2 + j] = jnp.where(core == 0, first, second)
            send[py, pz, 2 + j] = jnp.where(core == 0, second, first)


def ffn_tile(step, sc):
    mine = 2 * sc[X]
    rest = 2 - mine
    return jnp.where(step == 0, mine + 1 - sc[C], jnp.where(step == 1, mine + sc[C], rest + step - 2))


def ffn_weights(scalars, layer, grad, grad_spec, grad_o, grad_o_spec, s2, s2_o, act, dh, weights, deps=()):
    gain, shift, w_up, b_up, w_down = weights
    packed = (2, 4, 4, PART, HALF)
    return call(
        ffn_weight_body,
        (FF // BT,),
        [
            grad_spec,
            grad_o_spec,
            whole((ROWS, D)),
            whole((ROWS, D)),
            at_layer((1, 1, D), layer),
            at_layer((1, 1, D), layer),
            pl.BlockSpec((ROWS, BT), lambda i, sc: (0, ffn_tile(i, sc))),
            pl.BlockSpec((ROWS, BT), lambda i, sc: (0, ffn_tile(jnp.minimum(i, 1), sc))),
            pl.BlockSpec((1, D, BT), lambda i, sc: (layer, 0, ffn_tile(i, sc))),
            pl.BlockSpec((1, 1, BT), lambda i, sc: (layer, 0, ffn_tile(i, sc))),
            pl.BlockSpec((1, BT, D), lambda i, sc: (layer, ffn_tile(jnp.minimum(i, 1), sc), 0)),
        ],
        [whole(packed), whole(packed)],
        [shape(packed, BF), shape(packed, BF)],
        [
            pltpu.VMEM((D, ROWS), BF),
            pltpu.VMEM((ROWS, D), BF),
            pltpu.VMEM((D, ROWS), BF),
            pltpu.VMEM((HALF, ROWS), BF),
            pltpu.VMEM((HALF, ROWS), BF),
        ],
        (8.6e9, 22e6),
        deps,
    )(scalars, grad, grad_o, s2, s2_o, gain, shift, act, dh, w_up, b_up, w_down)


def attn_back_body(
    sc, gr_own, gr_rcv, qkv, ctx, lse, ep, w_out, wq, wk, wv, d_qkv, part_own, part_oth, bias, d_ctx, delta, d_k, d_v
):
    core = sc[C]
    for b in range(4):
        rows = slice(b * BLOCK, (b + 1) * BLOCK)
        d_ctx[rows] = dot_nt(in_order(gr_own, gr_rcv, b, core), w_out[0]).astype(BF)
    product = d_ctx[...].astype(F32) * ctx[...].astype(F32)
    high = product.astype(BF)
    rest = (product - high.astype(F32)).astype(BF)
    picks = (
        lax.broadcasted_iota(jnp.int32, (8, HALF), 0) == lax.broadcasted_iota(jnp.int32, (8, HALF), 1) // HEAD_DIM
    ).astype(BF)
    delta[...] = dot_nt(picks, high) + dot_nt(picks, rest)
    ep_row, ep_col = episode_columns(ep)
    for i in range(4):
        lo, hi = first_key(i), (i + 1) * BLOCK
        key_at = lo + lax.broadcasted_iota(jnp.int32, (hi - lo, BLOCK), 0)
        row_at = i * BLOCK + lax.broadcasted_iota(jnp.int32, (hi - lo, BLOCK), 1)
        same = ep_col[lo:hi, 0:1] == ep_row[0:1, i * BLOCK : hi]
        bias[i, 0 : hi - lo, :] = jnp.where((key_at <= row_at) & same, 0.0, MASKED)

    @pl.loop(0, 3)
    def _(p):
        at = pl.multiple_of(p * PAIR, PAIR)
        d_k[...] = jnp.zeros_like(d_k)
        d_v[...] = jnp.zeros_like(d_v)
        for i in range(4):
            lo, hi = first_key(i), (i + 1) * BLOCK
            rows = slice(i * BLOCK, hi)
            q = qkv[rows, pl.ds(at, PAIR)]
            k = qkv[lo:hi, pl.ds(HALF + at, PAIR)]
            v = qkv[lo:hi, pl.ds(2 * HALF + at, PAIR)]
            dc = d_ctx[rows, pl.ds(at, PAIR)]
            d_q = jnp.zeros((BLOCK, PAIR), F32)
            for h in range(2):

                def only(array):
                    lane = lax.broadcasted_iota(jnp.int32, array.shape, 1)
                    mine = (lane >= HEAD_DIM) if h else (lane < HEAD_DIM)
                    return jnp.where(mine, array, jnp.zeros_like(array))

                q_h, dc_h = only(q), only(dc)
                s = dot_nt(k, q_h) + bias[i, 0 : hi - lo, :]
                prob = jnp.exp(s - lse[pl.ds(2 * p + h, 1), rows])
                d_p = dot_nt(v, dc_h)
                d_s = (prob * (d_p - delta[pl.ds(2 * p + h, 1), rows])).astype(BF)
                d_v[lo:hi] += dot(prob.astype(BF), dc_h)
                d_k[lo:hi] += dot(d_s, q_h)
                d_q += dot_tn(d_s, only(k))
            d_qkv[rows, pl.ds(at, PAIR)] = (d_q * 0.125).astype(BF)
        d_qkv[:, pl.ds(HALF + at, PAIR)] = d_k[...].astype(BF)
        d_qkv[:, pl.ds(2 * HALF + at, PAIR)] = d_v[...].astype(BF)

    for b in range(4):
        rows = slice(b * BLOCK, (b + 1) * BLOCK)
        part = dot_nt(d_qkv[rows, 0:HALF], wq[0])
        part += dot_nt(d_qkv[rows, HALF : 2 * HALF], wk[0])
        part += dot_nt(d_qkv[rows, 2 * HALF : 3 * HALF], wv[0])

        @pl.when(core == b % 2)
        def _():
            part_own[b // 2] = part

        @pl.when(core != b % 2)
        def _():
            part_oth[b // 2] = part.astype(BF)


def attention_backward(scalars, layer, gr_own, gr_rcv, qkv, ctx, lse, episodes, ep_spec, w_out, w_qkv, deps=()):
    columns = [pl.BlockSpec((1, D, HALF), partial(lambda j, i, sc: (layer, 0, 2 * j + sc[C]), j)) for j in range(3)]
    block = whole((2, BLOCK, D))
    return call(
        attn_back_body,
        (1,),
        [
            block,
            block,
            whole((LENGTH, 3 * HALF)),
            whole((LENGTH, HALF)),
            whole((8, LENGTH)),
            ep_spec,
            pl.BlockSpec((1, HALF, D), lambda i, sc: (layer, sc[C], 0)),
        ]
        + columns,
        [whole((LENGTH, 3 * HALF)), block, block],
        [shape((LENGTH, 3 * HALF), BF), shape((2, BLOCK, D), F32), shape((2, BLOCK, D), BF)],
        [
            pltpu.VMEM((4, 3 * BLOCK, BLOCK), F32),
            pltpu.VMEM((LENGTH, HALF), BF),
            pltpu.VMEM((8, LENGTH), F32),
            pltpu.VMEM((LENGTH, PAIR), F32),
            pltpu.VMEM((LENGTH, PAIR), F32),
        ],
        (2.5e9 + 6e9, 12e6),
        deps,
    )(scalars, gr_own, gr_rcv, qkv, ctx, lse, episodes, w_out, w_qkv, w_qkv, w_qkv)


def attn_weight_body(
    sc, own, other, gain, shift, d_qkv, gr_own, gr_rcv, ctx_full, ctx_oth, ctx_rcv, keep, send, n_t, late
):
    core, x = sc[C], sc[X]
    own, other = own.at[0, :, 0], other.at[0, :, 0]
    for b in range(4):
        rows = slice(b * BLOCK, (b + 1) * BLOCK)
        n_t[:, rows] = norm_low(in_order(own, other, b, core), gain[0], shift[0]).T

    def columns(ref):
        rows = ref[...].reshape(ROWS, D)
        return jnp.where(core == 0, rows[:, 0:HALF], rows[:, HALF:D]).T

    a, b = ctx_oth[...].reshape(ROWS, HALF), ctx_rcv[...].reshape(ROWS, HALF)
    far = jnp.concatenate([jnp.where(core == 0, a, b), jnp.where(core == 0, b, a)], 1)
    g_out = (dot(columns(gr_own), ctx_full[...]) + dot(columns(gr_rcv), far)).astype(BF).T

    def grad(j):
        if j == 3:
            return g_out
        return dot(n_t[...], d_qkv[:, j * HALF : (j + 1) * HALF]).astype(BF)

    for j in range(2):
        first, second = grad(j), grad(j + 2)
        mine, yours = jnp.where(x == 0, first, second), jnp.where(x == 0, second, first)
        for piece in range(8):
            py, pz = place(sc, piece)
            keep[py, pz, j] = mine[piece * PART : (piece + 1) * PART]
            send[py, pz, j] = yours[piece * PART : (piece + 1) * PART]


def attention_weights(
    scalars, layer, own, own_spec, other, other_spec, gain, shift, d_qkv, gr_own, gr_rcv, ctx_full, ctx_oth, ctx_rcv, deps=()):
    packed = (2, 4, 2, PART, HALF)
    block = whole((2, BLOCK, D))
    return call(
        attn_weight_body,
        (1,),
        [
            own_spec,
            other_spec,
            at_layer((1, 1, D), layer),
            at_layer((1, 1, D), layer),
            whole((LENGTH, 3 * HALF)),
            block,
            block,
            whole((ROWS, D)),
            whole((2, BLOCK, HALF)),
            whole((2, BLOCK, HALF)),
        ],
        [whole(packed), whole(packed)],
        [shape(packed, BF), shape(packed, BF)],
        [pltpu.VMEM((D, LENGTH), BF), pltpu.VMEM((8, PAIR), F32)],
        (2.5e9, 12e6),
        deps,
    )(scalars, own, other, gain, shift, d_qkv, gr_own, gr_rcv, ctx_full, ctx_oth, ctx_rcv)


def to_core(value):
    return lax.ppermute(value, "section", [(0, 1), (1, 0), (2, 3), (3, 2)])


def to_chip(value):
    return lax.ppermute(value, "section", [(0, 2), (2, 0), (1, 3), (3, 1)])


def to_dp(value, distance):
    return lax.ppermute(value, "dp", [(i, i ^ distance) for i in range(8)])


def total(*terms):
    out = terms[0].astype(F32)
    for term in terms[1:]:
        out = out + term.astype(F32)
    return out.astype(BF)


def reduced_any(keep, send, first):
    both = total(keep, first(send))
    count = both.shape[2]
    return jnp.moveaxis(both, 0, 1).reshape(8, count, PART, HALF)


def gathered(share):
    far, near = to_chip(share), to_core(share)
    return share, far, near, to_core(far)


def unpack_body(sc, *refs):
    shares, (up, down, qkv, out) = refs[:16], refs[16:]
    for layer in range(2):
        for n in range(4):
            x, core = sc[X] ^ (n % 2), sc[C] ^ (n // 2)
            ffn, attn = shares[layer * 8 + n], shares[layer * 8 + 4 + n]
            for j in range(2):
                at = pl.multiple_of(x * 4 * HALF + core * 2 * HALF + j * HALF, PAIR)
                up[layer, :, pl.ds(at, HALF)] = ffn[j].astype(F32)
                rows = pl.ds(pl.multiple_of(core * 2 * PART + j * PART, 8), PART)
                down[layer, rows, pl.ds(pl.multiple_of(x * HALF, PAIR), HALF)] = ffn[2 + j].astype(F32)
            side = pl.multiple_of(core * HALF, PAIR)
            qkv[layer, :, pl.ds(pl.multiple_of(x * 2 * D + side, PAIR), HALF)] = attn[0].astype(F32)

            @pl.when(x == 0)
            def _():
                qkv[layer, :, pl.ds(pl.multiple_of(D + side, PAIR), HALF)] = attn[1].astype(F32)

            @pl.when(x == 1)
            def _():
                out[layer, :, pl.ds(side, HALF)] = attn[1].astype(F32)


def unpacked(scalars, shares):
    dims = ((2, PART, FF), (2, 4 * PART, D), (2, PART, 3 * D), (2, PART, D))
    return call(
        unpack_body,
        (1,),
        [whole(share.shape) for share in shares],
        [whole(d) for d in dims],
        [shape(d, F32) for d in dims],
        [],
        (1e6, 11e6),
    )(scalars, *shares)


def on_device(
    tokens,
    episodes,
    attn_gain,
    attn_shift,
    qkv_weight,
    out_weight,
    out_bias,
    ffn_gain,
    ffn_shift,
    up_weight,
    up_bias,
    down_weight,
    down_bias,
    cotangent,
):
    replicas = lax.axis_size("dp")
    section = lax.axis_index("section")
    replica = lax.axis_index("dp")
    chip, core = section // 2, section % 2
    direct = replicas == 8
    y, z = (replica % 2, replica // 2) if direct else (0, 0)
    scalars = jnp.stack([jnp.asarray(v, jnp.int32) for v in (chip, core, y, z)])

    stream = tokens.reshape(2, 2, 2, BLOCK, D)
    cot = cotangent.reshape(2, 2, 2, BLOCK, D)
    eps = episodes.reshape(2, 1, LENGTH)
    ep_spec = pl.BlockSpec((1, 1, LENGTH), lambda i, sc: (sc[X], 0, 0))

    def input_spec(micro, side):
        return pl.BlockSpec((1, 2, 1, BLOCK, D), lambda i, sc: (micro(sc[X]), 0, side(sc[C]), 0, 0))

    same, flip = (lambda v: v), (lambda v: 1 - v)
    own_in, other_in, far_in = input_spec(same, same), input_spec(same, flip), input_spec(flip, same)
    local = pl.BlockSpec((1, 2, 1, BLOCK, D), lambda i, sc: (0, 0, 0, 0, 0))

    def rows5(value):
        return value.reshape(1, 2, 1, BLOCK, D)

    def vec(array):
        return array.reshape(2, 1, -1)

    a_gain, a_shift, b_out = vec(attn_gain), vec(attn_shift), vec(out_bias)
    f_gain, f_shift, b_up, b_down = vec(ffn_gain), vec(ffn_shift), vec(up_bias), vec(down_bias)

    kept = []
    own, own_spec, other, other_spec = stream, own_in, stream, other_in
    for layer in range(2):
        qkv, ctx, ctx_own, ctx_oth, lse = attention_forward(
            scalars, layer, own, own_spec, other, other_spec, eps, ep_spec, a_gain, a_shift, qkv_weight
        )
        ctx_rcv = to_core(ctx_oth)
        ctx_far = to_core(ctx_own)
        s2, ctx_full, act, slope, *result = ffn_forward(
            scalars,
            layer,
            layer == 1,
            ctx_own,
            ctx_rcv,
            own,
            own_spec,
            (out_weight, b_out, f_gain, f_shift, up_weight, b_up, down_weight, b_down),
        )
        s2_o = to_chip(s2)
        kept.append((own, own_spec, other, other_spec, qkv, ctx, ctx_oth, ctx_far, ctx_full, lse, s2, s2_o, act, slope))
        if layer == 0:
            s3 = result[0]
            own, own_spec, other, other_spec = rows5(s3), local, rows5(to_core(s3)), local
    final_keep, final_send = result

    def ffn_back(layer, grad, grad_spec, deps=()):
        kept_now = kept[layer]
        s2, slope = kept_now[10], kept_now[13]
        return ffn_backward(scalars, layer, grad, grad_spec, s2, slope, (f_gain, up_weight, down_weight), deps)

    def ffn_grads(layer, grad, grad_spec, grad_o, grad_o_spec, dh, deps=()):
        s2, s2_o, act, slope = kept[layer][10:]
        weights = (f_gain, f_shift, up_weight, b_up, down_weight)
        return ffn_weights(
            scalars, layer, grad, grad_spec, grad_o, grad_o_spec, s2, s2_o, act, dh, weights, deps
        )

    def attn_back(layer, ds, ds_rcv, deps=()):
        own, own_spec, other, other_spec, qkv, ctx, ctx_oth, ctx_far, ctx_full, lse = kept[layer][:10]
        return attention_backward(
            scalars, layer, ds, ds_rcv, qkv, ctx, lse, eps, ep_spec, out_weight, qkv_weight, deps
        )

    def attn_grads(layer, ds, ds_rcv, d_qkv, deps=()):
        own, own_spec, other, other_spec, qkv, ctx, ctx_oth, ctx_far, ctx_full, lse = kept[layer][:10]
        return attention_weights(
            scalars, layer, own, own_spec, other, other_spec, a_gain, a_shift, d_qkv, ds, ds_rcv, ctx_full, ctx_oth,
            ctx_far, deps,
        )

    def attn_norm(layer, ds, part_own, part_rcv, deps=()):
        own, own_spec = kept[layer][:2]
        return attention_norm_back(
            scalars, layer, layer == 0, ds, part_own, part_rcv, own, own_spec, a_gain, deps
        )

    def y_sum(keep, got):
        return total(keep[1], got[1])

    def z_sums(keep, got, y_got):
        return [total(keep[0, k], got[0, k], y_got[k]) for k in (1, 2, 3)]

    def last_sum(keep, got, y_got, z_got):
        return total(keep[0, 0], got[0, 0], y_got[0], *z_got)

    def z_moved(sums):
        return [to_dp(value, 2 * k) for k, value in zip((1, 2, 3), sums)]

    def small_of(a_small, f_small, g_up_bias):
        return jnp.concatenate([a_small, f_small, g_up_bias.reshape(4, D)])

    if direct:
        dh1, ds1, fsmall1, ub1 = ffn_back(1, cot, own_in)
        ds1_rcv = to_core(ds1)
        fk1, fs1 = ffn_grads(1, cot, own_in, cot, far_in, dh1)
        fg1 = to_core(fs1)
        d_qkv1, part1, part1_oth = attn_back(1, ds1, ds1_rcv, [fk1])
        part1_rcv = to_core(part1_oth)
        fys1 = y_sum(fk1, fg1)
        fy1 = to_dp(fys1, 1)
        g0, asmall1 = attn_norm(1, ds1, part1, part1_rcv, [fys1])
        g0_o = to_chip(g0)
        ak1, as1 = attn_grads(1, ds1, ds1_rcv, d_qkv1, [g0])
        ag1 = to_chip(as1)
        dh0, ds0, fsmall0, ub0 = ffn_back(0, rows5(g0), local, [ak1])
        ds0_rcv = to_core(ds0)
        fzs1 = z_sums(fk1, fg1, fy1)
        fz1 = z_moved(fzs1)
        fk0, fs0 = ffn_grads(0, rows5(g0), local, rows5(g0_o), local, dh0, fzs1)
        fg0 = to_core(fs0)
        ays1 = y_sum(ak1, ag1)
        ay1 = to_dp(ays1, 1)
        d_qkv0, part0, part0_oth = attn_back(0, ds0, ds0_rcv, [fk0, ays1])
        part0_rcv = to_core(part0_oth)
        fys0 = y_sum(fk0, fg0)
        fy0 = to_dp(fys0, 1)
        azs1 = z_sums(ak1, ag1, ay1)
        az1 = z_moved(azs1)
        f1 = last_sum(fk1, fg1, fy1, fz1)
        f1_all = gathered(f1)
        ak0, as0 = attn_grads(0, ds0, ds0_rcv, d_qkv0, [fys0, f1] + azs1)
        ag0 = to_chip(as0)
        *result, asmall0 = attn_norm(0, ds0, part0, part0_rcv, [ak0])
        fz0 = z_moved(z_sums(fk0, fg0, fy0))
        a1_all = gathered(last_sum(ak1, ag1, ay1, az1))
        ay0 = to_dp(y_sum(ak0, ag0), 1)
        az0 = z_moved(z_sums(ak0, ag0, ay0))
        f0_all = gathered(last_sum(fk0, fg0, fy0, fz0))
        a0_all = gathered(last_sum(ak0, ag0, ay0, az0))
        ups, downs, qkvs, outs = unpacked(scalars, f0_all + a0_all + f1_all + a1_all)

        def small_pieces(a_small, f_small, g_up_bias):
            vectors = jnp.concatenate([a_small, f_small]).reshape(6, 8, PART).transpose(1, 0, 2)
            return jnp.concatenate([vectors, g_up_bias.reshape(8, 4, PART)], 1)

        small = jnp.concatenate([small_pieces(asmall0, fsmall0, ub0), small_pieces(asmall1, fsmall1, ub1)], 1)
        small = small + to_core(small)
        small = small + to_chip(small)

        def near(distance):
            return lax.dynamic_index_in_dim(small, replica ^ distance, 0, keepdims=False)

        halves = jnp.stack([near(2 * k + 1) for k in range(4)])
        y_got = to_dp(halves, 1)
        small = near(0) + y_got[0] + sum(to_dp(near(2 * k) + y_got[k], 2 * k) for k in (1, 2, 3))
        small = small.reshape(2, 10, PART)

        def piece(first):
            return small[:, first]

        up_bias_grad = small[:, 6:10].reshape(2, 4 * PART)
    else:
        grads = [None, None]
        smalls = [None, None]
        grad, grad_spec, grad_o, grad_o_spec = cot, own_in, cot, far_in
        for layer in (1, 0):
            dh, ds, f_small, g_up_bias = ffn_back(layer, grad, grad_spec)
            ds_rcv = to_core(ds)
            f_keep, f_send = ffn_grads(layer, grad, grad_spec, grad_o, grad_o_spec, dh)
            d_qkv, part_own, part_oth = attn_back(layer, ds, ds_rcv)
            a_keep, a_send = attn_grads(layer, ds, ds_rcv, d_qkv)
            *result, a_small = attn_norm(layer, ds, part_own, to_core(part_oth))
            if layer == 1:
                grad, grad_spec = rows5(result[0]), local
                grad_o, grad_o_spec = rows5(to_chip(result[0])), local
            smalls[layer] = small_of(a_small, f_small, g_up_bias)
            ordered = []
            for share in (reduced_any(f_keep, f_send, to_core), reduced_any(a_keep, a_send, to_chip)):
                mine, far, near, both = gathered(share)
                here = jnp.stack([jnp.where(chip == 0, mine, far), jnp.where(chip == 0, far, mine)])
                there = jnp.stack([jnp.where(chip == 0, near, both), jnp.where(chip == 0, both, near)])
                pair = jnp.stack([jnp.where(core == 0, here, there), jnp.where(core == 0, there, here)], 1)
                ordered.append(pair.astype(F32))
            f_all, a_all = ordered
            up = f_all[:, :, :, 0:2].transpose(2, 4, 0, 1, 3, 5).reshape(D, FF)
            down = f_all[:, :, :, 2:4].transpose(2, 1, 3, 4, 0, 5).reshape(FF, D)
            q_k = a_all[0].transpose(1, 3, 2, 0, 4).reshape(D, 2 * D)
            v = a_all[1, :, :, 0].transpose(1, 2, 0, 3).reshape(D, D)
            out = a_all[1, :, :, 1].transpose(1, 2, 0, 3).reshape(D, D)
            grads[layer] = [
                lax.psum_scatter(array, "dp", scatter_dimension=0, tiled=True)
                for array in (up, down, jnp.concatenate([q_k, v], 1), out)
            ]
        ups, downs, qkvs, outs = (jnp.stack(pair) for pair in zip(*grads))
        small = lax.psum(jnp.stack(smalls), ("section", "dp"))

        def mine_of(rows):
            width = rows.shape[-1] // replicas
            return lax.dynamic_slice_in_dim(rows, replica * width, width, 1)

        def piece(first):
            return mine_of(small[:, first])

        up_bias_grad = mine_of(small[:, 6:10].reshape(2, FF))
    input_keep, input_send = result

    def placed(keep, send):
        got = to_chip(send).astype(F32)
        return jnp.stack([jnp.where(chip == 0, keep, got), jnp.where(chip == 0, got, keep)])[:, None]

    final_out, input_out = placed(final_keep, final_send), placed(input_keep, input_send)
    return (
        final_out,
        input_out,
        piece(0),
        piece(1),
        qkvs,
        outs,
        piece(2),
        piece(3),
        piece(4),
        ups,
        up_bias_grad,
        downs,
        piece(5),
    )


def solution(mesh):
    split = P(None, "dp", None, None)
    placed = (split, P(None, "dp", None)) + (P(),) * 11 + (split,)
    rows = P(None, "dp", "section", None)
    vector, matrix = P(None, "dp"), P(None, "dp", None)
    return jax.shard_map(
        on_device,
        mesh=mesh,
        in_specs=placed,
        out_specs=(
            rows,
            rows,
            vector,
            vector,
            matrix,
            matrix,
            vector,
            vector,
            vector,
            matrix,
            vector,
            matrix,
            vector,
        ),
        check_vma=False,
    )
```

```python
from functools import partial

import jax
import jax.numpy as jnp
from jax import lax
from jax.experimental import pallas as pl
from jax.experimental.pallas import tpu as pltpu
from jax.sharding import PartitionSpec as P

BF = jnp.bfloat16
F32 = jnp.float32
EPS = 1e-05
MASKED = -1e30
D = 768
HALF = 384
PAIR = 128
HEAD_DIM = 64
FF = 3072
LENGTH = 1024
BLOCK = 256
ROWS = 512
PART = 96
GELU_A = 0.7978845608028654
GELU_B = GELU_A * 0.044715


def dot(a, b):
    return jnp.dot(a, b, preferred_element_type=F32)


def dot_nt(a, b):
    return lax.dot_general(a, b, (((1,), (1,)), ((), ())), preferred_element_type=F32)


def dot_tn(a, b):
    return lax.dot_general(a, b, (((0,), (0,)), ((), ())), preferred_element_type=F32)


def normalise(rows):
    center = rows - jnp.mean(rows, -1, keepdims=True)
    spread = lax.rsqrt(jnp.mean(center * center, -1, keepdims=True) + EPS)
    return center * spread, spread


def norm_low(rows, gain, shift):
    unit, _ = normalise(rows.astype(F32))
    return (unit * gain + shift).astype(BF)


def call(body, grid, in_specs, out_specs, out_shape, scratch, cost, deps=()):
    count = len(in_specs)

    def with_deps(sc, *refs):
        return body(sc, *refs[:count], *refs[count + len(deps) :])

    kernel = pl.pallas_call(
        with_deps,
        grid_spec=pltpu.PrefetchScalarGridSpec(
            num_scalar_prefetch=1,
            grid=grid,
            in_specs=list(in_specs) + [pl.BlockSpec(memory_space=pl.ANY)] * len(deps),
            out_specs=out_specs,
            scratch_shapes=scratch,
        ),
        out_shape=out_shape,
        compiler_params=pltpu.CompilerParams(vmem_limit_bytes=32 * 1024 * 1024),
        cost_estimate=pl.CostEstimate(flops=int(5 * cost[0]), bytes_accessed=int(5 * cost[1]), transcendentals=0),
    )
    return lambda *args: kernel(*args, *deps)


def shape(dims, dtype):
    return jax.ShapeDtypeStruct(dims, dtype)


def stored(dims, dtype):
    return pltpu.MemorySpace.HBM(dims, dtype)


def from_hbm(array):
    return pltpu.with_memory_space_constraint(array, pltpu.MemorySpace.HBM)


def whole(dims):
    count = len(dims)
    return pl.BlockSpec(dims, lambda i, sc: (0,) * count)


def at_layer(dims, layer):
    count = len(dims) - 1
    return pl.BlockSpec(dims, lambda i, sc: (layer,) + (0,) * count)


X, C, Y, Z = 0, 1, 2, 3


def in_order(own, other, block, core):
    return jnp.where(core == block % 2, own[block // 2], other[block // 2])


def episode_columns(ep_ref):
    row = jnp.broadcast_to(ep_ref[...].reshape(1, LENGTH).astype(F32), (PAIR, LENGTH))
    return row, row.T


def first_key(i):
    return max(0, i - 2) * BLOCK


def attn_fwd_body(sc, own, other, ep, gain, shift, wq, wk, wv, qkv, ctx, ctx_own, ctx_oth, lse, bias, vext, lse_cols):
    core = sc[C]
    own, other = own.at[0, :, 0], other.at[0, :, 0]
    for b in range(4):
        rows = slice(b * BLOCK, (b + 1) * BLOCK)
        normed = norm_low(in_order(own, other, b, core), gain[0], shift[0])
        qkv[rows, 0:HALF] = (dot(normed, wq[0]).astype(BF) * 0.125).astype(BF)
        qkv[rows, HALF : 2 * HALF] = dot(normed, wk[0]).astype(BF)
        qkv[rows, 2 * HALF : 3 * HALF] = dot(normed, wv[0]).astype(BF)
    ep_row, ep_col = episode_columns(ep)
    for i in range(4):
        lo, hi = first_key(i), (i + 1) * BLOCK
        key_at = lo + lax.broadcasted_iota(jnp.int32, (BLOCK, hi - lo), 1)
        row_at = i * BLOCK + lax.broadcasted_iota(jnp.int32, (BLOCK, hi - lo), 0)
        same = ep_col[i * BLOCK : hi, 0:1] == ep_row[0:1, lo:hi]
        bias[i, :, 0 : hi - lo] = jnp.where((key_at <= row_at) & same, 0.0, MASKED)
    vext[:, PAIR:] = jnp.ones((LENGTH, PAIR), BF)
    lane = lax.broadcasted_iota(jnp.int32, (BLOCK, PAIR), 1)

    @pl.loop(0, 3)
    def _(p):
        at = pl.multiple_of(p * PAIR, PAIR)
        vext[:, 0:PAIR] = qkv[:, pl.ds(2 * HALF + at, PAIR)]
        for i in range(4):
            lo, hi = first_key(i), (i + 1) * BLOCK
            rows = slice(i * BLOCK, hi)
            q = qkv[rows, pl.ds(at, PAIR)]
            k = qkv[lo:hi, pl.ds(HALF + at, PAIR)]
            outs = []
            for h in range(2):
                mine = (lane >= HEAD_DIM) if h else (lane < HEAD_DIM)
                s = dot_nt(jnp.where(mine, q, jnp.zeros_like(q)), k) + bias[i, :, 0 : hi - lo]
                top = jnp.max(s, -1, keepdims=True)
                prob = jnp.exp(s - top).astype(BF)
                o = dot(prob, vext[lo:hi, :])
                total = o[:, PAIR : PAIR + 1]
                outs.append(o[:, 0:PAIR] / total)
                lse_cols[rows, :] = jnp.where(lane == 2 * p + h, top + jnp.log(total), lse_cols[rows, :])
            ctx[rows, pl.ds(at, PAIR)] = jnp.where(lane < HEAD_DIM, outs[0], outs[1]).astype(BF)

    lse[...] = lse_cols[...].T[0:8]
    for b in range(4):
        piece = ctx[b * BLOCK : (b + 1) * BLOCK]

        @pl.when(core == b % 2)
        def _():
            ctx_own[b // 2] = piece

        @pl.when(core != b % 2)
        def _():
            ctx_oth[b // 2] = piece


def attention_forward(scalars, layer, own, own_spec, other, other_spec, episodes, ep_spec, gain, shift, w_qkv):
    columns = [pl.BlockSpec((1, D, HALF), partial(lambda j, i, sc: (layer, 0, 2 * j + sc[C]), j)) for j in range(3)]
    return call(
        attn_fwd_body,
        (1,),
        [own_spec, other_spec, ep_spec, at_layer((1, 1, D), layer), at_layer((1, 1, D), layer)] + columns,
        [
            whole((LENGTH, 3 * HALF)),
            whole((LENGTH, HALF)),
            whole((2, BLOCK, HALF)),
            whole((2, BLOCK, HALF)),
            whole((8, LENGTH)),
        ],
        [
            stored((LENGTH, 3 * HALF), BF),
            stored((LENGTH, HALF), BF),
            shape((2, BLOCK, HALF), BF),
            shape((2, BLOCK, HALF), BF),
            shape((8, LENGTH), F32),
        ],
        [
            pltpu.VMEM((4, BLOCK, 3 * BLOCK), F32),
            pltpu.VMEM((LENGTH, 2 * PAIR), BF),
            pltpu.VMEM((LENGTH, PAIR), F32),
        ],
        (1.8e9 + 2.4e9, 8e6),
    )(scalars, own, other, episodes, gain, shift, *[from_hbm(w_qkv)] * 3)


def gelu_parts(u):
    cubic = GELU_B * (u * u)
    t = jnp.tanh(u * (GELU_A + cubic))
    half = 0.5 * t + 0.5
    active = u * half
    slope = half + (active * (1.0 - half)) * (6.0 * cubic + 2.0 * GELU_A)
    return active, slope


FT = 512


def ffn_fwd_body(last, sc, ctx_own, ctx_rcv, own, w_out, b_out, gain, shift, w_up, b_up, w_down, b_down, *rest):
    if last:
        s2, ctx_full, act, slope, keep, send, normed, acc = rest
    else:
        s2, ctx_full, act, slope, s3, normed, acc = rest
    t = pl.program_id(0)
    core = sc[C]

    @pl.when(t == 0)
    def _():
        a, b = ctx_own[...].reshape(ROWS, HALF), ctx_rcv[...].reshape(ROWS, HALF)
        both = jnp.concatenate([jnp.where(core == 0, a, b), jnp.where(core == 0, b, a)], 1)
        ctx_full[...] = both
        stream = own[0, :, 0].reshape(ROWS, D).astype(F32) + dot(both, w_out[0]) + b_out[0]
        low = stream.astype(BF)
        s2[...] = low
        normed[...] = norm_low(low, gain[0], shift[0])
        acc[...] = low.astype(F32) + b_down[0]

    u = dot(normed[...], w_up[0]) + b_up[0]
    a, d = gelu_parts(u)
    a = a.astype(BF)
    act[...] = a
    slope[...] = d.astype(BF)
    acc[...] += dot(a, w_down[0])

    @pl.when(t == FF // FT - 1)
    def _():
        if last:
            x = sc[X]
            keep[...] = acc[pl.ds(pl.multiple_of(x * BLOCK, BLOCK), BLOCK)]
            send[...] = acc[pl.ds(pl.multiple_of((1 - x) * BLOCK, BLOCK), BLOCK)].astype(BF)
        else:
            s3[...] = acc[...].reshape(2, BLOCK, D).astype(BF)


def ffn_forward(scalars, layer, last, ctx_own, ctx_rcv, own, own_spec, weights, dep):
    w_out, b_out, gain, shift, w_up, b_up, w_down, b_down = weights
    vector = at_layer((1, 1, D), layer)
    out_specs = [
        whole((ROWS, D)),
        whole((ROWS, D)),
        pl.BlockSpec((ROWS, FT), lambda i, sc: (0, i)),
        pl.BlockSpec((ROWS, FT), lambda i, sc: (0, i)),
    ]
    out_shape = [shape((ROWS, D), BF), shape((ROWS, D), BF), stored((ROWS, FF), BF), stored((ROWS, FF), BF)]
    if last:
        out_specs += [whole((BLOCK, D)), whole((BLOCK, D))]
        out_shape += [shape((BLOCK, D), F32), shape((BLOCK, D), BF)]
    else:
        out_specs += [whole((2, BLOCK, D))]
        out_shape += [shape((2, BLOCK, D), BF)]
    return call(
        partial(ffn_fwd_body, last),
        (FF // FT,),
        [
            whole((2, BLOCK, HALF)),
            whole((2, BLOCK, HALF)),
            own_spec,
            at_layer((1, D, D), layer),
            vector,
            vector,
            vector,
            pl.BlockSpec((1, D, FT), lambda i, sc: (layer, 0, i)),
            pl.BlockSpec((1, 1, FT), lambda i, sc: (layer, 0, i)),
            pl.BlockSpec((1, FT, D), lambda i, sc: (layer, i, 0)),
            vector,
        ],
        out_specs,
        out_shape,
        [pltpu.VMEM((ROWS, D), BF), pltpu.VMEM((ROWS, D), F32)],
        (5.4e9, 20e6),
        () if dep is None else (dep,),
    )(scalars, ctx_own, ctx_rcv, own, from_hbm(w_out), b_out, gain, shift, from_hbm(w_up), b_up, from_hbm(w_down), b_down)


def norm_back(d_normed, rows, gain):
    unit, spread = normalise(rows)
    d_unit = d_normed * gain
    first = jnp.mean(d_unit, -1, keepdims=True)
    second = jnp.mean(d_unit * unit, -1, keepdims=True)
    d_rows = spread * (d_unit - first - unit * second)
    return d_rows, jnp.sum(d_normed * unit, 0, keepdims=True), jnp.sum(d_normed, 0, keepdims=True)


def small_rows(*vectors):
    return jnp.concatenate(vectors + (jnp.zeros((8 - len(vectors), D), F32),))


def attn_norm_body(last, sc, grad, part, part_rcv, own, gain, *rest):
    before, outs = rest[:3] if last else (), rest[3:] if last else rest
    grad_rows = grad[...].reshape(ROWS, D).astype(F32)
    d_normed = part[...].reshape(ROWS, D) + part_rcv[...].reshape(ROWS, D).astype(F32)
    d_rows, g_gain, g_shift = norm_back(d_normed, own[0, :, 0].reshape(ROWS, D).astype(F32), gain[0])
    total = grad_rows + d_rows
    small = outs[-1]
    small[0:8] = small_rows(g_gain, g_shift, jnp.sum(grad_rows, 0, keepdims=True))
    for j, ref in enumerate(before):
        small[8 * (j + 1) : 8 * (j + 2)] = ref[...]
    if last:
        keep, send = outs[0:2]
        keep[...] = jnp.where(sc[X] == 0, total[0:BLOCK], total[BLOCK:ROWS])
        send[...] = jnp.where(sc[X] == 0, total[BLOCK:ROWS], total[0:BLOCK]).astype(BF)
    else:
        outs[0][...] = total.astype(BF).reshape(2, BLOCK, D)


def attention_norm_back(scalars, layer, grad, part, part_rcv, own, own_spec, gain, smalls=(), deps=()):
    block = whole((2, BLOCK, D))
    last = bool(smalls)
    if last:
        out_specs = [whole((BLOCK, D)), whole((BLOCK, D))]
        out_shape = [shape((BLOCK, D), F32), shape((BLOCK, D), BF)]
    else:
        out_specs, out_shape = [block], [shape((2, BLOCK, D), BF)]
    rows = 8 * (1 + len(smalls))
    return call(
        partial(attn_norm_body, last),
        (1,),
        [block, block, block, own_spec, at_layer((1, 1, D), layer)] + [whole((8, D))] * len(smalls),
        out_specs + [whole((rows, D))],
        out_shape + [shape((rows, D), F32)],
        [],
        (2e8, 5e6),
        deps,
    )(scalars, grad, part, part_rcv, own, gain, *smalls)


BT = 768


def ffn_back_body(sc, grad, s2, gain, w_up, w_down, slope, dh, ds, small, acc):
    t = pl.program_id(0)
    low = grad[0, :, 0].reshape(ROWS, D)
    d_act = dot_nt(low, w_down[0])
    d_hidden = d_act * slope[...].astype(F32)
    d_low = d_hidden.astype(BF)
    dh[...] = d_low
    small[pl.ds(4 + t, 1)] = jnp.sum(d_low.astype(F32), 0, keepdims=True)
    part = dot_nt(d_low, w_up[0])

    @pl.when(t == 0)
    def _():
        acc[...] = part

    @pl.when(t > 0)
    def _():
        acc[...] += part

    @pl.when(t == FF // BT - 1)
    def _():
        rows = low.astype(F32)
        d_rows, g_gain, g_shift = norm_back(acc[...], s2[...].astype(F32), gain[0])
        ds[...] = (rows + d_rows).astype(BF).reshape(2, BLOCK, D)
        small[0:4] = small_rows(g_gain, g_shift, jnp.sum(rows, 0, keepdims=True))[0:4]


def ffn_backward(scalars, layer, grad, grad_spec, s2, slope, weights, deps=()):
    gain, w_up, w_down = weights
    return call(
        ffn_back_body,
        (FF // BT,),
        [
            grad_spec,
            whole((ROWS, D)),
            at_layer((1, 1, D), layer),
            pl.BlockSpec((1, D, BT), lambda i, sc: (layer, 0, i)),
            pl.BlockSpec((1, BT, D), lambda i, sc: (layer, i, 0)),
            pl.BlockSpec((ROWS, BT), lambda i, sc: (0, i)),
        ],
        [
            pl.BlockSpec((ROWS, BT), lambda i, sc: (0, i)),
            whole((2, BLOCK, D)),
            whole((8, D)),
        ],
        [stored((ROWS, FF), BF), shape((2, BLOCK, D), BF), shape((8, D), F32)],
        [pltpu.VMEM((ROWS, D), F32)],
        (4.9e9, 18e6),
        deps,
    )(scalars, grad, s2, gain, from_hbm(w_up), from_hbm(w_down), from_hbm(slope))


def place(sc, piece):
    return (piece % 2) ^ sc[Y], (piece // 2) ^ sc[Z]


def ffn_weight_body(
    sc, grad, grad_o, s2, s2_o, gain, shift, act, dh, w_up, b_up, w_down, keep, send, n_t, n_o, n_t_o, g_t, g_t_o
):
    t = pl.program_id(0)
    core = sc[C]
    low, low_o = grad[0, :, 0].reshape(ROWS, D), grad_o[0, :, 0].reshape(ROWS, D)

    @pl.when(t == 0)
    def _():
        n_t[...] = norm_low(s2[...], gain[0], shift[0]).T
        other = norm_low(s2_o[...], gain[0], shift[0])
        n_o[...] = other
        n_t_o[...] = other.T
        x = sc[X]
        g_t[...] = jnp.where(x == 0, low[:, 0:HALF], low[:, HALF:D]).T
        g_t_o[...] = jnp.where(x == 0, low_o[:, 0:HALF], low_o[:, HALF:D]).T

    u = dot(n_o[...], w_up[0]) + b_up[0]
    active_o, slope_o = gelu_parts(u)

    @pl.when(t < 2)
    def _():
        dh_o = (dot_nt(low_o, w_down[0]) * slope_o).astype(BF)
        g_up = (dot(n_t[...], dh[...]) + dot(n_t_o[...], dh_o)).astype(BF)
        for ref, when in ((send, 0), (keep, 1)):

            @pl.when(t == when)
            def _():
                for piece in range(8):
                    py, pz = place(sc, piece)
                    for j in range(2):
                        ref[py, pz, j] = g_up[piece * PART : (piece + 1) * PART, j * HALF : (j + 1) * HALF]

    g_down = (dot(g_t[...], act[...]) + dot(g_t_o[...], active_o.astype(BF))).astype(BF).T
    tile = ffn_tile(t, sc)
    for half in range(2):
        py, pz = place(sc, 2 * tile + half)
        for j in range(2):
            first = g_down[half * HALF + j * PART : half * HALF + (j + 1) * PART]
            second = g_down[half * HALF + (j + 2) * PART : half * HALF + (j + 3) * PART]
            keep[py, pz, 2 + j] = jnp.where(core == 0, first, second)
            send[py, pz, 2 + j] = jnp.where(core == 0, second, first)


def ffn_tile(step, sc):
    mine = 2 * sc[X]
    rest = 2 - mine
    return jnp.where(step == 0, mine + 1 - sc[C], jnp.where(step == 1, mine + sc[C], rest + step - 2))


def ffn_weights(scalars, layer, grad, grad_spec, grad_o, grad_o_spec, s2, s2_o, act, dh, weights, deps=()):
    gain, shift, w_up, b_up, w_down = weights
    packed = (2, 4, 4, PART, HALF)
    return call(
        ffn_weight_body,
        (FF // BT,),
        [
            grad_spec,
            grad_o_spec,
            whole((ROWS, D)),
            whole((ROWS, D)),
            at_layer((1, 1, D), layer),
            at_layer((1, 1, D), layer),
            pl.BlockSpec((ROWS, BT), lambda i, sc: (0, ffn_tile(i, sc))),
            pl.BlockSpec((ROWS, BT), lambda i, sc: (0, ffn_tile(jnp.minimum(i, 1), sc))),
            pl.BlockSpec((1, D, BT), lambda i, sc: (layer, 0, ffn_tile(i, sc))),
            pl.BlockSpec((1, 1, BT), lambda i, sc: (layer, 0, ffn_tile(i, sc))),
            pl.BlockSpec((1, BT, D), lambda i, sc: (layer, ffn_tile(jnp.minimum(i, 1), sc), 0)),
        ],
        [whole(packed), whole(packed)],
        [stored(packed, BF), shape(packed, BF)],
        [
            pltpu.VMEM((D, ROWS), BF),
            pltpu.VMEM((ROWS, D), BF),
            pltpu.VMEM((D, ROWS), BF),
            pltpu.VMEM((HALF, ROWS), BF),
            pltpu.VMEM((HALF, ROWS), BF),
        ],
        (8.6e9, 22e6),
        deps,
    )(scalars, grad, grad_o, s2, s2_o, gain, shift, from_hbm(act), from_hbm(dh), from_hbm(w_up), b_up, from_hbm(w_down))


def attn_back_body(
    sc, gr_own, gr_rcv, qkv, ctx, lse, ep, w_out, wq, wk, wv, d_qkv, part_own, part_oth, bias, d_ctx, delta, d_k, d_v
):
    core = sc[C]
    for b in range(4):
        rows = slice(b * BLOCK, (b + 1) * BLOCK)
        d_ctx[rows] = dot_nt(in_order(gr_own, gr_rcv, b, core), w_out[0]).astype(BF)
    product = d_ctx[...].astype(F32) * ctx[...].astype(F32)
    high = product.astype(BF)
    rest = (product - high.astype(F32)).astype(BF)
    picks = (
        lax.broadcasted_iota(jnp.int32, (8, HALF), 0) == lax.broadcasted_iota(jnp.int32, (8, HALF), 1) // HEAD_DIM
    ).astype(BF)
    delta[...] = dot_nt(picks, high) + dot_nt(picks, rest)
    ep_row, ep_col = episode_columns(ep)
    for i in range(4):
        lo, hi = first_key(i), (i + 1) * BLOCK
        key_at = lo + lax.broadcasted_iota(jnp.int32, (hi - lo, BLOCK), 0)
        row_at = i * BLOCK + lax.broadcasted_iota(jnp.int32, (hi - lo, BLOCK), 1)
        same = ep_col[lo:hi, 0:1] == ep_row[0:1, i * BLOCK : hi]
        bias[i, 0 : hi - lo, :] = jnp.where((key_at <= row_at) & same, 0.0, MASKED)

    @pl.loop(0, 3)
    def _(p):
        at = pl.multiple_of(p * PAIR, PAIR)
        d_k[...] = jnp.zeros_like(d_k)
        d_v[...] = jnp.zeros_like(d_v)
        for i in range(4):
            lo, hi = first_key(i), (i + 1) * BLOCK
            rows = slice(i * BLOCK, hi)
            q = qkv[rows, pl.ds(at, PAIR)]
            k = qkv[lo:hi, pl.ds(HALF + at, PAIR)]
            v = qkv[lo:hi, pl.ds(2 * HALF + at, PAIR)]
            dc = d_ctx[rows, pl.ds(at, PAIR)]
            d_q = jnp.zeros((BLOCK, PAIR), F32)
            for h in range(2):

                def only(array):
                    lane = lax.broadcasted_iota(jnp.int32, array.shape, 1)
                    mine = (lane >= HEAD_DIM) if h else (lane < HEAD_DIM)
                    return jnp.where(mine, array, jnp.zeros_like(array))

                q_h, dc_h = only(q), only(dc)
                s = dot_nt(k, q_h) + bias[i, 0 : hi - lo, :]
                prob = jnp.exp(s - lse[pl.ds(2 * p + h, 1), rows])
                d_p = dot_nt(v, dc_h)
                d_s = (prob * (d_p - delta[pl.ds(2 * p + h, 1), rows])).astype(BF)
                d_v[lo:hi] += dot(prob.astype(BF), dc_h)
                d_k[lo:hi] += dot(d_s, q_h)
                d_q += dot_tn(d_s, only(k))
            d_qkv[rows, pl.ds(at, PAIR)] = (d_q * 0.125).astype(BF)
        d_qkv[:, pl.ds(HALF + at, PAIR)] = d_k[...].astype(BF)
        d_qkv[:, pl.ds(2 * HALF + at, PAIR)] = d_v[...].astype(BF)

    for b in range(4):
        rows = slice(b * BLOCK, (b + 1) * BLOCK)
        part = dot_nt(d_qkv[rows, 0:HALF], wq[0])
        part += dot_nt(d_qkv[rows, HALF : 2 * HALF], wk[0])
        part += dot_nt(d_qkv[rows, 2 * HALF : 3 * HALF], wv[0])

        @pl.when(core == b % 2)
        def _():
            part_own[b // 2] = part

        @pl.when(core != b % 2)
        def _():
            part_oth[b // 2] = part.astype(BF)


def attention_backward(scalars, layer, gr_own, gr_rcv, qkv, ctx, lse, episodes, ep_spec, w_out, w_qkv, deps=()):
    columns = [pl.BlockSpec((1, D, HALF), partial(lambda j, i, sc: (layer, 0, 2 * j + sc[C]), j)) for j in range(3)]
    block = whole((2, BLOCK, D))
    return call(
        attn_back_body,
        (1,),
        [
            block,
            block,
            whole((LENGTH, 3 * HALF)),
            whole((LENGTH, HALF)),
            whole((8, LENGTH)),
            ep_spec,
            pl.BlockSpec((1, HALF, D), lambda i, sc: (layer, sc[C], 0)),
        ]
        + columns,
        [whole((LENGTH, 3 * HALF)), block, block],
        [shape((LENGTH, 3 * HALF), BF), shape((2, BLOCK, D), F32), shape((2, BLOCK, D), BF)],
        [
            pltpu.VMEM((4, 3 * BLOCK, BLOCK), F32),
            pltpu.VMEM((LENGTH, HALF), BF),
            pltpu.VMEM((8, LENGTH), F32),
            pltpu.VMEM((LENGTH, PAIR), F32),
            pltpu.VMEM((LENGTH, PAIR), F32),
        ],
        (2.5e9 + 6e9, 12e6),
        deps,
    )(scalars, gr_own, gr_rcv, from_hbm(qkv), from_hbm(ctx), lse, episodes, from_hbm(w_out), *[from_hbm(w_qkv)] * 3)


def attn_weight_body(
    z_first, sc, own, other, gain, shift, d_qkv, gr_own, gr_rcv, ctx_full, ctx_oth, ctx_rcv, keep, send, z_keep, z_send, n_t
):
    core, x = sc[C], sc[X]
    own, other = own.at[0, :, 0], other.at[0, :, 0]
    for b in range(4):
        rows = slice(b * BLOCK, (b + 1) * BLOCK)
        n_t[:, rows] = norm_low(in_order(own, other, b, core), gain[0], shift[0]).T

    def columns(ref):
        rows = ref[...].reshape(ROWS, D)
        return jnp.where(core == 0, rows[:, 0:HALF], rows[:, HALF:D]).T

    def grad(j):
        return dot(n_t[...], d_qkv[:, j * HALF : (j + 1) * HALF]).astype(BF)

    first, second = grad(0), grad(2)
    mine, yours = jnp.where(x == 0, first, second), jnp.where(x == 0, second, first)
    for piece in range(8):
        py, pz = place(sc, piece)
        keep[py, pz] = mine[piece * PART : (piece + 1) * PART]
        send[py, pz] = yours[piece * PART : (piece + 1) * PART]

    a, b = ctx_oth[...].reshape(ROWS, HALF), ctx_rcv[...].reshape(ROWS, HALF)
    far = jnp.concatenate([jnp.where(core == 0, a, b), jnp.where(core == 0, b, a)], 1)
    g_out = (dot(columns(gr_own), ctx_full[...]) + dot(columns(gr_rcv), far)).astype(BF).T
    for j, rows in enumerate((grad(1), g_out)):
        for piece in range(8):
            py, pz = place(sc, piece)
            value = rows[piece * PART : (piece + 1) * PART]

            far = pz % 2 if z_first else py

            @pl.when(far == 0)
            def _():
                if z_first:
                    z_keep[pz // 2, py, j] = value
                else:
                    z_keep[pz, j] = value

            @pl.when(far == 1)
            def _():
                if z_first:
                    z_send[pz // 2, py, j] = value
                else:
                    z_send[pz, j] = value


def attention_weights(
    scalars, layer, own, own_spec, other, other_spec, gain, shift, d_qkv, gr_own, gr_rcv, ctx_full, ctx_oth, ctx_rcv, deps=()
):
    z_first = layer == 1
    packed, z_packed = (2, 4, PART, HALF), ((2, 2) if z_first else (4,)) + (2, PART, HALF)
    block = whole((2, BLOCK, D))
    return call(
        partial(attn_weight_body, z_first),
        (1,),
        [
            own_spec,
            other_spec,
            at_layer((1, 1, D), layer),
            at_layer((1, 1, D), layer),
            whole((LENGTH, 3 * HALF)),
            block,
            block,
            whole((ROWS, D)),
            whole((2, BLOCK, HALF)),
            whole((2, BLOCK, HALF)),
        ],
        [whole(packed), whole(packed), whole(z_packed), whole(z_packed)],
        [stored(packed, BF), shape(packed, BF), stored(z_packed, BF), shape(z_packed, BF)],
        [pltpu.VMEM((D, LENGTH), BF)],
        (2.5e9, 12e6),
        deps,
    )(scalars, own, other, gain, shift, d_qkv, gr_own, gr_rcv, ctx_full, ctx_oth, ctx_rcv)


def to_core(value):
    return lax.ppermute(value, "section", [(0, 1), (1, 0), (2, 3), (3, 2)])


def to_chip(value):
    return lax.ppermute(value, "section", [(0, 2), (2, 0), (1, 3), (3, 1)])


def to_dp(value, distance):
    return lax.ppermute(value, "dp", [(i, i ^ distance) for i in range(8)])


def total(*terms):
    out = terms[0].astype(F32)
    for term in terms[1:]:
        out = out + term.astype(F32)
    return out.astype(BF)


def combined(scalars, outputs, deps=(), pinned=()):
    terms, dims, dtypes = [], [], []
    for pieces in outputs:
        first = pieces[0][0]
        rest = first[0].shape[len(first) - 1 :]
        dims.append(((len(pieces),) if len(pieces) > 1 else ()) + rest)
        dtypes.append(first[0].dtype)
        terms += [term for piece in pieces for term in piece]

    def spec(term):
        array, *index = term
        rest = array.shape[len(index) :]
        return pl.BlockSpec((None,) * len(index) + rest, lambda i, sc: (*index, *(0 for _ in rest)))

    def body(sc, *refs):
        given = iter(refs[: len(terms)])
        for out, pieces in zip(refs[len(terms) :], outputs):
            for n, piece in enumerate(pieces):
                value = next(given)[...].astype(F32)
                for _ in piece[1:]:
                    value = value + next(given)[...].astype(F32)
                if len(pieces) > 1:
                    out[n] = value.astype(out.dtype)
                else:
                    out[...] = value.astype(out.dtype)

    return call(
        body,
        (1,),
        [spec(term) for term in terms],
        [whole(d) for d in dims],
        [shape(d, t) for d, t in zip(dims, dtypes)],
        [],
        (1e10, 1e7),
        deps,
    )(scalars, *[from_hbm(term[0]) if any(term[0] is a for a in pinned) else term[0] for term in terms])


def in_dp_order(both):
    return jnp.moveaxis(both, 0, 1).reshape((8,) + both.shape[2:])


def gathered(share):
    far, near = to_chip(share), to_core(share)
    return share, far, near, to_core(far)


def unpack_body(sc, *refs):
    (final_keep, final_got, input_keep, input_got, small), shares, outs = refs[:5], refs[5:25], refs[25:]
    final, inputs, up, down, qkv, out, a_gain, a_shift, b_out, f_gain, f_shift, b_down, b_up = outs
    x = sc[X]
    for ref, mine, got in ((final, final_keep, final_got), (inputs, input_keep, input_got)):
        ref[x, 0] = mine[...]
        ref[1 - x, 0] = got[...].astype(F32)
    for layer in range(2):
        ffn, qv, ko = shares[10 * layer : 10 * layer + 4], shares[10 * layer + 4 : 10 * layer + 8], shares[10 * layer + 8 : 10 * layer + 10]
        for n in range(4):
            x, core = sc[X] ^ (n % 2), sc[C] ^ (n // 2)
            for j in range(2):
                at = pl.multiple_of(x * 4 * HALF + core * 2 * HALF + j * HALF, PAIR)
                up[layer, :, pl.ds(at, HALF)] = ffn[n][j].astype(F32)
                rows = pl.ds(pl.multiple_of(core * 2 * PART + j * PART, 8), PART)
                down[layer, rows, pl.ds(pl.multiple_of(x * HALF, PAIR), HALF)] = ffn[n][2 + j].astype(F32)
            qkv[layer, :, pl.ds(pl.multiple_of(x * 2 * D + core * HALF, PAIR), HALF)] = qv[n][...].astype(F32)
        for n in range(2):
            side = pl.multiple_of((sc[C] ^ n) * HALF, PAIR)
            qkv[layer, :, pl.ds(pl.multiple_of(D + side, PAIR), HALF)] = ko[n][0].astype(F32)
            out[layer, :, pl.ds(side, HALF)] = ko[n][1].astype(F32)
    piece = 2 * sc[Z] + sc[Y]
    mine = jnp.zeros((32, PART), F32)
    for d in range(8):
        mine = jnp.where(piece == d, small[:, d * PART : (d + 1) * PART], mine)
    for layer in range(2):
        for j, (a_ref, f_ref) in enumerate(((a_gain, f_gain), (a_shift, f_shift), (b_out, b_down))):
            a_ref[layer : layer + 1] = mine[8 * layer + j : 8 * layer + j + 1]
            f_ref[layer : layer + 1] = mine[16 + 8 * layer + j : 16 + 8 * layer + j + 1]
        row = jnp.zeros((1, 4 * PART), F32)
        for d in range(8):
            at = 16 + 8 * layer + 4 + d // 2
            row = jnp.where(piece == d, small[at : at + 1, (d % 2) * HALF : (d % 2 + 1) * HALF], row)
        b_up[layer : layer + 1] = row


def unpacked(scalars, rows, small, shares):
    moved = ((2, 1, BLOCK, D),) * 2
    dims = ((2, PART, FF), (2, 4 * PART, D), (2, PART, 3 * D), (2, PART, D)) + ((2, PART),) * 6 + ((2, 4 * PART),)
    return call(
        unpack_body,
        (1,),
        [whole((BLOCK, D))] * 4 + [whole((32, D))] + [whole(share.shape) for share in shares],
        [whole(d) for d in moved + dims],
        [shape(d, F32) for d in moved + dims],
        [],
        (1e6, 11e6),
    )(scalars, *rows, small, *shares)


def on_device(
    tokens,
    episodes,
    attn_gain,
    attn_shift,
    qkv_weight,
    out_weight,
    out_bias,
    ffn_gain,
    ffn_shift,
    up_weight,
    up_bias,
    down_weight,
    down_bias,
    cotangent,
):
    replicas = lax.axis_size("dp")
    section = lax.axis_index("section")
    replica = lax.axis_index("dp")
    chip, core = section // 2, section % 2
    direct = replicas == 8
    y, z = (replica % 2, replica // 2) if direct else (0, 0)
    scalars = jnp.stack([jnp.asarray(v, jnp.int32) for v in (chip, core, y, z)])

    stream = tokens.reshape(2, 2, 2, BLOCK, D)
    cot = cotangent.reshape(2, 2, 2, BLOCK, D)
    eps = episodes.reshape(2, 1, LENGTH)
    ep_spec = pl.BlockSpec((1, 1, LENGTH), lambda i, sc: (sc[X], 0, 0))

    def input_spec(micro, side):
        return pl.BlockSpec((1, 2, 1, BLOCK, D), lambda i, sc: (micro(sc[X]), 0, side(sc[C]), 0, 0))

    same, flip = (lambda v: v), (lambda v: 1 - v)
    own_in, other_in, far_in = input_spec(same, same), input_spec(same, flip), input_spec(flip, same)
    local = pl.BlockSpec((1, 2, 1, BLOCK, D), lambda i, sc: (0, 0, 0, 0, 0))

    def rows5(value):
        return value.reshape(1, 2, 1, BLOCK, D)

    def vec(array):
        return array.reshape(2, 1, -1)

    a_gain, a_shift, b_out = vec(attn_gain), vec(attn_shift), vec(out_bias)
    f_gain, f_shift, b_up, b_down = vec(ffn_gain), vec(ffn_shift), vec(up_bias), vec(down_bias)

    kept = []
    own, own_spec, other, other_spec = stream, own_in, stream, other_in
    for layer in range(2):
        qkv, ctx, ctx_own, ctx_oth, lse = attention_forward(
            scalars, layer, own, own_spec, other, other_spec, eps, ep_spec, a_gain, a_shift, qkv_weight
        )
        ctx_rcv = to_core(ctx_oth)
        ctx_far = to_core(ctx_own)
        s2, ctx_full, act, slope, *result = ffn_forward(
            scalars,
            layer,
            layer == 1,
            ctx_own,
            ctx_rcv,
            own,
            own_spec,
            (out_weight, b_out, f_gain, f_shift, up_weight, b_up, down_weight, b_down),
            None if layer == 0 else kept[0][7],
        )
        s2_o = to_chip(s2)
        kept.append((own, own_spec, other, other_spec, qkv, ctx, ctx_oth, ctx_far, ctx_full, lse, s2, s2_o, act, slope))
        if layer == 0:
            s3 = result[0]
            own, own_spec, other, other_spec = rows5(s3), local, rows5(to_core(s3)), local
    final_keep, final_send = result

    def ffn_back(layer, grad, grad_spec, deps=()):
        kept_now = kept[layer]
        s2, slope = kept_now[10], kept_now[13]
        return ffn_backward(scalars, layer, grad, grad_spec, s2, slope, (f_gain, up_weight, down_weight), deps)

    def ffn_grads(layer, grad, grad_spec, grad_o, grad_o_spec, dh, deps=()):
        s2, s2_o, act, slope = kept[layer][10:]
        weights = (f_gain, f_shift, up_weight, b_up, down_weight)
        return ffn_weights(
            scalars, layer, grad, grad_spec, grad_o, grad_o_spec, s2, s2_o, act, dh, weights, deps
        )

    def attn_back(layer, ds, ds_rcv, deps=()):
        own, own_spec, other, other_spec, qkv, ctx, ctx_oth, ctx_far, ctx_full, lse = kept[layer][:10]
        return attention_backward(
            scalars, layer, ds, ds_rcv, qkv, ctx, lse, eps, ep_spec, out_weight, qkv_weight, deps
        )

    def attn_grads(layer, ds, ds_rcv, d_qkv, deps=()):
        own, own_spec, other, other_spec, qkv, ctx, ctx_oth, ctx_far, ctx_full, lse = kept[layer][:10]
        return attention_weights(
            scalars, layer, own, own_spec, other, other_spec, a_gain, a_shift, d_qkv, ds, ds_rcv, ctx_full, ctx_oth,
            ctx_far, deps,
        )

    def attn_norm(layer, ds, part_own, part_rcv, smalls=(), deps=()):
        own, own_spec = kept[layer][:2]
        return attention_norm_back(scalars, layer, ds, part_own, part_rcv, own, own_spec, a_gain, smalls, deps)

    if direct:
        pinned = []

        def summed(*outputs, deps=()):
            return combined(scalars, outputs, deps, pinned)

        def y_sum(keep, got):
            return [[(keep, 1), (got, 1)]]

        def z_sum(keep, got, y_got):
            return [[(keep, 0, k), (got, 0, k), (y_got, k)] for k in (1, 3)]

        def far_sum(keep, got, y_got, z_got):
            return [[(keep, 0, 2), (got, 0, 2), (y_got, 2), (z_got, 1)]]

        def share(keep, got, y_got, z_got, far_got):
            return [[(keep, 0, 0), (got, 0, 0), (y_got, 0), (z_got, 0), (far_got,)]]

        dh1, ds1, f_small1 = ffn_back(1, cot, own_in, [kept[0][11], kept[1][7]])
        ds1_rcv = to_core(ds1)
        fk1, send = ffn_grads(1, cot, own_in, cot, far_in, dh1)
        pinned.append(fk1)
        fg1 = to_core(send)
        d_qkv1, part1, part1_oth = attn_back(1, ds1, ds1_rcv, [fk1])
        part1_rcv = to_core(part1_oth)
        value, final_low = summed(y_sum(fk1, fg1), [[(final_send,)]], deps=[part1])
        fy1 = to_dp(value, 1)
        g0, a_small1 = attn_norm(1, ds1, part1, part1_rcv, deps=[value])
        g0_o = to_chip(g0)
        dh0, ds0, f_small0 = ffn_back(0, rows5(g0), local)
        ds0_rcv = to_core(ds0)
        fk0, send = ffn_grads(0, rows5(g0), local, rows5(g0_o), local, dh0)
        pinned.append(fk0)
        (fz1,) = summed(z_sum(fk1, fg1, fy1), deps=[fk0])
        fg0 = to_core(send)
        qk1, send, ok1, z_send = attn_grads(1, ds1, ds1_rcv, d_qkv1, [fz1])
        pinned += [qk1, ok1]
        qg1, og1 = to_chip(send), to_dp(z_send, 2)
        fy0, final_low = summed(y_sum(fk0, fg0), [[(final_low,)]], deps=[qk1])
        d_qkv0, part0, part0_oth = attn_back(0, ds0, ds0_rcv, [fy0])
        final_got = to_chip(final_low)
        fz1, fy0 = to_dp(fz1, 2), to_dp(fy0, 1)
        part0_rcv = to_core(part0_oth)
        far1, oy1, qy1 = summed(
            far_sum(fk1, fg1, fy1, fz1),
            [[(ok1, 0, 1), (og1, 0, 1)], [(ok1, 1, 1), (og1, 1, 1)]],
            y_sum(qk1, qg1),
            deps=[part0],
        )
        input_keep, input_send, small = attn_norm(
            0, ds0, part0, part0_rcv, (a_small1, f_small0, f_small1), [far1, final_got]
        )
        far1, oy1, qy1 = to_dp(far1, 4), to_dp(oy1, 1), to_dp(qy1, 1)
        small_got = to_core(small)
        input_got = to_chip(input_send)
        fz0, small = summed(z_sum(fk0, fg0, fy0), [[(small,), (small_got,)]], deps=[input_keep])
        qk0, send, ok0, y_send = attn_grads(0, ds0, ds0_rcv, d_qkv0, [fz0])
        fz0, small_got = to_dp(fz0, 2), to_dp(small, 1)
        pinned += [qk0, ok0]
        qg0, oy0 = to_chip(send), to_dp(y_send, 1)

        of1, qz1, far0, f1, small = summed(
            [[(ok1, 1, 0), (og1, 1, 0), (oy1, 1)]],
            z_sum(qk1, qg1, qy1),
            far_sum(fk0, fg0, fy0, fz0),
            share(fk1, fg1, fy1, fz1, far1),
            [[(small,), (small_got,)]],
            deps=[qk0],
        )
        of1, qz1, far0, small_got = to_dp(of1, 4), to_dp(qz1, 2), to_dp(far0, 4), to_dp(small, 2)
        f1_all = gathered(f1)

        qy0, oz_1, oz_2, oz_3, ox1, qf1, small = summed(
            y_sum(qk0, qg0),
            *[[[(ok0, k), (oy0, k)]] for k in (1, 2, 3)],
            [[(ok1, 0, 0), (og1, 0, 0), (oy1, 0), (of1,)]],
            far_sum(qk1, qg1, qy1, qz1),
            [[(small,), (small_got,)]],
            deps=[input_got],
        )
        qy0, ox1_got, qf1, small_got = to_dp(qy0, 1), to_chip(ox1), to_dp(qf1, 4), to_dp(small, 4)
        oz0 = [to_dp(value, 2 * k) for k, value in ((1, oz_1), (2, oz_2), (3, oz_3))]

        qz_1, qz_2, qz_3, ox0, f0, q1, o1, small = summed(
            *[[[(qk0, 0, k), (qg0, 0, k), (qy0, k)]] for k in (1, 2, 3)],
            [[(ok0, 0), (oy0, 0)] + [(got,) for got in oz0]],
            share(fk0, fg0, fy0, fz0, far0),
            share(qk1, qg1, qy1, qz1, qf1),
            [[(ox1,), (ox1_got,)]],
            [[(small,), (small_got,)]],
            deps=f1_all[1:],
        )
        ox0_got, small_got = to_chip(ox0), to_chip(small)
        qz0 = [to_dp(value, 2 * k) for k, value in ((1, qz_1), (2, qz_2), (3, qz_3))]
        f0_all, a1_all = gathered(f0), gathered(q1) + (o1, to_core(o1))

        q0, o0, small = summed(
            [[(qk0, 0, 0), (qg0, 0, 0), (qy0, 0)] + [(got,) for got in qz0]],
            [[(ox0,), (ox0_got,)]],
            [[(small,), (small_got,)]],
        )
        a0_all = gathered(q0) + (o0, to_core(o0))
        (final_out, input_out, ups, downs, qkvs, outs, *vectors) = unpacked(
            scalars,
            (final_keep, final_got, input_keep, input_got),
            small,
            f0_all + a0_all + f1_all + a1_all,
        )
        g_a_gain, g_a_shift, g_b_out, g_f_gain, g_f_shift, g_b_down, g_b_up = vectors
    else:
        final_got = to_chip(final_send)
        grads = [None, None]
        grad, grad_spec, grad_o, grad_o_spec = cot, own_in, cot, far_in
        for layer in (1, 0):
            dh, ds, f_small = ffn_back(layer, grad, grad_spec)
            ds_rcv = to_core(ds)
            f_keep, f_send = ffn_grads(layer, grad, grad_spec, grad_o, grad_o_spec, dh)
            d_qkv, part_own, part_oth = attn_back(layer, ds, ds_rcv)
            keep, send, z_keep, z_send = attn_grads(layer, ds, ds_rcv, d_qkv)
            if layer == 1:
                g0, a_small1 = attn_norm(1, ds, part_own, to_core(part_oth))
                grad, grad_spec, grad_o, grad_o_spec = rows5(g0), local, rows5(to_chip(g0)), local
                f_small1 = f_small
            else:
                input_keep, input_send, small = attn_norm(
                    0, ds, part_own, to_core(part_oth), (a_small1, f_small, f_small1)
                )
            ffn = in_dp_order(total(f_keep, to_core(f_send)))
            qv = in_dp_order(total(keep, to_chip(send)))
            ko = jnp.stack([z_keep, z_send], 1).reshape(8, 2, PART, HALF)
            ko = total(ko, to_chip(ko))
            ordered = []
            for mine, far, near, both in (gathered(ffn), gathered(qv)):
                here = jnp.stack([jnp.where(chip == 0, mine, far), jnp.where(chip == 0, far, mine)])
                there = jnp.stack([jnp.where(chip == 0, near, both), jnp.where(chip == 0, both, near)])
                pair = jnp.stack([jnp.where(core == 0, here, there), jnp.where(core == 0, there, here)], 1)
                ordered.append(pair.astype(F32))
            ko_other = to_core(ko)
            ko_all = jnp.stack([jnp.where(core == 0, ko, ko_other), jnp.where(core == 0, ko_other, ko)]).astype(F32)
            f_all, qv_all = ordered
            up = f_all[:, :, :, 0:2].transpose(2, 4, 0, 1, 3, 5).reshape(D, FF)
            down = f_all[:, :, :, 2:4].transpose(2, 1, 3, 4, 0, 5).reshape(FF, D)
            q, v = (qv_all[n].transpose(1, 2, 0, 3).reshape(D, D) for n in range(2))
            k, out = (ko_all[:, :, n].transpose(1, 2, 0, 3).reshape(D, D) for n in range(2))
            grads[layer] = [
                lax.psum_scatter(array, "dp", scatter_dimension=0, tiled=True)
                for array in (up, down, jnp.concatenate([q, k, v], 1), out)
            ]
        ups, downs, qkvs, outs = (jnp.stack(pair) for pair in zip(*grads))
        small = lax.psum(small, ("section", "dp")).reshape(4, 8, D)

        def mine_of(rows):
            width = rows.shape[-1] // replicas
            return lax.dynamic_slice_in_dim(rows, replica * width, width, 1)

        g_a_gain, g_a_shift, g_b_out = (mine_of(small[0:2, n]) for n in range(3))
        g_f_gain, g_f_shift, g_b_down = (mine_of(small[2:4, n]) for n in range(3))
        g_b_up = mine_of(small[2:4, 4:8].reshape(2, FF))

        def placed(keep, got):
            got = got.astype(F32)
            return jnp.stack([jnp.where(chip == 0, keep, got), jnp.where(chip == 0, got, keep)])[:, None]

        final_out, input_out = placed(final_keep, final_got), placed(input_keep, to_chip(input_send))

    return (
        final_out,
        input_out,
        g_a_gain,
        g_a_shift,
        qkvs,
        outs,
        g_b_out,
        g_f_gain,
        g_f_shift,
        ups,
        g_b_up,
        downs,
        g_b_down,
    )


def solution(mesh):
    split = P(None, "dp", None, None)
    placed = (split, P(None, "dp", None)) + (P(),) * 11 + (split,)
    rows = P(None, "dp", "section", None)
    vector, matrix = P(None, "dp"), P(None, "dp", None)
    return jax.shard_map(
        on_device,
        mesh=mesh,
        in_specs=placed,
        out_specs=(
            rows,
            rows,
            vector,
            vector,
            matrix,
            matrix,
            vector,
            vector,
            vector,
            matrix,
            vector,
            matrix,
            vector,
        ),
        check_vma=False,
    )
```

```python
from functools import partial

import jax
import jax.numpy as jnp
from jax import lax
from jax.experimental import pallas as pl
from jax.experimental.pallas import tpu as pltpu
from jax.sharding import PartitionSpec as P

BF = jnp.bfloat16
F32 = jnp.float32
EPS = 1e-05
MASKED = -1e30
D = 768
HALF = 384
PAIR = 128
HEAD_DIM = 64
FF = 3072
LENGTH = 1024
BLOCK = 256
ROWS = 512
PART = 96
GELU_A = 0.7978845608028654
GELU_B = GELU_A * 0.044715


def dot(a, b):
    return jnp.dot(a, b, preferred_element_type=F32)


def dot_nt(a, b):
    return lax.dot_general(a, b, (((1,), (1,)), ((), ())), preferred_element_type=F32)


def dot_tn(a, b):
    return lax.dot_general(a, b, (((0,), (0,)), ((), ())), preferred_element_type=F32)


def normalise(rows):
    center = rows - jnp.mean(rows, -1, keepdims=True)
    spread = lax.rsqrt(jnp.mean(center * center, -1, keepdims=True) + EPS)
    return center * spread, spread


def norm_low(rows, gain, shift):
    unit, _ = normalise(rows.astype(F32))
    return (unit * gain + shift).astype(BF)


def call(body, grid, in_specs, out_specs, out_shape, scratch, cost, deps=()):
    count = len(in_specs)

    def with_deps(sc, *refs):
        return body(sc, *refs[:count], *refs[count + len(deps) :])

    kernel = pl.pallas_call(
        with_deps,
        grid_spec=pltpu.PrefetchScalarGridSpec(
            num_scalar_prefetch=1,
            grid=grid,
            in_specs=list(in_specs) + [pl.BlockSpec(memory_space=pl.ANY)] * len(deps),
            out_specs=out_specs,
            scratch_shapes=scratch,
        ),
        out_shape=out_shape,
        compiler_params=pltpu.CompilerParams(vmem_limit_bytes=32 * 1024 * 1024),
        cost_estimate=pl.CostEstimate(flops=int(5 * cost[0]), bytes_accessed=int(5 * cost[1]), transcendentals=0),
    )
    return lambda *args: kernel(*args, *deps)


def shape(dims, dtype):
    return jax.ShapeDtypeStruct(dims, dtype)


def stored(dims, dtype):
    return pltpu.MemorySpace.HBM(dims, dtype)


def from_hbm(array):
    return pltpu.with_memory_space_constraint(array, pltpu.MemorySpace.HBM)


def whole(dims):
    count = len(dims)
    return pl.BlockSpec(dims, lambda i, sc: (0,) * count)


def at_layer(dims, layer):
    count = len(dims) - 1
    return pl.BlockSpec(dims, lambda i, sc: (layer,) + (0,) * count)


X, C, Y, Z = 0, 1, 2, 3


def in_order(own, other, block, core):
    return jnp.where(core == block % 2, own[block // 2], other[block // 2])


def weight_copies(layer, core, weights, sides, sems):
    return [
        pltpu.make_async_copy(
            weights.at[layer, :, pl.ds(pl.multiple_of(j * D + core * HALF, PAIR), HALF)],
            sides.at[:, j * HALF : (j + 1) * HALF],
            sems.at[j],
        )
        for j in range(3)
    ]


def episode_columns(ep_ref):
    row = jnp.broadcast_to(ep_ref[...].reshape(1, LENGTH).astype(F32), (PAIR, LENGTH))
    return row, row.T


def first_key(i):
    return max(0, i - 2) * BLOCK


def attn_fwd_body(sc, own, other, ep, gain, shift, wq, wk, wv, qkv, ctx, ctx_own, ctx_oth, lse, bias, vext, lse_cols):
    core = sc[C]
    own, other = own.at[0, :, 0], other.at[0, :, 0]
    for b in range(4):
        rows = slice(b * BLOCK, (b + 1) * BLOCK)
        normed = norm_low(in_order(own, other, b, core), gain[0], shift[0])
        qkv[rows, 0:HALF] = (dot(normed, wq[0]).astype(BF) * 0.125).astype(BF)
        qkv[rows, HALF : 2 * HALF] = dot(normed, wk[0]).astype(BF)
        qkv[rows, 2 * HALF : 3 * HALF] = dot(normed, wv[0]).astype(BF)
    ep_row, ep_col = episode_columns(ep)
    for i in range(4):
        lo, hi = first_key(i), (i + 1) * BLOCK
        key_at = lo + lax.broadcasted_iota(jnp.int32, (BLOCK, hi - lo), 1)
        row_at = i * BLOCK + lax.broadcasted_iota(jnp.int32, (BLOCK, hi - lo), 0)
        same = ep_col[i * BLOCK : hi, 0:1] == ep_row[0:1, lo:hi]
        bias[i, :, 0 : hi - lo] = jnp.where((key_at <= row_at) & same, 0.0, MASKED)
    vext[:, PAIR:] = jnp.ones((LENGTH, PAIR), BF)
    lane = lax.broadcasted_iota(jnp.int32, (BLOCK, PAIR), 1)

    @pl.loop(0, 3)
    def _(p):
        at = pl.multiple_of(p * PAIR, PAIR)
        vext[:, 0:PAIR] = qkv[:, pl.ds(2 * HALF + at, PAIR)]
        for i in range(4):
            lo, hi = first_key(i), (i + 1) * BLOCK
            rows = slice(i * BLOCK, hi)
            q = qkv[rows, pl.ds(at, PAIR)]
            k = qkv[lo:hi, pl.ds(HALF + at, PAIR)]
            outs = []
            for h in range(2):
                mine = (lane >= HEAD_DIM) if h else (lane < HEAD_DIM)
                s = dot_nt(jnp.where(mine, q, jnp.zeros_like(q)), k) + bias[i, :, 0 : hi - lo]
                top = jnp.max(s, -1, keepdims=True)
                prob = jnp.exp(s - top).astype(BF)
                o = dot(prob, vext[lo:hi, :])
                total = o[:, PAIR : PAIR + 1]
                outs.append(o[:, 0:PAIR] / total)
                lse_cols[rows, :] = jnp.where(lane == 2 * p + h, top + jnp.log(total), lse_cols[rows, :])
            ctx[rows, pl.ds(at, PAIR)] = jnp.where(lane < HEAD_DIM, outs[0], outs[1]).astype(BF)

    lse[...] = lse_cols[...].T[0:8]
    for b in range(4):
        piece = ctx[b * BLOCK : (b + 1) * BLOCK]

        @pl.when(core == b % 2)
        def _():
            ctx_own[b // 2] = piece

        @pl.when(core != b % 2)
        def _():
            ctx_oth[b // 2] = piece


def attention_forward(scalars, layer, own, own_spec, other, other_spec, episodes, ep_spec, gain, shift, w_qkv):
    columns = [pl.BlockSpec((1, D, HALF), partial(lambda j, i, sc: (layer, 0, 2 * j + sc[C]), j)) for j in range(3)]
    return call(
        attn_fwd_body,
        (1,),
        [own_spec, other_spec, ep_spec, at_layer((1, 1, D), layer), at_layer((1, 1, D), layer)] + columns,
        [
            whole((LENGTH, 3 * HALF)),
            whole((LENGTH, HALF)),
            whole((2, BLOCK, HALF)),
            whole((2, BLOCK, HALF)),
            whole((8, LENGTH)),
        ],
        [
            stored((LENGTH, 3 * HALF), BF),
            stored((LENGTH, HALF), BF),
            shape((2, BLOCK, HALF), BF),
            shape((2, BLOCK, HALF), BF),
            shape((8, LENGTH), F32),
        ],
        [
            pltpu.VMEM((4, BLOCK, 3 * BLOCK), F32),
            pltpu.VMEM((LENGTH, 2 * PAIR), BF),
            pltpu.VMEM((LENGTH, PAIR), F32),
        ],
        (1.8e9 + 2.4e9, 8e6),
    )(scalars, own, other, episodes, gain, shift, *[from_hbm(w_qkv)] * 3)


def gelu_parts(u):
    cubic = GELU_B * (u * u)
    t = jnp.tanh(u * (GELU_A + cubic))
    half = 0.5 * t + 0.5
    active = u * half
    slope = half + (active * (1.0 - half)) * (6.0 * cubic + 2.0 * GELU_A)
    return active, slope


FT = 1024


def project_body(sc, ctx_own, ctx_rcv, own, w_out, b_out, s2, ctx_full):
    core = sc[C]
    a, b = ctx_own[...].reshape(ROWS, HALF), ctx_rcv[...].reshape(ROWS, HALF)
    both = jnp.concatenate([jnp.where(core == 0, a, b), jnp.where(core == 0, b, a)], 1)
    ctx_full[...] = both
    stream = own[0, :, 0].reshape(ROWS, D).astype(F32) + dot(both, w_out[0]) + b_out[0]
    s2[...] = stream.astype(BF)


def ffn_fwd_body(last, sc, *refs):
    if last:
        s2, gain, shift, w_up, b_up, w_down, b_down, act, slope, keep, send, normed, acc = refs
    else:
        gain, shift, w_up, b_up, w_down, b_down, s2, ctx_full, act, slope, s3, normed, acc = refs[5:]
    t = pl.program_id(0)

    @pl.when(t == 0)
    def _():
        if not last:
            project_body(sc, *refs[:5], s2, ctx_full)
        low = s2[...]
        normed[...] = norm_low(low, gain[0], shift[0])
        acc[...] = low.astype(F32) + b_down[0]

    u = dot(normed[...], w_up[0]) + b_up[0]
    a, d = gelu_parts(u)
    a = a.astype(BF)
    act[...] = a
    slope[...] = d.astype(BF)
    acc[...] += dot(a, w_down[0])

    @pl.when(t == FF // FT - 1)
    def _():
        if last:
            x = sc[X]
            keep[...] = acc[pl.ds(pl.multiple_of(x * BLOCK, BLOCK), BLOCK)]
            send[...] = acc[pl.ds(pl.multiple_of((1 - x) * BLOCK, BLOCK), BLOCK)].astype(BF)
        else:
            s3[...] = acc[...].reshape(2, BLOCK, D).astype(BF)


def ffn_forward(scalars, layer, ctx_own, ctx_rcv, own, own_spec, weights, deps):
    specs, ffn_weight_specs, hidden = projection_specs(layer, own_spec), ffn_specs(layer), hidden_specs()
    w_out, b_out, gain, shift, w_up, b_up, w_down, b_down = weights
    return call(
        partial(ffn_fwd_body, False),
        (FF // FT,),
        specs + ffn_weight_specs,
        [whole((ROWS, D)), whole((ROWS, D))] + hidden + [whole((2, BLOCK, D))],
        [shape((ROWS, D), BF)] * 2 + [stored((ROWS, FF), BF)] * 2 + [shape((2, BLOCK, D), BF)],
        [pltpu.VMEM((ROWS, D), BF), pltpu.VMEM((ROWS, D), F32)],
        (5.4e9, 20e6),
        deps,
    )(scalars, ctx_own, ctx_rcv, own, from_hbm(w_out), b_out, gain, shift, from_hbm(w_up), b_up, from_hbm(w_down), b_down)


def projected(scalars, layer, ctx_own, ctx_rcv, own, own_spec, w_out, b_out, deps):
    return call(
        project_body,
        (1,),
        projection_specs(layer, own_spec),
        [whole((ROWS, D)), whole((ROWS, D))],
        [shape((ROWS, D), BF)] * 2,
        [],
        (6e8, 5e6),
        deps,
    )(scalars, ctx_own, ctx_rcv, own, from_hbm(w_out), b_out)


def last_ffn_forward(scalars, layer, s2, weights):
    gain, shift, w_up, b_up, w_down, b_down = weights
    return call(
        partial(ffn_fwd_body, True),
        (FF // FT,),
        [whole((ROWS, D))] + ffn_specs(layer),
        hidden_specs() + [whole((BLOCK, D)), whole((BLOCK, D))],
        [shape((ROWS, FF), BF)] * 2 + [shape((BLOCK, D), F32), shape((BLOCK, D), BF)],
        [pltpu.VMEM((ROWS, D), BF), pltpu.VMEM((ROWS, D), F32)],
        (4.8e9, 18e6),
    )(scalars, s2, gain, shift, from_hbm(w_up), b_up, from_hbm(w_down), b_down)


def projection_specs(layer, own_spec):
    part = whole((2, BLOCK, HALF))
    return [part, part, own_spec, at_layer((1, D, D), layer), at_layer((1, 1, D), layer)]


def ffn_specs(layer):
    vector = at_layer((1, 1, D), layer)
    return [
        vector,
        vector,
        pl.BlockSpec((1, D, FT), lambda i, sc: (layer, 0, i)),
        pl.BlockSpec((1, 1, FT), lambda i, sc: (layer, 0, i)),
        pl.BlockSpec((1, FT, D), lambda i, sc: (layer, i, 0)),
        vector,
    ]


def hidden_specs():
    return [pl.BlockSpec((ROWS, FT), lambda i, sc: (0, i))] * 2


def norm_back(d_normed, rows, gain):
    unit, spread = normalise(rows)
    d_unit = d_normed * gain
    first = jnp.mean(d_unit, -1, keepdims=True)
    second = jnp.mean(d_unit * unit, -1, keepdims=True)
    d_rows = spread * (d_unit - first - unit * second)
    return d_rows, jnp.sum(d_normed * unit, 0, keepdims=True), jnp.sum(d_normed, 0, keepdims=True)


def small_rows(*vectors):
    return jnp.concatenate(vectors + (jnp.zeros((8 - len(vectors), D), F32),))


def attn_norm_body(last, sc, grad, part, part_rcv, own, gain, *rest):
    before, outs = rest[:3] if last else (), rest[3:] if last else rest
    grad_rows = grad[...].reshape(ROWS, D).astype(F32)
    d_normed = part[...].reshape(ROWS, D) + part_rcv[...].reshape(ROWS, D).astype(F32)
    d_rows, g_gain, g_shift = norm_back(d_normed, own[0, :, 0].reshape(ROWS, D).astype(F32), gain[0])
    total = grad_rows + d_rows
    small = outs[-1]
    small[0:8] = small_rows(g_gain, g_shift, jnp.sum(grad_rows, 0, keepdims=True))
    for j, ref in enumerate(before):
        small[8 * (j + 1) : 8 * (j + 2)] = ref[...]
    if last:
        keep, send = outs[0:2]
        keep[...] = jnp.where(sc[X] == 0, total[0:BLOCK], total[BLOCK:ROWS])
        send[...] = jnp.where(sc[X] == 0, total[BLOCK:ROWS], total[0:BLOCK]).astype(BF)
    else:
        outs[0][...] = total.astype(BF).reshape(2, BLOCK, D)


def attention_norm_back(scalars, layer, grad, part, part_rcv, own, own_spec, gain, smalls=(), deps=()):
    block = whole((2, BLOCK, D))
    last = bool(smalls)
    if last:
        out_specs = [whole((BLOCK, D)), whole((BLOCK, D))]
        out_shape = [shape((BLOCK, D), F32), shape((BLOCK, D), BF)]
    else:
        out_specs, out_shape = [block], [shape((2, BLOCK, D), BF)]
    rows = 8 * (1 + len(smalls))
    return call(
        partial(attn_norm_body, last),
        (1,),
        [block, block, block, own_spec, at_layer((1, 1, D), layer)] + [whole((8, D))] * len(smalls),
        out_specs + [whole((rows, D))],
        out_shape + [shape((rows, D), F32)],
        [],
        (2e8, 5e6),
        deps,
    )(scalars, grad, part, part_rcv, own, gain, *smalls)


BT = 768
AT = 1536


def ffn_back_body(sc, grad, s2, gain, w_up, w_down, slope, dh, ds, small, acc):
    t = pl.program_id(0)
    low = grad[0, :, 0].reshape(ROWS, D)
    d_act = dot_nt(low, w_down[0])
    d_hidden = d_act * slope[...].astype(F32)
    d_low = d_hidden.astype(BF)
    dh[...] = d_low
    sums = jnp.sum(d_low.astype(F32), 0, keepdims=True)
    for j in range(2):
        small[pl.ds(4 + 2 * t + j, 1)] = sums[:, j * D : (j + 1) * D]
    part = dot_nt(d_low, w_up[0])

    @pl.when(t == 0)
    def _():
        acc[...] = part

    @pl.when(t > 0)
    def _():
        acc[...] += part

    @pl.when(t == FF // AT - 1)
    def _():
        rows = low.astype(F32)
        d_rows, g_gain, g_shift = norm_back(acc[...], s2[...].astype(F32), gain[0])
        ds[...] = (rows + d_rows).astype(BF).reshape(2, BLOCK, D)
        small[0:4] = small_rows(g_gain, g_shift, jnp.sum(rows, 0, keepdims=True))[0:4]


def ffn_backward(scalars, layer, grad, grad_spec, s2, slope, weights, deps=()):
    gain, w_up, w_down = weights
    return call(
        ffn_back_body,
        (FF // AT,),
        [
            grad_spec,
            whole((ROWS, D)),
            at_layer((1, 1, D), layer),
            pl.BlockSpec((1, D, AT), lambda i, sc: (layer, 0, i)),
            pl.BlockSpec((1, AT, D), lambda i, sc: (layer, i, 0)),
            pl.BlockSpec((ROWS, AT), lambda i, sc: (0, i)),
        ],
        [
            pl.BlockSpec((ROWS, AT), lambda i, sc: (0, i)),
            whole((2, BLOCK, D)),
            whole((8, D)),
        ],
        [shape((ROWS, FF), BF), shape((2, BLOCK, D), BF), shape((8, D), F32)],
        [pltpu.VMEM((ROWS, D), F32)],
        (4.9e9, 18e6),
        deps,
    )(scalars, grad, s2, gain, from_hbm(w_up), from_hbm(w_down), (slope if layer == 1 else from_hbm(slope)))


def place(sc, piece):
    return (piece % 2) ^ sc[Y], (piece // 2) ^ sc[Z]


def ffn_weight_body(
    sc, grad, grad_o, s2, s2_o, gain, shift, act, dh, w_up, b_up, w_down, keep, send, n_t, n_o, n_t_o, g_t, g_t_o
):
    t = pl.program_id(0)
    core = sc[C]
    low, low_o = grad[0, :, 0].reshape(ROWS, D), grad_o[0, :, 0].reshape(ROWS, D)

    @pl.when(t == 0)
    def _():
        n_t[...] = norm_low(s2[...], gain[0], shift[0]).T
        other = norm_low(s2_o[...], gain[0], shift[0])
        n_o[...] = other
        n_t_o[...] = other.T
        x = sc[X]
        g_t[...] = jnp.where(x == 0, low[:, 0:HALF], low[:, HALF:D]).T
        g_t_o[...] = jnp.where(x == 0, low_o[:, 0:HALF], low_o[:, HALF:D]).T

    u = dot(n_o[...], w_up[0]) + b_up[0]
    active_o, slope_o = gelu_parts(u)

    @pl.when(t < 2)
    def _():
        dh_o = (dot_nt(low_o, w_down[0]) * slope_o).astype(BF)
        g_up = (dot(n_t[...], dh[...]) + dot(n_t_o[...], dh_o)).astype(BF)
        for ref, when in ((send, 0), (keep, 1)):

            @pl.when(t == when)
            def _():
                for piece in range(8):
                    py, pz = place(sc, piece)
                    for j in range(2):
                        ref[py, pz, j] = g_up[piece * PART : (piece + 1) * PART, j * HALF : (j + 1) * HALF]

    g_down = (dot(g_t[...], act[...]) + dot(g_t_o[...], active_o.astype(BF))).astype(BF).T
    tile = ffn_tile(t, sc)
    for half in range(2):
        py, pz = place(sc, 2 * tile + half)
        for j in range(2):
            first = g_down[half * HALF + j * PART : half * HALF + (j + 1) * PART]
            second = g_down[half * HALF + (j + 2) * PART : half * HALF + (j + 3) * PART]
            keep[py, pz, 2 + j] = jnp.where(core == 0, first, second)
            send[py, pz, 2 + j] = jnp.where(core == 0, second, first)


def ffn_tile(step, sc):
    mine = 2 * sc[X]
    rest = 2 - mine
    return jnp.where(step == 0, mine + 1 - sc[C], jnp.where(step == 1, mine + sc[C], rest + step - 2))


def ffn_weights(scalars, layer, grad, grad_spec, grad_o, grad_o_spec, s2, s2_o, act, dh, weights, deps=()):
    gain, shift, w_up, b_up, w_down = weights
    packed = (2, 4, 4, PART, HALF)
    return call(
        ffn_weight_body,
        (FF // BT,),
        [
            grad_spec,
            grad_o_spec,
            whole((ROWS, D)),
            whole((ROWS, D)),
            at_layer((1, 1, D), layer),
            at_layer((1, 1, D), layer),
            pl.BlockSpec((ROWS, BT), lambda i, sc: (0, ffn_tile(i, sc))),
            pl.BlockSpec((ROWS, BT), lambda i, sc: (0, ffn_tile(jnp.minimum(i, 1), sc))),
            pl.BlockSpec((1, D, BT), lambda i, sc: (layer, 0, ffn_tile(i, sc))),
            pl.BlockSpec((1, 1, BT), lambda i, sc: (layer, 0, ffn_tile(i, sc))),
            pl.BlockSpec((1, BT, D), lambda i, sc: (layer, ffn_tile(jnp.minimum(i, 1), sc), 0)),
        ],
        [whole(packed), whole(packed)],
        [stored(packed, BF), shape(packed, BF)],
        [
            pltpu.VMEM((D, ROWS), BF),
            pltpu.VMEM((ROWS, D), BF),
            pltpu.VMEM((D, ROWS), BF),
            pltpu.VMEM((HALF, ROWS), BF),
            pltpu.VMEM((HALF, ROWS), BF),
        ],
        (8.6e9, 22e6),
        deps,
    )(scalars, grad, grad_o, s2, s2_o, gain, shift, (act if layer == 1 else from_hbm(act)), dh, from_hbm(w_up), b_up, from_hbm(w_down))


def attn_back_body(
    layer, sc, gr_own, gr_rcv, qkv, ctx, lse, ep, w_out, weights, d_qkv, part_own, part_oth, bias, d_ctx, delta, d_k, d_v,
    sides, sems
):
    core = sc[C]
    copies = weight_copies(layer, core, weights, sides, sems)
    for copy in copies:
        copy.start()
    for b in range(4):
        rows = slice(b * BLOCK, (b + 1) * BLOCK)
        d_ctx[rows] = dot_nt(in_order(gr_own, gr_rcv, b, core), w_out[0]).astype(BF)
    product = d_ctx[...].astype(F32) * ctx[...].astype(F32)
    high = product.astype(BF)
    rest = (product - high.astype(F32)).astype(BF)
    picks = (
        lax.broadcasted_iota(jnp.int32, (8, HALF), 0) == lax.broadcasted_iota(jnp.int32, (8, HALF), 1) // HEAD_DIM
    ).astype(BF)
    delta[...] = dot_nt(picks, high) + dot_nt(picks, rest)
    ep_row, ep_col = episode_columns(ep)
    for i in range(4):
        lo, hi = first_key(i), (i + 1) * BLOCK
        key_at = lo + lax.broadcasted_iota(jnp.int32, (hi - lo, BLOCK), 0)
        row_at = i * BLOCK + lax.broadcasted_iota(jnp.int32, (hi - lo, BLOCK), 1)
        same = ep_col[lo:hi, 0:1] == ep_row[0:1, i * BLOCK : hi]
        bias[i, 0 : hi - lo, :] = jnp.where((key_at <= row_at) & same, 0.0, MASKED)

    @pl.loop(0, 3)
    def _(p):
        at = pl.multiple_of(p * PAIR, PAIR)
        d_k[...] = jnp.zeros_like(d_k)
        d_v[...] = jnp.zeros_like(d_v)
        for i in range(4):
            lo, hi = first_key(i), (i + 1) * BLOCK
            rows = slice(i * BLOCK, hi)
            q = qkv[rows, pl.ds(at, PAIR)]
            k = qkv[lo:hi, pl.ds(HALF + at, PAIR)]
            v = qkv[lo:hi, pl.ds(2 * HALF + at, PAIR)]
            dc = d_ctx[rows, pl.ds(at, PAIR)]
            d_q = jnp.zeros((BLOCK, PAIR), F32)
            for h in range(2):

                def only(array):
                    lane = lax.broadcasted_iota(jnp.int32, array.shape, 1)
                    mine = (lane >= HEAD_DIM) if h else (lane < HEAD_DIM)
                    return jnp.where(mine, array, jnp.zeros_like(array))

                q_h, dc_h = only(q), only(dc)
                s = dot_nt(k, q_h) + bias[i, 0 : hi - lo, :]
                prob = jnp.exp(s - lse[pl.ds(2 * p + h, 1), rows])
                d_p = dot_nt(v, dc_h)
                d_s = (prob * (d_p - delta[pl.ds(2 * p + h, 1), rows])).astype(BF)
                d_v[lo:hi] += dot(prob.astype(BF), dc_h)
                d_k[lo:hi] += dot(d_s, q_h)
                d_q += dot_tn(d_s, only(k))
            d_qkv[rows, pl.ds(at, PAIR)] = (d_q * 0.125).astype(BF)
        d_qkv[:, pl.ds(HALF + at, PAIR)] = d_k[...].astype(BF)
        d_qkv[:, pl.ds(2 * HALF + at, PAIR)] = d_v[...].astype(BF)

    for copy in copies:
        copy.wait()
    for b in range(4):
        rows = slice(b * BLOCK, (b + 1) * BLOCK)
        part = dot_nt(d_qkv[rows], sides[...])

        @pl.when(core == b % 2)
        def _():
            part_own[b // 2] = part

        @pl.when(core != b % 2)
        def _():
            part_oth[b // 2] = part.astype(BF)


def attention_backward(scalars, layer, gr_own, gr_rcv, qkv, ctx, lse, episodes, ep_spec, w_out, w_qkv, deps=()):
    block = whole((2, BLOCK, D))
    return call(
        partial(attn_back_body, layer),
        (1,),
        [
            block,
            block,
            whole((LENGTH, 3 * HALF)),
            whole((LENGTH, HALF)),
            whole((8, LENGTH)),
            ep_spec,
            pl.BlockSpec((1, HALF, D), lambda i, sc: (layer, sc[C], 0)),
            pl.BlockSpec(memory_space=pl.ANY),
        ],
        [whole((LENGTH, 3 * HALF)), block, block],
        [shape((LENGTH, 3 * HALF), BF), shape((2, BLOCK, D), F32), shape((2, BLOCK, D), BF)],
        [
            pltpu.VMEM((4, 3 * BLOCK, BLOCK), F32),
            pltpu.VMEM((LENGTH, HALF), BF),
            pltpu.VMEM((8, LENGTH), F32),
            pltpu.VMEM((LENGTH, PAIR), F32),
            pltpu.VMEM((LENGTH, PAIR), F32),
            pltpu.VMEM((D, 3 * HALF), BF),
            pltpu.SemaphoreType.DMA((3,)),
        ],
        (2.5e9 + 6e9, 12e6),
        deps,
    )(scalars, gr_own, gr_rcv, from_hbm(qkv), from_hbm(ctx), lse, episodes, from_hbm(w_out), from_hbm(w_qkv))


def attn_weight_body(
    z_first, sc, own, other, gain, shift, d_qkv, gr_own, gr_rcv, ctx_full, ctx_oth, ctx_rcv, keep, send, z_keep, z_send, n_t
):
    core, x = sc[C], sc[X]
    own, other = own.at[0, :, 0], other.at[0, :, 0]
    for b in range(4):
        rows = slice(b * BLOCK, (b + 1) * BLOCK)
        n_t[:, rows] = norm_low(in_order(own, other, b, core), gain[0], shift[0]).T

    def columns(ref):
        rows = ref[...].reshape(ROWS, D)
        return jnp.where(core == 0, rows[:, 0:HALF], rows[:, HALF:D]).T

    def grad(j):
        return dot(n_t[...], d_qkv[:, j * HALF : (j + 1) * HALF]).astype(BF)

    first, second = grad(0), grad(2)
    mine, yours = jnp.where(x == 0, first, second), jnp.where(x == 0, second, first)
    for piece in range(8):
        py, pz = place(sc, piece)
        keep[py, pz] = mine[piece * PART : (piece + 1) * PART]
        send[py, pz] = yours[piece * PART : (piece + 1) * PART]

    a, b = ctx_oth[...].reshape(ROWS, HALF), ctx_rcv[...].reshape(ROWS, HALF)
    far = jnp.concatenate([jnp.where(core == 0, a, b), jnp.where(core == 0, b, a)], 1)
    g_out = (dot(columns(gr_own), ctx_full[...]) + dot(columns(gr_rcv), far)).astype(BF).T
    for j, rows in enumerate((grad(1), g_out)):
        for piece in range(8):
            py, pz = place(sc, piece)
            value = rows[piece * PART : (piece + 1) * PART]

            far = pz % 2 if z_first else py

            @pl.when(far == 0)
            def _():
                if z_first:
                    z_keep[pz // 2, py, j] = value
                else:
                    z_keep[pz, j] = value

            @pl.when(far == 1)
            def _():
                if z_first:
                    z_send[pz // 2, py, j] = value
                else:
                    z_send[pz, j] = value


def attention_weights(
    scalars, layer, own, own_spec, other, other_spec, gain, shift, d_qkv, gr_own, gr_rcv, ctx_full, ctx_oth, ctx_rcv, deps=()
):
    z_first = layer == 1
    packed, z_packed = (2, 4, PART, HALF), ((2, 2) if z_first else (4,)) + (2, PART, HALF)
    block = whole((2, BLOCK, D))
    return call(
        partial(attn_weight_body, z_first),
        (1,),
        [
            own_spec,
            other_spec,
            at_layer((1, 1, D), layer),
            at_layer((1, 1, D), layer),
            whole((LENGTH, 3 * HALF)),
            block,
            block,
            whole((ROWS, D)),
            whole((2, BLOCK, HALF)),
            whole((2, BLOCK, HALF)),
        ],
        [whole(packed), whole(packed), whole(z_packed), whole(z_packed)],
        [stored(packed, BF), shape(packed, BF), stored(z_packed, BF), shape(z_packed, BF)],
        [pltpu.VMEM((D, LENGTH), BF)],
        (2.5e9, 12e6),
        deps,
    )(scalars, own, other, gain, shift, d_qkv, gr_own, gr_rcv, ctx_full, ctx_oth, ctx_rcv)


def to_core(value):
    return lax.ppermute(value, "section", [(0, 1), (1, 0), (2, 3), (3, 2)])


def to_chip(value):
    return lax.ppermute(value, "section", [(0, 2), (2, 0), (1, 3), (3, 1)])


def to_dp(value, distance):
    return lax.ppermute(value, "dp", [(i, i ^ distance) for i in range(8)])


def total(*terms):
    out = terms[0].astype(F32)
    for term in terms[1:]:
        out = out + term.astype(F32)
    return out.astype(BF)


class Flat(list):
    pass


def combined(scalars, outputs, deps=(), pinned=()):
    terms, dims, dtypes = [], [], []

    def block_of(term):
        array, *index = term
        if index and isinstance(index[0], slice):
            count = index[0].stop - index[0].start
            return (count,) + array.shape[1:], (index[0].start // count,) + (0,) * (array.ndim - 1)
        rest = array.shape[len(index) :]
        return (None,) * len(index) + rest, tuple(index) + (0,) * len(rest)

    def dims_of(term):
        return tuple(d for d in block_of(term)[0] if d is not None)

    def rows_of(piece):
        found = dims_of(piece[0])
        return found[0] if len(found) == 3 else 1

    for pieces in outputs:
        rest = dims_of(pieces[0][0])
        if isinstance(pieces, Flat):
            dims.append((sum(rows_of(piece) for piece in pieces),) + rest[-2:])
        else:
            dims.append(((len(pieces),) if len(pieces) > 1 else ()) + rest)
        dtypes.append(pieces[0][0][0].dtype)
        terms += [term for piece in pieces for term in piece]

    def spec(term):
        block, index = block_of(term)
        return pl.BlockSpec(block, lambda i, sc: index)

    def body(sc, *refs):
        given = iter(refs[: len(terms)])
        for out, pieces in zip(refs[len(terms) :], outputs):
            at = 0
            for n, piece in enumerate(pieces):
                value = next(given)[...].astype(F32)
                for _ in piece[1:]:
                    value = value + next(given)[...].astype(F32)
                value = value.astype(out.dtype)
                if isinstance(pieces, Flat):
                    rows = rows_of(piece)
                    if len(value.shape) == 3:
                        out[at : at + rows] = value
                    else:
                        out[at] = value
                    at += rows
                elif len(pieces) > 1:
                    out[n] = value
                else:
                    out[...] = value

    return call(
        body,
        (1,),
        [spec(term) for term in terms],
        [whole(d) for d in dims],
        [shape(d, t) for d, t in zip(dims, dtypes)],
        [],
        (1e10, 1e7),
        deps,
    )(scalars, *[from_hbm(term[0]) if any(term[0] is a for a in pinned) else term[0] for term in terms])


def in_dp_order(both):
    return jnp.moveaxis(both, 0, 1).reshape((8,) + both.shape[2:])


def gathered(share):
    far, near = to_chip(share), to_core(share)
    return share, far, near, to_core(far)


def unpack_body(shares, sc, *refs):
    (final_keep, final_got, input_keep, input_got, small), refs = refs[:5], refs[5:]
    final, inputs, up, down, qkv, out, a_gain, a_shift, b_out, f_gain, f_shift, b_down, b_up = refs[-13:]
    x = sc[X]
    for ref, mine, got in ((final, final_keep, final_got), (inputs, input_keep, input_got)):
        ref[x, 0] = mine[...]
        ref[1 - x, 0] = got[...].astype(F32)
    for layer in range(2):
        ffn, qv, ko = shares[layer]
        for n in range(4):
            x, core = sc[X] ^ (n % 2), sc[C] ^ (n // 2)
            for j in range(2):
                at = pl.multiple_of(x * 4 * HALF + core * 2 * HALF + j * HALF, PAIR)
                up[layer, :, pl.ds(at, HALF)] = refs[ffn[n]][j].astype(F32)
                rows = pl.ds(pl.multiple_of(core * 2 * PART + j * PART, 8), PART)
                down[layer, rows, pl.ds(pl.multiple_of(x * HALF, PAIR), HALF)] = refs[ffn[n]][2 + j].astype(F32)
            index, at = qv[n]
            value = refs[index][...] if at is None else refs[index][at]
            qkv[layer, :, pl.ds(pl.multiple_of(x * 2 * D + core * HALF, PAIR), HALF)] = value.astype(F32)
        for n in range(2):
            side = pl.multiple_of((sc[C] ^ n) * HALF, PAIR)
            qkv[layer, :, pl.ds(pl.multiple_of(D + side, PAIR), HALF)] = refs[ko[n]][0].astype(F32)
            out[layer, :, pl.ds(side, HALF)] = refs[ko[n]][1].astype(F32)
    piece = 2 * sc[Z] + sc[Y]
    mine = jnp.zeros((32, PART), F32)
    for d in range(8):
        mine = jnp.where(piece == d, small[:, d * PART : (d + 1) * PART], mine)
    for layer in range(2):
        for j, (a_ref, f_ref) in enumerate(((a_gain, f_gain), (a_shift, f_shift), (b_out, b_down))):
            a_ref[layer : layer + 1] = mine[8 * layer + j : 8 * layer + j + 1]
            f_ref[layer : layer + 1] = mine[16 + 8 * layer + j : 16 + 8 * layer + j + 1]
        row = jnp.zeros((1, 4 * PART), F32)
        for d in range(8):
            at = 16 + 8 * layer + 4 + d // 2
            row = jnp.where(piece == d, small[at : at + 1, (d % 2) * HALF : (d % 2 + 1) * HALF], row)
        b_up[layer : layer + 1] = row


def unpacked(scalars, rows, small, arrays, shares):
    moved = ((2, 1, BLOCK, D),) * 2
    dims = ((2, PART, FF), (2, 4 * PART, D), (2, PART, 3 * D), (2, PART, D)) + ((2, PART),) * 6 + ((2, 4 * PART),)
    return call(
        partial(unpack_body, shares),
        (1,),
        [whole((BLOCK, D))] * 4 + [whole((32, D))] + [whole(array.shape) for array in arrays],
        [whole(d) for d in moved + dims],
        [shape(d, F32) for d in moved + dims],
        [],
        (1e6, 11e6),
    )(scalars, *rows, small, *arrays)


def on_device(
    tokens,
    episodes,
    attn_gain,
    attn_shift,
    qkv_weight,
    out_weight,
    out_bias,
    ffn_gain,
    ffn_shift,
    up_weight,
    up_bias,
    down_weight,
    down_bias,
    cotangent,
):
    replicas = lax.axis_size("dp")
    section = lax.axis_index("section")
    replica = lax.axis_index("dp")
    chip, core = section // 2, section % 2
    direct = replicas == 8
    y, z = (replica % 2, replica // 2) if direct else (0, 0)
    scalars = jnp.stack([jnp.asarray(v, jnp.int32) for v in (chip, core, y, z)])

    stream = tokens.reshape(2, 2, 2, BLOCK, D)
    cot = cotangent.reshape(2, 2, 2, BLOCK, D)
    eps = episodes.reshape(2, 1, LENGTH)
    ep_spec = pl.BlockSpec((1, 1, LENGTH), lambda i, sc: (sc[X], 0, 0))

    def input_spec(micro, side):
        return pl.BlockSpec((1, 2, 1, BLOCK, D), lambda i, sc: (micro(sc[X]), 0, side(sc[C]), 0, 0))

    same, flip = (lambda v: v), (lambda v: 1 - v)
    own_in, other_in, far_in = input_spec(same, same), input_spec(same, flip), input_spec(flip, same)
    local = pl.BlockSpec((1, 2, 1, BLOCK, D), lambda i, sc: (0, 0, 0, 0, 0))

    def rows5(value):
        return value.reshape(1, 2, 1, BLOCK, D)

    def vec(array):
        return array.reshape(2, 1, -1)

    a_gain, a_shift, b_out = vec(attn_gain), vec(attn_shift), vec(out_bias)
    f_gain, f_shift, b_up, b_down = vec(ffn_gain), vec(ffn_shift), vec(up_bias), vec(down_bias)

    kept = []
    own, own_spec, other, other_spec = stream, own_in, stream, other_in
    for layer in range(2):
        qkv, ctx, ctx_own, ctx_oth, lse = attention_forward(
            scalars, layer, own, own_spec, other, other_spec, eps, ep_spec, a_gain, a_shift, qkv_weight
        )
        ctx_rcv = to_core(ctx_oth)
        ctx_far = to_core(ctx_own)
        ffn = (f_gain, f_shift, up_weight, b_up, down_weight, b_down)
        if layer == 0:
            s2, ctx_full, act, slope, *result = ffn_forward(
                scalars, layer, ctx_own, ctx_rcv, own, own_spec, (out_weight, b_out) + ffn, ()
            )
            s2_o = to_chip(s2)
        else:
            s2, ctx_full = projected(
                scalars, layer, ctx_own, ctx_rcv, own, own_spec, out_weight, b_out, (kept[0][7], kept[0][11])
            )
            s2_o = to_chip(s2)
            act, slope, *result = last_ffn_forward(scalars, layer, s2, ffn)
        kept.append((own, own_spec, other, other_spec, qkv, ctx, ctx_oth, ctx_far, ctx_full, lse, s2, s2_o, act, slope))
        if layer == 0:
            s3 = result[0]
            own, own_spec, other, other_spec = rows5(s3), local, rows5(to_core(s3)), local
    final_keep, final_send = result

    def ffn_back(layer, grad, grad_spec, deps=()):
        kept_now = kept[layer]
        s2, slope = kept_now[10], kept_now[13]
        return ffn_backward(scalars, layer, grad, grad_spec, s2, slope, (f_gain, up_weight, down_weight), deps)

    def ffn_grads(layer, grad, grad_spec, grad_o, grad_o_spec, dh, deps=()):
        s2, s2_o, act, slope = kept[layer][10:]
        weights = (f_gain, f_shift, up_weight, b_up, down_weight)
        return ffn_weights(
            scalars, layer, grad, grad_spec, grad_o, grad_o_spec, s2, s2_o, act, dh, weights, deps
        )

    def attn_back(layer, ds, ds_rcv, deps=()):
        own, own_spec, other, other_spec, qkv, ctx, ctx_oth, ctx_far, ctx_full, lse = kept[layer][:10]
        return attention_backward(
            scalars, layer, ds, ds_rcv, qkv, ctx, lse, eps, ep_spec, out_weight, qkv_weight, deps
        )

    def attn_grads(layer, ds, ds_rcv, d_qkv, deps=()):
        own, own_spec, other, other_spec, qkv, ctx, ctx_oth, ctx_far, ctx_full, lse = kept[layer][:10]
        return attention_weights(
            scalars, layer, own, own_spec, other, other_spec, a_gain, a_shift, d_qkv, ds, ds_rcv, ctx_full, ctx_oth,
            ctx_far, deps,
        )

    def attn_norm(layer, ds, part_own, part_rcv, smalls=(), deps=()):
        own, own_spec = kept[layer][:2]
        return attention_norm_back(scalars, layer, ds, part_own, part_rcv, own, own_spec, a_gain, smalls, deps)

    if direct:
        pinned = []

        def summed(*outputs, deps=()):
            return combined(scalars, outputs, deps, pinned)

        def y_sum(keep, got):
            return [[(keep, 1), (got, 1)]]

        def z_sum(keep, got, y_got):
            return [[(keep, 0, k), (got, 0, k), (y_got, k)] for k in (1, 3)]

        def far_sum(keep, got, y_got, z_got):
            return [[(keep, 0, 2), (got, 0, 2), (y_got, 2), (z_got, 1)]]

        def share(keep, got, y_got, z_got, far_got):
            return [[(keep, 0, 0), (got, 0, 0), (y_got, 0), (z_got, 0), (far_got,)]]

        dh1, ds1, f_small1 = ffn_back(1, cot, own_in, [kept[1][7]])
        ds1_rcv = to_core(ds1)
        fk1, send = ffn_grads(1, cot, own_in, cot, far_in, dh1)
        pinned.append(fk1)
        fg1 = to_core(send)
        d_qkv1, part1, part1_oth = attn_back(1, ds1, ds1_rcv, [from_hbm(fk1)])
        part1_rcv = to_core(part1_oth)
        value, final_low = summed(y_sum(fk1, fg1), [[(final_send,)]], deps=[part1])
        fy1 = to_dp(value, 1)
        g0, a_small1 = attn_norm(1, ds1, part1, part1_rcv, deps=[value])
        g0_o = to_chip(g0)
        dh0, ds0, f_small0 = ffn_back(0, rows5(g0), local)
        ds0_rcv = to_core(ds0)
        fk0, send = ffn_grads(0, rows5(g0), local, rows5(g0_o), local, dh0)
        pinned.append(fk0)
        (fz1,) = summed(z_sum(fk1, fg1, fy1), deps=[from_hbm(fk0)])
        fg0 = to_core(send)
        qk1, send, ok1, z_send = attn_grads(1, ds1, ds1_rcv, d_qkv1, [fz1])
        pinned += [qk1, ok1]
        qg1, og1 = to_chip(send), to_dp(z_send, 2)
        fy0, final_low = summed(y_sum(fk0, fg0), [[(final_low,)]], deps=[from_hbm(qk1)])
        d_qkv0, part0, part0_oth = attn_back(0, ds0, ds0_rcv, [fy0])
        final_got = to_chip(final_low)
        fz1, fy0 = to_dp(fz1, 2), to_dp(fy0, 1)
        part0_rcv = to_core(part0_oth)
        far1, y1 = summed(
            far_sum(fk1, fg1, fy1, fz1),
            Flat([[(ok1, 0, 1), (og1, 0, 1)], [(ok1, 1, 1), (og1, 1, 1)]] + y_sum(qk1, qg1)),
            deps=[part0],
        )
        input_keep, input_send, small = attn_norm(
            0, ds0, part0, part0_rcv, (a_small1, f_small0, f_small1), [far1, final_got]
        )
        far1, y1 = to_dp(far1, 4), to_dp(y1, 1)
        small_got = to_core(small)
        input_got = to_chip(input_send)
        fz0, small = summed(z_sum(fk0, fg0, fy0), [[(small,), (small_got,)]], deps=[input_keep])
        qk0, send, ok0, y_send = attn_grads(0, ds0, ds0_rcv, d_qkv0, [fz0])
        fz0, small_got = to_dp(fz0, 2), to_dp(small, 4)
        pinned += [qk0, ok0]
        qg0, oy0 = to_chip(send), to_dp(y_send, 1)

        far, qz1, f1, small = summed(
            Flat(far_sum(fk0, fg0, fy0, fz0) + [[(ok1, 1, 0), (og1, 1, 0), (y1, slice(2, 4))]]),
            [[(qk1, 0, k), (qg1, 0, k), (y1, 4 + k)] for k in (1, 3)],
            share(fk1, fg1, fy1, fz1, far1),
            [[(small,), (small_got,)]],
            deps=[from_hbm(qk0)],
        )
        far, qz1, small_got = to_dp(far, 4), to_dp(qz1, 2), to_dp(small, 1)
        f1_all = gathered(f1)

        qy0, oz0, qf1, small = summed(
            y_sum(qk0, qg0),
            [[(ok0, k), (oy0, k)] for k in (1, 3)],
            [[(qk1, 0, 2), (qg1, 0, 2), (y1, 6), (qz1, 1)]],
            [[(small,), (small_got,)]],
            deps=[input_got],
        )
        qy0, oz0, qf1, small_got = to_dp(qy0, 1), to_dp(oz0, 2), to_dp(qf1, 4), to_chip(small)

        of0, qz0, f0, ox1, small = summed(
            [[(ok0, 2), (oy0, 2), (oz0, 1)]],
            z_sum(qk0, qg0, qy0),
            [[(fk0, 0, 0), (fg0, 0, 0), (fy0, 0), (fz0, 0), (far, slice(0, 4))]],
            [[(ok1, 0, 0), (og1, 0, 0), (y1, slice(0, 2)), (far, slice(4, 6))]],
            [[(small,), (small_got,)]],
            deps=f1_all[1:],
        )
        of0, qz0, ox1_got, small_got = to_dp(of0, 4), to_dp(qz0, 2), to_chip(ox1), to_dp(small, 2)
        f0_all = gathered(f0)

        qf0, ox0, o1, small = summed(
            far_sum(qk0, qg0, qy0, qz0),
            [[(ok0, 0), (oy0, 0), (oz0, 0), (of0,)]],
            [[(ox1,), (ox1_got,)]],
            [[(small,), (small_got,)]],
        )
        qf0, ox0_got = to_dp(qf0, 4), to_chip(ox0)

        both, o0 = summed(
            share(qk0, qg0, qy0, qz0, qf0) + [[(qk1, 0, 0), (qg1, 0, 0), (y1, 4), (qz1, 0), (qf1,)]],
            [[(ox0,), (ox0_got,)]],
            deps=f0_all[1:],
        )
        arrays = f0_all + f1_all + gathered(both) + (o0, to_core(o0), o1, to_core(o1))
        shares = (
            ((0, 1, 2, 3), tuple((n, 0) for n in range(8, 12)), (12, 13)),
            ((4, 5, 6, 7), tuple((n, 1) for n in range(8, 12)), (14, 15)),
        )
        (final_out, input_out, ups, downs, qkvs, outs, *vectors) = unpacked(
            scalars, (final_keep, final_got, input_keep, input_got), small, arrays, shares
        )
        g_a_gain, g_a_shift, g_b_out, g_f_gain, g_f_shift, g_b_down, g_b_up = vectors
    else:
        final_got = to_chip(final_send)
        grads = [None, None]
        grad, grad_spec, grad_o, grad_o_spec = cot, own_in, cot, far_in
        for layer in (1, 0):
            dh, ds, f_small = ffn_back(layer, grad, grad_spec)
            ds_rcv = to_core(ds)
            f_keep, f_send = ffn_grads(layer, grad, grad_spec, grad_o, grad_o_spec, dh)
            d_qkv, part_own, part_oth = attn_back(layer, ds, ds_rcv)
            keep, send, z_keep, z_send = attn_grads(layer, ds, ds_rcv, d_qkv)
            if layer == 1:
                g0, a_small1 = attn_norm(1, ds, part_own, to_core(part_oth))
                grad, grad_spec, grad_o, grad_o_spec = rows5(g0), local, rows5(to_chip(g0)), local
                f_small1 = f_small
            else:
                input_keep, input_send, small = attn_norm(
                    0, ds, part_own, to_core(part_oth), (a_small1, f_small, f_small1)
                )
            ffn = in_dp_order(total(f_keep, to_core(f_send)))
            qv = in_dp_order(total(keep, to_chip(send)))
            ko = jnp.stack([z_keep, z_send], 1).reshape(8, 2, PART, HALF)
            ko = total(ko, to_chip(ko))
            ordered = []
            for mine, far, near, both in (gathered(ffn), gathered(qv)):
                here = jnp.stack([jnp.where(chip == 0, mine, far), jnp.where(chip == 0, far, mine)])
                there = jnp.stack([jnp.where(chip == 0, near, both), jnp.where(chip == 0, both, near)])
                pair = jnp.stack([jnp.where(core == 0, here, there), jnp.where(core == 0, there, here)], 1)
                ordered.append(pair.astype(F32))
            ko_other = to_core(ko)
            ko_all = jnp.stack([jnp.where(core == 0, ko, ko_other), jnp.where(core == 0, ko_other, ko)]).astype(F32)
            f_all, qv_all = ordered
            up = f_all[:, :, :, 0:2].transpose(2, 4, 0, 1, 3, 5).reshape(D, FF)
            down = f_all[:, :, :, 2:4].transpose(2, 1, 3, 4, 0, 5).reshape(FF, D)
            q, v = (qv_all[n].transpose(1, 2, 0, 3).reshape(D, D) for n in range(2))
            k, out = (ko_all[:, :, n].transpose(1, 2, 0, 3).reshape(D, D) for n in range(2))
            grads[layer] = [
                lax.psum_scatter(array, "dp", scatter_dimension=0, tiled=True)
                for array in (up, down, jnp.concatenate([q, k, v], 1), out)
            ]
        ups, downs, qkvs, outs = (jnp.stack(pair) for pair in zip(*grads))
        small = lax.psum(small, ("section", "dp")).reshape(4, 8, D)

        def mine_of(rows):
            width = rows.shape[-1] // replicas
            return lax.dynamic_slice_in_dim(rows, replica * width, width, 1)

        g_a_gain, g_a_shift, g_b_out = (mine_of(small[0:2, n]) for n in range(3))
        g_f_gain, g_f_shift, g_b_down = (mine_of(small[2:4, n]) for n in range(3))
        g_b_up = mine_of(small[2:4, 4:8].reshape(2, FF))

        def placed(keep, got):
            got = got.astype(F32)
            return jnp.stack([jnp.where(chip == 0, keep, got), jnp.where(chip == 0, got, keep)])[:, None]

        final_out, input_out = placed(final_keep, final_got), placed(input_keep, to_chip(input_send))

    return (
        final_out,
        input_out,
        g_a_gain,
        g_a_shift,
        qkvs,
        outs,
        g_b_out,
        g_f_gain,
        g_f_shift,
        ups,
        g_b_up,
        downs,
        g_b_down,
    )


def solution(mesh):
    split = P(None, "dp", None, None)
    placed = (split, P(None, "dp", None)) + (P(),) * 11 + (split,)
    rows = P(None, "dp", "section", None)
    vector, matrix = P(None, "dp"), P(None, "dp", None)
    return jax.shard_map(
        on_device,
        mesh=mesh,
        in_specs=placed,
        out_specs=(
            rows,
            rows,
            vector,
            vector,
            matrix,
            matrix,
            vector,
            vector,
            vector,
            matrix,
            vector,
            matrix,
            vector,
        ),
        check_vma=False,
    )
```

```python
from functools import partial

import jax
import jax.numpy as jnp
from jax import lax
from jax.experimental import pallas as pl
from jax.experimental.pallas import tpu as pltpu
from jax.sharding import PartitionSpec as P

BF = jnp.bfloat16
F32 = jnp.float32
EPS = 1e-05
MASKED = -1e30
D = 768
HALF = 384
PAIR = 128
HEAD_DIM = 64
FF = 3072
LENGTH = 1024
BLOCK = 256
ROWS = 512
PART = 96
GELU_A = 0.7978845608028654
GELU_B = GELU_A * 0.044715


def dot(a, b):
    return jnp.dot(a, b, preferred_element_type=F32)


def dot_nt(a, b):
    return lax.dot_general(a, b, (((1,), (1,)), ((), ())), preferred_element_type=F32)


def dot_tn(a, b):
    return lax.dot_general(a, b, (((0,), (0,)), ((), ())), preferred_element_type=F32)


def normalise(rows):
    center = rows - jnp.mean(rows, -1, keepdims=True)
    spread = lax.rsqrt(jnp.mean(center * center, -1, keepdims=True) + EPS)
    return center * spread, spread


def norm_low(rows, gain, shift):
    unit, _ = normalise(rows.astype(F32))
    return (unit * gain + shift).astype(BF)


def call(body, grid, in_specs, out_specs, out_shape, scratch, cost, deps=(), aliases=None):
    count = len(in_specs)

    def with_deps(sc, *refs):
        return body(sc, *refs[:count], *refs[count + len(deps) :])

    kernel = pl.pallas_call(
        with_deps,
        grid_spec=pltpu.PrefetchScalarGridSpec(
            num_scalar_prefetch=1,
            grid=grid,
            in_specs=list(in_specs) + [pl.BlockSpec(memory_space=pl.ANY)] * len(deps),
            out_specs=out_specs,
            scratch_shapes=scratch,
        ),
        out_shape=out_shape,
        input_output_aliases=aliases or {},
        compiler_params=pltpu.CompilerParams(vmem_limit_bytes=32 * 1024 * 1024),
        cost_estimate=pl.CostEstimate(flops=int(5 * cost[0]), bytes_accessed=int(5 * cost[1]), transcendentals=0),
    )
    return lambda *args: kernel(*args, *deps)


def shape(dims, dtype):
    return jax.ShapeDtypeStruct(dims, dtype)


def stored(dims, dtype):
    return pltpu.MemorySpace.HBM(dims, dtype)


def from_hbm(array):
    return pltpu.with_memory_space_constraint(array, pltpu.MemorySpace.HBM)


def whole(dims):
    count = len(dims)
    return pl.BlockSpec(dims, lambda i, sc: (0,) * count)


def at_layer(dims, layer):
    count = len(dims) - 1
    return pl.BlockSpec(dims, lambda i, sc: (layer,) + (0,) * count)


X, C, Y, Z = 0, 1, 2, 3


def in_order(own, other, block, core):
    return jnp.where(core == block % 2, own[block // 2], other[block // 2])


def weight_copies(layer, core, weights, sides, sems):
    return [
        pltpu.make_async_copy(
            weights.at[layer, :, pl.ds(pl.multiple_of(j * D + core * HALF, PAIR), HALF)],
            sides.at[:, j * HALF : (j + 1) * HALF],
            sems.at[j],
        )
        for j in range(3)
    ]


def episode_columns(ep_ref):
    row = jnp.broadcast_to(ep_ref[...].reshape(1, LENGTH).astype(F32), (PAIR, LENGTH))
    return row, row.T


def first_key(i):
    return max(0, i - 2) * BLOCK


def attn_fwd_body(sc, own, other, ep, gain, shift, wq, wk, wv, qkv, ctx, ctx_own, ctx_oth, lse, bias, vext, lse_cols):
    core = sc[C]
    own, other = own.at[0, :, 0], other.at[0, :, 0]
    for b in range(4):
        rows = slice(b * BLOCK, (b + 1) * BLOCK)
        normed = norm_low(in_order(own, other, b, core), gain[0], shift[0])
        qkv[rows, 0:HALF] = (dot(normed, wq[0]).astype(BF) * 0.125).astype(BF)
        qkv[rows, HALF : 2 * HALF] = dot(normed, wk[0]).astype(BF)
        qkv[rows, 2 * HALF : 3 * HALF] = dot(normed, wv[0]).astype(BF)
    ep_row, ep_col = episode_columns(ep)
    for i in range(4):
        lo, hi = first_key(i), (i + 1) * BLOCK
        key_at = lo + lax.broadcasted_iota(jnp.int32, (BLOCK, hi - lo), 1)
        row_at = i * BLOCK + lax.broadcasted_iota(jnp.int32, (BLOCK, hi - lo), 0)
        same = ep_col[i * BLOCK : hi, 0:1] == ep_row[0:1, lo:hi]
        bias[i, :, 0 : hi - lo] = jnp.where((key_at <= row_at) & same, 0.0, MASKED)
    vext[:, PAIR:] = jnp.ones((LENGTH, PAIR), BF)
    lane = lax.broadcasted_iota(jnp.int32, (BLOCK, PAIR), 1)

    @pl.loop(0, 3)
    def _(p):
        at = pl.multiple_of(p * PAIR, PAIR)
        vext[:, 0:PAIR] = qkv[:, pl.ds(2 * HALF + at, PAIR)]
        for i in range(4):
            lo, hi = first_key(i), (i + 1) * BLOCK
            rows = slice(i * BLOCK, hi)
            q = qkv[rows, pl.ds(at, PAIR)]
            k = qkv[lo:hi, pl.ds(HALF + at, PAIR)]
            outs = []
            for h in range(2):
                mine = (lane >= HEAD_DIM) if h else (lane < HEAD_DIM)
                s = dot_nt(jnp.where(mine, q, jnp.zeros_like(q)), k) + bias[i, :, 0 : hi - lo]
                top = jnp.max(s, -1, keepdims=True)
                prob = jnp.exp(s - top).astype(BF)
                o = dot(prob, vext[lo:hi, :])
                total = o[:, PAIR : PAIR + 1]
                outs.append(o[:, 0:PAIR] / total)
                lse_cols[rows, :] = jnp.where(lane == 2 * p + h, top + jnp.log(total), lse_cols[rows, :])
            ctx[rows, pl.ds(at, PAIR)] = jnp.where(lane < HEAD_DIM, outs[0], outs[1]).astype(BF)

    lse[...] = lse_cols[...].T[0:8]
    for b in range(4):
        piece = ctx[b * BLOCK : (b + 1) * BLOCK]

        @pl.when(core == b % 2)
        def _():
            ctx_own[b // 2] = piece

        @pl.when(core != b % 2)
        def _():
            ctx_oth[b // 2] = piece


def attention_forward(scalars, layer, own, own_spec, other, other_spec, episodes, ep_spec, gain, shift, w_qkv):
    columns = [pl.BlockSpec((1, D, HALF), partial(lambda j, i, sc: (layer, 0, 2 * j + sc[C]), j)) for j in range(3)]
    return call(
        attn_fwd_body,
        (1,),
        [own_spec, other_spec, ep_spec, at_layer((1, 1, D), layer), at_layer((1, 1, D), layer)] + columns,
        [
            whole((LENGTH, 3 * HALF)),
            whole((LENGTH, HALF)),
            whole((2, BLOCK, HALF)),
            whole((2, BLOCK, HALF)),
            whole((8, LENGTH)),
        ],
        [
            stored((LENGTH, 3 * HALF), BF),
            stored((LENGTH, HALF), BF),
            shape((2, BLOCK, HALF), BF),
            shape((2, BLOCK, HALF), BF),
            shape((8, LENGTH), F32),
        ],
        [
            pltpu.VMEM((4, BLOCK, 3 * BLOCK), F32),
            pltpu.VMEM((LENGTH, 2 * PAIR), BF),
            pltpu.VMEM((LENGTH, PAIR), F32),
        ],
        (1.8e9 + 2.4e9, 8e6),
    )(scalars, own, other, episodes, gain, shift, *[from_hbm(w_qkv)] * 3)


def gelu_parts(u):
    cubic = GELU_B * (u * u)
    t = jnp.tanh(u * (GELU_A + cubic))
    half = 0.5 * t + 0.5
    active = u * half
    slope = half + (active * (1.0 - half)) * (6.0 * cubic + 2.0 * GELU_A)
    return active, slope


FT = 1024


def project_body(sc, ctx_own, ctx_rcv, own, w_out, b_out, s2, ctx_full):
    core = sc[C]
    a, b = ctx_own[...].reshape(ROWS, HALF), ctx_rcv[...].reshape(ROWS, HALF)
    both = jnp.concatenate([jnp.where(core == 0, a, b), jnp.where(core == 0, b, a)], 1)
    ctx_full[...] = both
    stream = own[0, :, 0].reshape(ROWS, D).astype(F32) + dot(both, w_out[0]) + b_out[0]
    s2[...] = stream.astype(BF)


def ffn_fwd_body(last, sc, *refs):
    if last:
        s2, gain, shift, w_up, b_up, w_down, b_down, act, slope, keep, send, normed, acc = refs
    else:
        gain, shift, w_up, b_up, w_down, b_down, s2, ctx_full, act, slope, s3, normed, acc = refs[5:]
    t = pl.program_id(0)

    @pl.when(t == 0)
    def _():
        if not last:
            project_body(sc, *refs[:5], s2, ctx_full)
        low = s2[...]
        normed[...] = norm_low(low, gain[0], shift[0])
        acc[...] = low.astype(F32) + b_down[0]

    u = dot(normed[...], w_up[0]) + b_up[0]
    a, d = gelu_parts(u)
    a = a.astype(BF)
    act[...] = a
    slope[...] = d.astype(BF)
    acc[...] += dot(a, w_down[0])

    @pl.when(t == FF // FT - 1)
    def _():
        if last:
            x = sc[X]
            keep[...] = acc[pl.ds(pl.multiple_of(x * BLOCK, BLOCK), BLOCK)]
            send[...] = acc[pl.ds(pl.multiple_of((1 - x) * BLOCK, BLOCK), BLOCK)].astype(BF)
        else:
            s3[...] = acc[...].reshape(2, BLOCK, D).astype(BF)


def ffn_forward(scalars, layer, ctx_own, ctx_rcv, own, own_spec, weights, deps):
    specs, ffn_weight_specs, hidden = projection_specs(layer, own_spec), ffn_specs(layer), hidden_specs()
    w_out, b_out, gain, shift, w_up, b_up, w_down, b_down = weights
    return call(
        partial(ffn_fwd_body, False),
        (FF // FT,),
        specs + ffn_weight_specs,
        [whole((ROWS, D)), whole((ROWS, D))] + hidden + [whole((2, BLOCK, D))],
        [shape((ROWS, D), BF)] * 2 + [stored((ROWS, FF), BF)] * 2 + [shape((2, BLOCK, D), BF)],
        [pltpu.VMEM((ROWS, D), BF), pltpu.VMEM((ROWS, D), F32)],
        (5.4e9, 20e6),
        deps,
    )(scalars, ctx_own, ctx_rcv, own, from_hbm(w_out), b_out, gain, shift, from_hbm(w_up), b_up, from_hbm(w_down), b_down)


def projected(scalars, layer, ctx_own, ctx_rcv, own, own_spec, w_out, b_out, deps):
    return call(
        project_body,
        (1,),
        projection_specs(layer, own_spec),
        [whole((ROWS, D)), whole((ROWS, D))],
        [shape((ROWS, D), BF)] * 2,
        [],
        (6e8, 5e6),
        deps,
    )(scalars, ctx_own, ctx_rcv, own, from_hbm(w_out), b_out)


def last_ffn_forward(scalars, layer, s2, weights):
    gain, shift, w_up, b_up, w_down, b_down = weights
    return call(
        partial(ffn_fwd_body, True),
        (FF // FT,),
        [whole((ROWS, D))] + ffn_specs(layer),
        hidden_specs() + [whole((BLOCK, D)), whole((BLOCK, D))],
        [shape((ROWS, FF), BF)] * 2 + [shape((BLOCK, D), F32), shape((BLOCK, D), BF)],
        [pltpu.VMEM((ROWS, D), BF), pltpu.VMEM((ROWS, D), F32)],
        (4.8e9, 18e6),
    )(scalars, s2, gain, shift, from_hbm(w_up), b_up, from_hbm(w_down), b_down)


def projection_specs(layer, own_spec):
    part = whole((2, BLOCK, HALF))
    return [part, part, own_spec, at_layer((1, D, D), layer), at_layer((1, 1, D), layer)]


def ffn_specs(layer):
    vector = at_layer((1, 1, D), layer)
    return [
        vector,
        vector,
        pl.BlockSpec((1, D, FT), lambda i, sc: (layer, 0, i)),
        pl.BlockSpec((1, 1, FT), lambda i, sc: (layer, 0, i)),
        pl.BlockSpec((1, FT, D), lambda i, sc: (layer, i, 0)),
        vector,
    ]


def hidden_specs():
    return [pl.BlockSpec((ROWS, FT), lambda i, sc: (0, i))] * 2


def norm_back(d_normed, rows, gain):
    unit, spread = normalise(rows)
    d_unit = d_normed * gain
    first = jnp.mean(d_unit, -1, keepdims=True)
    second = jnp.mean(d_unit * unit, -1, keepdims=True)
    d_rows = spread * (d_unit - first - unit * second)
    return d_rows, jnp.sum(d_normed * unit, 0, keepdims=True), jnp.sum(d_normed, 0, keepdims=True)


def small_rows(*vectors):
    return jnp.concatenate(vectors + (jnp.zeros((8 - len(vectors), D), F32),))


def attn_norm_body(last, sc, grad, part, part_rcv, own, gain, *rest):
    before, outs = rest[:3] if last else (), rest[3:] if last else rest
    grad_rows = grad[...].reshape(ROWS, D).astype(F32)
    d_normed = part[...].reshape(ROWS, D) + part_rcv[...].reshape(ROWS, D).astype(F32)
    d_rows, g_gain, g_shift = norm_back(d_normed, own[0, :, 0].reshape(ROWS, D).astype(F32), gain[0])
    total = grad_rows + d_rows
    small = outs[-1]
    small[0:8] = small_rows(g_gain, g_shift, jnp.sum(grad_rows, 0, keepdims=True))
    for j, ref in enumerate(before):
        small[8 * (j + 1) : 8 * (j + 2)] = ref[...]
    if last:
        keep, send = outs[0:2]
        keep[...] = jnp.where(sc[X] == 0, total[0:BLOCK], total[BLOCK:ROWS])
        send[...] = jnp.where(sc[X] == 0, total[BLOCK:ROWS], total[0:BLOCK]).astype(BF)
    else:
        outs[0][...] = total.astype(BF).reshape(2, BLOCK, D)


def attention_norm_back(scalars, layer, grad, part, part_rcv, own, own_spec, gain, smalls=(), deps=()):
    block = whole((2, BLOCK, D))
    last = bool(smalls)
    if last:
        out_specs = [whole((BLOCK, D)), whole((BLOCK, D))]
        out_shape = [shape((BLOCK, D), F32), shape((BLOCK, D), BF)]
    else:
        out_specs, out_shape = [block], [shape((2, BLOCK, D), BF)]
    rows = 8 * (1 + len(smalls))
    return call(
        partial(attn_norm_body, last),
        (1,),
        [block, block, block, own_spec, at_layer((1, 1, D), layer)] + [whole((8, D))] * len(smalls),
        out_specs + [whole((rows, D))],
        out_shape + [shape((rows, D), F32)],
        [],
        (2e8, 5e6),
        deps,
    )(scalars, grad, part, part_rcv, own, gain, *smalls)


BT = 768
AT = 1536


def ffn_back_body(sc, grad, s2, gain, w_up, w_down, slope, dh, ds, small, acc):
    t = pl.program_id(0)
    low = grad[0, :, 0].reshape(ROWS, D)
    d_act = dot_nt(low, w_down[0])
    d_hidden = d_act * slope[...].astype(F32)
    d_low = d_hidden.astype(BF)
    dh[...] = d_low
    sums = jnp.sum(d_low.astype(F32), 0, keepdims=True)
    for j in range(2):
        small[pl.ds(4 + 2 * t + j, 1)] = sums[:, j * D : (j + 1) * D]
    part = dot_nt(d_low, w_up[0])

    @pl.when(t == 0)
    def _():
        acc[...] = part

    @pl.when(t > 0)
    def _():
        acc[...] += part

    @pl.when(t == FF // AT - 1)
    def _():
        rows = low.astype(F32)
        d_rows, g_gain, g_shift = norm_back(acc[...], s2[...].astype(F32), gain[0])
        ds[...] = (rows + d_rows).astype(BF).reshape(2, BLOCK, D)
        small[0:4] = small_rows(g_gain, g_shift, jnp.sum(rows, 0, keepdims=True))[0:4]


def ffn_backward(scalars, layer, grad, grad_spec, s2, slope, weights, deps=()):
    gain, w_up, w_down = weights
    return call(
        ffn_back_body,
        (FF // AT,),
        [
            grad_spec,
            whole((ROWS, D)),
            at_layer((1, 1, D), layer),
            pl.BlockSpec((1, D, AT), lambda i, sc: (layer, 0, i)),
            pl.BlockSpec((1, AT, D), lambda i, sc: (layer, i, 0)),
            pl.BlockSpec((ROWS, AT), lambda i, sc: (0, i)),
        ],
        [
            pl.BlockSpec((ROWS, AT), lambda i, sc: (0, i)),
            whole((2, BLOCK, D)),
            whole((8, D)),
        ],
        [shape((ROWS, FF), BF), shape((2, BLOCK, D), BF), shape((8, D), F32)],
        [pltpu.VMEM((ROWS, D), F32)],
        (4.9e9, 18e6),
        deps,
    )(scalars, grad, s2, gain, from_hbm(w_up), from_hbm(w_down), (slope if layer == 1 else from_hbm(slope)))


def place(sc, piece):
    return (piece % 2) ^ sc[Y], (piece // 2) ^ sc[Z]


def ffn_weight_body(
    sc, grad, grad_o, s2, s2_o, gain, shift, act, dh, w_up, b_up, w_down, keep, send, n_t, n_o, n_t_o, g_t, g_t_o
):
    t = pl.program_id(0)
    core = sc[C]
    low, low_o = grad[0, :, 0].reshape(ROWS, D), grad_o[0, :, 0].reshape(ROWS, D)

    @pl.when(t == 0)
    def _():
        n_t[...] = norm_low(s2[...], gain[0], shift[0]).T
        other = norm_low(s2_o[...], gain[0], shift[0])
        n_o[...] = other
        n_t_o[...] = other.T
        x = sc[X]
        g_t[...] = jnp.where(x == 0, low[:, 0:HALF], low[:, HALF:D]).T
        g_t_o[...] = jnp.where(x == 0, low_o[:, 0:HALF], low_o[:, HALF:D]).T

    u = dot(n_o[...], w_up[0]) + b_up[0]
    active_o, slope_o = gelu_parts(u)

    @pl.when(t < 2)
    def _():
        dh_o = (dot_nt(low_o, w_down[0]) * slope_o).astype(BF)
        g_up = (dot(n_t[...], dh[...]) + dot(n_t_o[...], dh_o)).astype(BF)
        for ref, when in ((send, 0), (keep, 1)):

            @pl.when(t == when)
            def _():
                for piece in range(8):
                    py, pz = place(sc, piece)
                    for j in range(2):
                        ref[py, pz, j] = g_up[piece * PART : (piece + 1) * PART, j * HALF : (j + 1) * HALF]

    g_down = (dot(g_t[...], act[...]) + dot(g_t_o[...], active_o.astype(BF))).astype(BF).T
    tile = ffn_tile(t, sc)
    for half in range(2):
        py, pz = place(sc, 2 * tile + half)
        for j in range(2):
            first = g_down[half * HALF + j * PART : half * HALF + (j + 1) * PART]
            second = g_down[half * HALF + (j + 2) * PART : half * HALF + (j + 3) * PART]
            keep[py, pz, 2 + j] = jnp.where(core == 0, first, second)
            send[py, pz, 2 + j] = jnp.where(core == 0, second, first)


def ffn_tile(step, sc):
    mine = 2 * sc[X]
    rest = 2 - mine
    return jnp.where(step == 0, mine + 1 - sc[C], jnp.where(step == 1, mine + sc[C], rest + step - 2))


def ffn_weights(scalars, layer, grad, grad_spec, grad_o, grad_o_spec, s2, s2_o, act, dh, weights, deps=()):
    gain, shift, w_up, b_up, w_down = weights
    packed = (2, 4, 4, PART, HALF)
    return call(
        ffn_weight_body,
        (FF // BT,),
        [
            grad_spec,
            grad_o_spec,
            whole((ROWS, D)),
            whole((ROWS, D)),
            at_layer((1, 1, D), layer),
            at_layer((1, 1, D), layer),
            pl.BlockSpec((ROWS, BT), lambda i, sc: (0, ffn_tile(i, sc))),
            pl.BlockSpec((ROWS, BT), lambda i, sc: (0, ffn_tile(jnp.minimum(i, 1), sc))),
            pl.BlockSpec((1, D, BT), lambda i, sc: (layer, 0, ffn_tile(i, sc))),
            pl.BlockSpec((1, 1, BT), lambda i, sc: (layer, 0, ffn_tile(i, sc))),
            pl.BlockSpec((1, BT, D), lambda i, sc: (layer, ffn_tile(jnp.minimum(i, 1), sc), 0)),
        ],
        [whole(packed), whole(packed)],
        [stored(packed, BF), shape(packed, BF)],
        [
            pltpu.VMEM((D, ROWS), BF),
            pltpu.VMEM((ROWS, D), BF),
            pltpu.VMEM((D, ROWS), BF),
            pltpu.VMEM((HALF, ROWS), BF),
            pltpu.VMEM((HALF, ROWS), BF),
        ],
        (8.6e9, 22e6),
        deps,
    )(scalars, grad, grad_o, s2, s2_o, gain, shift, (act if layer == 1 else from_hbm(act)), dh, from_hbm(w_up), b_up, from_hbm(w_down))


def attn_back_body(
    layer, sc, gr_own, gr_rcv, qkv, ctx, lse, ep, w_out, weights, d_qkv, part_own, part_oth, bias, d_ctx, delta, d_k, d_v,
    sides, sems
):
    core = sc[C]
    copies = weight_copies(layer, core, weights, sides, sems)
    for copy in copies:
        copy.start()
    for b in range(4):
        rows = slice(b * BLOCK, (b + 1) * BLOCK)
        d_ctx[rows] = dot_nt(in_order(gr_own, gr_rcv, b, core), w_out[0]).astype(BF)
    product = d_ctx[...].astype(F32) * ctx[...].astype(F32)
    high = product.astype(BF)
    rest = (product - high.astype(F32)).astype(BF)
    picks = (
        lax.broadcasted_iota(jnp.int32, (8, HALF), 0) == lax.broadcasted_iota(jnp.int32, (8, HALF), 1) // HEAD_DIM
    ).astype(BF)
    delta[...] = dot_nt(picks, high) + dot_nt(picks, rest)
    ep_row, ep_col = episode_columns(ep)
    for i in range(4):
        lo, hi = first_key(i), (i + 1) * BLOCK
        key_at = lo + lax.broadcasted_iota(jnp.int32, (hi - lo, BLOCK), 0)
        row_at = i * BLOCK + lax.broadcasted_iota(jnp.int32, (hi - lo, BLOCK), 1)
        same = ep_col[lo:hi, 0:1] == ep_row[0:1, i * BLOCK : hi]
        bias[i, 0 : hi - lo, :] = jnp.where((key_at <= row_at) & same, 0.0, MASKED)

    @pl.loop(0, 3)
    def _(p):
        at = pl.multiple_of(p * PAIR, PAIR)
        d_k[...] = jnp.zeros_like(d_k)
        d_v[...] = jnp.zeros_like(d_v)
        for i in range(4):
            lo, hi = first_key(i), (i + 1) * BLOCK
            rows = slice(i * BLOCK, hi)
            q = qkv[rows, pl.ds(at, PAIR)]
            k = qkv[lo:hi, pl.ds(HALF + at, PAIR)]
            v = qkv[lo:hi, pl.ds(2 * HALF + at, PAIR)]
            dc = d_ctx[rows, pl.ds(at, PAIR)]
            d_q = jnp.zeros((BLOCK, PAIR), F32)
            for h in range(2):

                def only(array):
                    lane = lax.broadcasted_iota(jnp.int32, array.shape, 1)
                    mine = (lane >= HEAD_DIM) if h else (lane < HEAD_DIM)
                    return jnp.where(mine, array, jnp.zeros_like(array))

                q_h, dc_h = only(q), only(dc)
                s = dot_nt(k, q_h) + bias[i, 0 : hi - lo, :]
                prob = jnp.exp(s - lse[pl.ds(2 * p + h, 1), rows])
                d_p = dot_nt(v, dc_h)
                d_s = (prob * (d_p - delta[pl.ds(2 * p + h, 1), rows])).astype(BF)
                d_v[lo:hi] += dot(prob.astype(BF), dc_h)
                d_k[lo:hi] += dot(d_s, q_h)
                d_q += dot_tn(d_s, only(k))
            d_qkv[rows, pl.ds(at, PAIR)] = (d_q * 0.125).astype(BF)
        d_qkv[:, pl.ds(HALF + at, PAIR)] = d_k[...].astype(BF)
        d_qkv[:, pl.ds(2 * HALF + at, PAIR)] = d_v[...].astype(BF)

    for copy in copies:
        copy.wait()
    for b in range(4):
        rows = slice(b * BLOCK, (b + 1) * BLOCK)
        part = dot_nt(d_qkv[rows], sides[...])

        @pl.when(core == b % 2)
        def _():
            part_own[b // 2] = part

        @pl.when(core != b % 2)
        def _():
            part_oth[b // 2] = part.astype(BF)


def attention_backward(scalars, layer, gr_own, gr_rcv, qkv, ctx, lse, episodes, ep_spec, w_out, w_qkv, deps=()):
    block = whole((2, BLOCK, D))
    return call(
        partial(attn_back_body, layer),
        (1,),
        [
            block,
            block,
            whole((LENGTH, 3 * HALF)),
            whole((LENGTH, HALF)),
            whole((8, LENGTH)),
            ep_spec,
            pl.BlockSpec((1, HALF, D), lambda i, sc: (layer, sc[C], 0)),
            pl.BlockSpec(memory_space=pl.ANY),
        ],
        [whole((LENGTH, 3 * HALF)), block, block],
        [shape((LENGTH, 3 * HALF), BF), shape((2, BLOCK, D), F32), shape((2, BLOCK, D), BF)],
        [
            pltpu.VMEM((4, 3 * BLOCK, BLOCK), F32),
            pltpu.VMEM((LENGTH, HALF), BF),
            pltpu.VMEM((8, LENGTH), F32),
            pltpu.VMEM((LENGTH, PAIR), F32),
            pltpu.VMEM((LENGTH, PAIR), F32),
            pltpu.VMEM((D, 3 * HALF), BF),
            pltpu.SemaphoreType.DMA((3,)),
        ],
        (2.5e9 + 6e9, 12e6),
        deps,
    )(scalars, gr_own, gr_rcv, from_hbm(qkv), from_hbm(ctx), lse, episodes, from_hbm(w_out), from_hbm(w_qkv))


def attn_weight_body(
    z_first, sc, own, other, gain, shift, d_qkv, gr_own, gr_rcv, ctx_full, ctx_oth, ctx_rcv, keep, send, z_keep, z_send, n_t
):
    core, x = sc[C], sc[X]
    own, other = own.at[0, :, 0], other.at[0, :, 0]
    for b in range(4):
        rows = slice(b * BLOCK, (b + 1) * BLOCK)
        n_t[:, rows] = norm_low(in_order(own, other, b, core), gain[0], shift[0]).T

    def columns(ref):
        rows = ref[...].reshape(ROWS, D)
        return jnp.where(core == 0, rows[:, 0:HALF], rows[:, HALF:D]).T

    def grad(j):
        return dot(n_t[...], d_qkv[:, j * HALF : (j + 1) * HALF]).astype(BF)

    first, second = grad(0), grad(2)
    mine, yours = jnp.where(x == 0, first, second), jnp.where(x == 0, second, first)
    for piece in range(8):
        py, pz = place(sc, piece)
        keep[py, pz] = mine[piece * PART : (piece + 1) * PART]
        send[py, pz] = yours[piece * PART : (piece + 1) * PART]

    a, b = ctx_oth[...].reshape(ROWS, HALF), ctx_rcv[...].reshape(ROWS, HALF)
    far = jnp.concatenate([jnp.where(core == 0, a, b), jnp.where(core == 0, b, a)], 1)
    g_out = (dot(columns(gr_own), ctx_full[...]) + dot(columns(gr_rcv), far)).astype(BF).T
    for j, rows in enumerate((grad(1), g_out)):
        for piece in range(8):
            py, pz = place(sc, piece)
            value = rows[piece * PART : (piece + 1) * PART]

            far = pz % 2 if z_first else py

            @pl.when(far == 0)
            def _():
                if z_first:
                    z_keep[pz // 2, py, j] = value
                else:
                    z_keep[pz, j] = value

            @pl.when(far == 1)
            def _():
                if z_first:
                    z_send[pz // 2, py, j] = value
                else:
                    z_send[pz, j] = value


def attention_weights(
    scalars, layer, own, own_spec, other, other_spec, gain, shift, d_qkv, gr_own, gr_rcv, ctx_full, ctx_oth, ctx_rcv, deps=()
):
    z_first = layer == 1
    packed, z_packed = (2, 4, PART, HALF), ((2, 2) if z_first else (4,)) + (2, PART, HALF)
    block = whole((2, BLOCK, D))
    return call(
        partial(attn_weight_body, z_first),
        (1,),
        [
            own_spec,
            other_spec,
            at_layer((1, 1, D), layer),
            at_layer((1, 1, D), layer),
            whole((LENGTH, 3 * HALF)),
            block,
            block,
            whole((ROWS, D)),
            whole((2, BLOCK, HALF)),
            whole((2, BLOCK, HALF)),
        ],
        [whole(packed), whole(packed), whole(z_packed), whole(z_packed)],
        [stored(packed, BF), shape(packed, BF), stored(z_packed, BF), shape(z_packed, BF)],
        [pltpu.VMEM((D, LENGTH), BF)],
        (2.5e9, 12e6),
        deps,
    )(scalars, own, other, gain, shift, d_qkv, gr_own, gr_rcv, ctx_full, ctx_oth, ctx_rcv)


def to_core(value):
    return lax.ppermute(value, "section", [(0, 1), (1, 0), (2, 3), (3, 2)])


def to_chip(value):
    return lax.ppermute(value, "section", [(0, 2), (2, 0), (1, 3), (3, 1)])


def to_dp(value, distance):
    return lax.ppermute(value, "dp", [(i, i ^ distance) for i in range(8)])


def total(*terms):
    out = terms[0].astype(F32)
    for term in terms[1:]:
        out = out + term.astype(F32)
    return out.astype(BF)


class Flat(list):
    pass


def combined(scalars, outputs, deps=(), pinned=()):
    terms, dims, dtypes = [], [], []

    def block_of(term):
        array, *index = term
        if index and isinstance(index[0], slice):
            count = index[0].stop - index[0].start
            return (count,) + array.shape[1:], (index[0].start // count,) + (0,) * (array.ndim - 1)
        rest = array.shape[len(index) :]
        return (None,) * len(index) + rest, tuple(index) + (0,) * len(rest)

    def dims_of(term):
        return tuple(d for d in block_of(term)[0] if d is not None)

    def rows_of(piece):
        found = dims_of(piece[0])
        return found[0] if len(found) == 3 else 1

    for pieces in outputs:
        rest = dims_of(pieces[0][0])
        if isinstance(pieces, Flat):
            dims.append((sum(rows_of(piece) for piece in pieces),) + rest[-2:])
        else:
            dims.append(((len(pieces),) if len(pieces) > 1 else ()) + rest)
        dtypes.append(pieces[0][0][0].dtype)
        terms += [term for piece in pieces for term in piece]

    def spec(term):
        block, index = block_of(term)
        return pl.BlockSpec(block, lambda i, sc: index)

    def body(sc, *refs):
        given = iter(refs[: len(terms)])
        for out, pieces in zip(refs[len(terms) :], outputs):
            at = 0
            for n, piece in enumerate(pieces):
                value = next(given)[...].astype(F32)
                for _ in piece[1:]:
                    value = value + next(given)[...].astype(F32)
                value = value.astype(out.dtype)
                if isinstance(pieces, Flat):
                    rows = rows_of(piece)
                    if len(value.shape) == 3:
                        out[at : at + rows] = value
                    else:
                        out[at] = value
                    at += rows
                elif len(pieces) > 1:
                    out[n] = value
                else:
                    out[...] = value

    return call(
        body,
        (1,),
        [spec(term) for term in terms],
        [whole(d) for d in dims],
        [shape(d, t) for d, t in zip(dims, dtypes)],
        [],
        (1e10, 1e7),
        deps,
    )(scalars, *[from_hbm(term[0]) if any(term[0] is a for a in pinned) else term[0] for term in terms])


def in_dp_order(both):
    return jnp.moveaxis(both, 0, 1).reshape((8,) + both.shape[2:])


def gathered(share):
    far, near = to_chip(share), to_core(share)
    return share, far, near, to_core(far)


def ffn_unpacked(sc, shares, up, down):
    for n in range(4):
        x, core = sc[X] ^ (n % 2), sc[C] ^ (n // 2)
        for j in range(2):
            at = pl.multiple_of(x * 4 * HALF + core * 2 * HALF + j * HALF, PAIR)
            up[0, :, pl.ds(at, HALF)] = shares[n][j].astype(F32)
            rows = pl.ds(pl.multiple_of(core * 2 * PART + j * PART, 8), PART)
            down[0, rows, pl.ds(pl.multiple_of(x * HALF, PAIR), HALF)] = shares[n][2 + j].astype(F32)


def unpack_early_body(sc, final_keep, final_got, input_keep, input_got, *refs):
    final, inputs, up, down = refs[-4:]
    x = sc[X]
    for ref, mine, got in ((final, final_keep, final_got), (inputs, input_keep, input_got)):
        ref[x, 0] = mine[...]
        ref[1 - x, 0] = got[...].astype(F32)
    ffn_unpacked(sc, refs[:4], up, down)


def unpack_body(shares, sc, small, up_before, down_before, *refs):
    up, down, qkv, out, a_gain, a_shift, b_out, f_gain, f_shift, b_down, b_up = refs[-11:]
    ffn_unpacked(sc, refs[:4], up, down)
    for layer in range(2):
        qv, ko = shares[layer]
        for n in range(4):
            x, core = sc[X] ^ (n % 2), sc[C] ^ (n // 2)
            index, at = qv[n]
            qkv[layer, :, pl.ds(pl.multiple_of(x * 2 * D + core * HALF, PAIR), HALF)] = refs[index][at].astype(F32)
        for n in range(2):
            side = pl.multiple_of((sc[C] ^ n) * HALF, PAIR)
            qkv[layer, :, pl.ds(pl.multiple_of(D + side, PAIR), HALF)] = refs[ko[n]][0].astype(F32)
            out[layer, :, pl.ds(side, HALF)] = refs[ko[n]][1].astype(F32)
    piece = 2 * sc[Z] + sc[Y]
    mine = jnp.zeros((32, PART), F32)
    for d in range(8):
        mine = jnp.where(piece == d, small[:, d * PART : (d + 1) * PART], mine)
    for layer in range(2):
        for j, (a_ref, f_ref) in enumerate(((a_gain, f_gain), (a_shift, f_shift), (b_out, b_down))):
            a_ref[layer : layer + 1] = mine[8 * layer + j : 8 * layer + j + 1]
            f_ref[layer : layer + 1] = mine[16 + 8 * layer + j : 16 + 8 * layer + j + 1]
        row = jnp.zeros((1, 4 * PART), F32)
        for d in range(8):
            at = 16 + 8 * layer + 4 + d // 2
            row = jnp.where(piece == d, small[at : at + 1, (d % 2) * HALF : (d % 2 + 1) * HALF], row)
        b_up[layer : layer + 1] = row


FFN_GRADS = ((2, PART, FF), (2, 4 * PART, D))


def unpacked_early(scalars, rows, arrays, layer):
    moved = ((2, 1, BLOCK, D),) * 2
    return call(
        unpack_early_body,
        (1,),
        [whole((BLOCK, D))] * 4 + [whole(array.shape) for array in arrays],
        [whole(d) for d in moved] + [at_layer((1,) + d[1:], layer) for d in FFN_GRADS],
        [shape(d, F32) for d in moved] + [stored(d, F32) for d in FFN_GRADS],
        [],
        (1e6, 9e6),
    )(scalars, *rows, *arrays)


def unpacked(scalars, small, up, down, arrays, shares):
    dims = ((2, PART, 3 * D), (2, PART, D)) + ((2, PART),) * 6 + ((2, 4 * PART),)
    held = pl.BlockSpec(memory_space=pl.ANY)
    return call(
        partial(unpack_body, shares),
        (1,),
        [whole((32, D)), held, held] + [whole(array.shape) for array in arrays],
        [at_layer((1,) + d[1:], 0) for d in FFN_GRADS] + [whole(d) for d in dims],
        [stored(d, F32) for d in FFN_GRADS] + [shape(d, F32) for d in dims],
        [],
        (1e6, 11e6),
        aliases={2: 0, 3: 1},
    )(scalars, small, from_hbm(up), from_hbm(down), *arrays)


def on_device(
    tokens,
    episodes,
    attn_gain,
    attn_shift,
    qkv_weight,
    out_weight,
    out_bias,
    ffn_gain,
    ffn_shift,
    up_weight,
    up_bias,
    down_weight,
    down_bias,
    cotangent,
):
    replicas = lax.axis_size("dp")
    section = lax.axis_index("section")
    replica = lax.axis_index("dp")
    chip, core = section // 2, section % 2
    direct = replicas == 8
    y, z = (replica % 2, replica // 2) if direct else (0, 0)
    scalars = jnp.stack([jnp.asarray(v, jnp.int32) for v in (chip, core, y, z)])

    stream = tokens.reshape(2, 2, 2, BLOCK, D)
    cot = cotangent.reshape(2, 2, 2, BLOCK, D)
    eps = episodes.reshape(2, 1, LENGTH)
    ep_spec = pl.BlockSpec((1, 1, LENGTH), lambda i, sc: (sc[X], 0, 0))

    def input_spec(micro, side):
        return pl.BlockSpec((1, 2, 1, BLOCK, D), lambda i, sc: (micro(sc[X]), 0, side(sc[C]), 0, 0))

    same, flip = (lambda v: v), (lambda v: 1 - v)
    own_in, other_in, far_in = input_spec(same, same), input_spec(same, flip), input_spec(flip, same)
    local = pl.BlockSpec((1, 2, 1, BLOCK, D), lambda i, sc: (0, 0, 0, 0, 0))

    def rows5(value):
        return value.reshape(1, 2, 1, BLOCK, D)

    def vec(array):
        return array.reshape(2, 1, -1)

    a_gain, a_shift, b_out = vec(attn_gain), vec(attn_shift), vec(out_bias)
    f_gain, f_shift, b_up, b_down = vec(ffn_gain), vec(ffn_shift), vec(up_bias), vec(down_bias)

    kept = []
    own, own_spec, other, other_spec = stream, own_in, stream, other_in
    for layer in range(2):
        seen = (own, own_spec, other, other_spec)
        if layer == 0:
            seen = (from_hbm(own), own_spec, from_hbm(other), other_spec)
        qkv, ctx, ctx_own, ctx_oth, lse = attention_forward(
            scalars, layer, *seen, eps, ep_spec, a_gain, a_shift, qkv_weight
        )
        ctx_rcv = to_core(ctx_oth)
        ctx_far = to_core(ctx_own)
        ffn = (f_gain, f_shift, up_weight, b_up, down_weight, b_down)
        if layer == 0:
            s2, ctx_full, act, slope, *result = ffn_forward(
                scalars, layer, ctx_own, ctx_rcv, own, own_spec, (out_weight, b_out) + ffn, ()
            )
            s2_o = to_chip(s2)
        else:
            s2, ctx_full = projected(
                scalars, layer, ctx_own, ctx_rcv, own, own_spec, out_weight, b_out, (kept[0][7], kept[0][11])
            )
            s2_o = to_chip(s2)
            act, slope, *result = last_ffn_forward(scalars, layer, s2, ffn)
        kept.append((own, own_spec, other, other_spec, qkv, ctx, ctx_oth, ctx_far, ctx_full, lse, s2, s2_o, act, slope))
        if layer == 0:
            s3 = result[0]
            own, own_spec, other, other_spec = rows5(s3), local, rows5(to_core(s3)), local
    final_keep, final_send = result

    def ffn_back(layer, grad, grad_spec, deps=()):
        kept_now = kept[layer]
        s2, slope = kept_now[10], kept_now[13]
        return ffn_backward(scalars, layer, grad, grad_spec, s2, slope, (f_gain, up_weight, down_weight), deps)

    def ffn_grads(layer, grad, grad_spec, grad_o, grad_o_spec, dh, deps=()):
        s2, s2_o, act, slope = kept[layer][10:]
        weights = (f_gain, f_shift, up_weight, b_up, down_weight)
        return ffn_weights(
            scalars, layer, grad, grad_spec, grad_o, grad_o_spec, s2, s2_o, act, dh, weights, deps
        )

    def attn_back(layer, ds, ds_rcv, deps=()):
        own, own_spec, other, other_spec, qkv, ctx, ctx_oth, ctx_far, ctx_full, lse = kept[layer][:10]
        return attention_backward(
            scalars, layer, ds, ds_rcv, qkv, ctx, lse, eps, ep_spec, out_weight, qkv_weight, deps
        )

    def attn_grads(layer, ds, ds_rcv, d_qkv, deps=()):
        own, own_spec, other, other_spec, qkv, ctx, ctx_oth, ctx_far, ctx_full, lse = kept[layer][:10]
        return attention_weights(
            scalars, layer, own, own_spec, other, other_spec, a_gain, a_shift, d_qkv, ds, ds_rcv, ctx_full, ctx_oth,
            ctx_far, deps,
        )

    def attn_norm(layer, ds, part_own, part_rcv, smalls=(), deps=()):
        own, own_spec = kept[layer][:2]
        return attention_norm_back(scalars, layer, ds, part_own, part_rcv, own, own_spec, a_gain, smalls, deps)

    if direct:
        pinned = []

        def summed(*outputs, deps=()):
            return combined(scalars, outputs, deps, pinned)

        def y_sum(keep, got):
            return [[(keep, 1), (got, 1)]]

        def z_sum(keep, got, y_got):
            return [[(keep, 0, k), (got, 0, k), (y_got, k)] for k in (1, 3)]

        def far_sum(keep, got, y_got, z_got):
            return [[(keep, 0, 2), (got, 0, 2), (y_got, 2), (z_got, 1)]]

        def share(keep, got, y_got, z_got, far_got):
            return [[(keep, 0, 0), (got, 0, 0), (y_got, 0), (z_got, 0), (far_got,)]]

        dh1, ds1, f_small1 = ffn_back(1, cot, own_in, [kept[1][7]])
        ds1_rcv = to_core(ds1)
        fk1, send = ffn_grads(1, cot, own_in, cot, far_in, dh1)
        pinned.append(fk1)
        fg1 = to_core(send)
        d_qkv1, part1, part1_oth = attn_back(1, ds1, ds1_rcv, [from_hbm(fk1)])
        part1_rcv = to_core(part1_oth)
        value, final_low = summed(y_sum(fk1, fg1), [[(final_send,)]], deps=[part1])
        fy1 = to_dp(value, 1)
        g0, a_small1 = attn_norm(1, ds1, part1, part1_rcv, deps=[value])
        g0_o = to_chip(g0)
        dh0, ds0, f_small0 = ffn_back(0, rows5(g0), local)
        ds0_rcv = to_core(ds0)
        qk1, send, ok1, z_send = attn_grads(1, ds1, ds1_rcv, d_qkv1, [ds0])
        pinned += [qk1, ok1]
        qg1, og1 = to_chip(send), to_dp(z_send, 2)
        fk0, send = ffn_grads(0, rows5(g0), local, rows5(g0_o), local, dh0, [from_hbm(qk1)])
        pinned.append(fk0)
        fg0 = to_core(send)
        (fz1,) = summed(z_sum(fk1, fg1, fy1), deps=[from_hbm(fk0)])
        fy0, final_low = summed(y_sum(fk0, fg0), [[(final_low,)]], deps=[fz1])
        d_qkv0, part0, part0_oth = attn_back(0, ds0, ds0_rcv, [fy0])
        final_got = to_chip(final_low)
        fz1, fy0 = to_dp(fz1, 2), to_dp(fy0, 1)
        part0_rcv = to_core(part0_oth)
        far1, y1 = summed(
            far_sum(fk1, fg1, fy1, fz1),
            Flat([[(ok1, 0, 1), (og1, 0, 1)], [(ok1, 1, 1), (og1, 1, 1)]] + y_sum(qk1, qg1)),
            deps=[part0],
        )
        input_keep, input_send, small = attn_norm(
            0, ds0, part0, part0_rcv, (a_small1, f_small0, f_small1), [far1, final_got]
        )
        far1, y1 = to_dp(far1, 4), to_dp(y1, 1)
        small_got = to_core(small)
        input_got = to_chip(input_send)
        fz0, small = summed(z_sum(fk0, fg0, fy0), [[(small,), (small_got,)]], deps=[input_keep])
        qk0, send, ok0, y_send = attn_grads(0, ds0, ds0_rcv, d_qkv0, [fz0])
        fz0, small_got = to_dp(fz0, 2), to_dp(small, 4)
        pinned += [qk0, ok0]
        qg0, oy0 = to_chip(send), to_dp(y_send, 1)

        far, qz1, f1, small = summed(
            Flat(far_sum(fk0, fg0, fy0, fz0) + [[(ok1, 1, 0), (og1, 1, 0), (y1, slice(2, 4))]]),
            [[(qk1, 0, k), (qg1, 0, k), (y1, 4 + k)] for k in (1, 3)],
            share(fk1, fg1, fy1, fz1, far1),
            [[(small,), (small_got,)]],
            deps=[from_hbm(qk0)],
        )
        far, qz1, small_got = to_dp(far, 4), to_dp(qz1, 2), to_dp(small, 1)
        f1_all = gathered(f1)

        qy0, oz0, qf1, small = summed(
            y_sum(qk0, qg0),
            [[(ok0, k), (oy0, k)] for k in (1, 3)],
            [[(qk1, 0, 2), (qg1, 0, 2), (y1, 6), (qz1, 1)]],
            [[(small,), (small_got,)]],
            deps=[input_got],
        )
        qy0, oz0, qf1, small_got = to_dp(qy0, 1), to_dp(oz0, 2), to_dp(qf1, 4), to_chip(small)

        of0, qz0, f0, ox1, small = summed(
            [[(ok0, 2), (oy0, 2), (oz0, 1)]],
            z_sum(qk0, qg0, qy0),
            [[(fk0, 0, 0), (fg0, 0, 0), (fy0, 0), (fz0, 0), (far, slice(0, 4))]],
            [[(ok1, 0, 0), (og1, 0, 0), (y1, slice(0, 2)), (far, slice(4, 6))]],
            [[(small,), (small_got,)]],
            deps=f1_all[1:],
        )
        of0, qz0, ox1_got, small_got = to_dp(of0, 4), to_dp(qz0, 2), to_chip(ox1), to_dp(small, 2)
        f0_all = gathered(f0)

        qf0, ox0, o1, small = summed(
            far_sum(qk0, qg0, qy0, qz0),
            [[(ok0, 0), (oy0, 0), (oz0, 0), (of0,)]],
            [[(ox1,), (ox1_got,)]],
            [[(small,), (small_got,)]],
        )
        qf0, ox0_got = to_dp(qf0, 4), to_chip(ox0)

        final_out, input_out, ups, downs = unpacked_early(
            scalars, (final_keep, final_got, input_keep, input_got), f1_all, 1
        )
        both, o0 = summed(
            share(qk0, qg0, qy0, qz0, qf0) + [[(qk1, 0, 0), (qg1, 0, 0), (y1, 4), (qz1, 0), (qf1,)]],
            [[(ox0,), (ox0_got,)]],
            deps=f0_all[1:] + (from_hbm(ups),),
        )
        arrays = f0_all + gathered(both) + (o0, to_core(o0), o1, to_core(o1))
        shares = ((tuple((n, 0) for n in range(4, 8)), (8, 9)), (tuple((n, 1) for n in range(4, 8)), (10, 11)))
        (ups, downs, qkvs, outs, *vectors) = unpacked(scalars, small, ups, downs, arrays, shares)
        g_a_gain, g_a_shift, g_b_out, g_f_gain, g_f_shift, g_b_down, g_b_up = vectors
    else:
        final_got = to_chip(final_send)
        grads = [None, None]
        grad, grad_spec, grad_o, grad_o_spec = cot, own_in, cot, far_in
        for layer in (1, 0):
            dh, ds, f_small = ffn_back(layer, grad, grad_spec)
            ds_rcv = to_core(ds)
            f_keep, f_send = ffn_grads(layer, grad, grad_spec, grad_o, grad_o_spec, dh)
            d_qkv, part_own, part_oth = attn_back(layer, ds, ds_rcv)
            keep, send, z_keep, z_send = attn_grads(layer, ds, ds_rcv, d_qkv)
            if layer == 1:
                g0, a_small1 = attn_norm(1, ds, part_own, to_core(part_oth))
                grad, grad_spec, grad_o, grad_o_spec = rows5(g0), local, rows5(to_chip(g0)), local
                f_small1 = f_small
            else:
                input_keep, input_send, small = attn_norm(
                    0, ds, part_own, to_core(part_oth), (a_small1, f_small, f_small1)
                )
            ffn = in_dp_order(total(f_keep, to_core(f_send)))
            qv = in_dp_order(total(keep, to_chip(send)))
            ko = jnp.stack([z_keep, z_send], 1).reshape(8, 2, PART, HALF)
            ko = total(ko, to_chip(ko))
            ordered = []
            for mine, far, near, both in (gathered(ffn), gathered(qv)):
                here = jnp.stack([jnp.where(chip == 0, mine, far), jnp.where(chip == 0, far, mine)])
                there = jnp.stack([jnp.where(chip == 0, near, both), jnp.where(chip == 0, both, near)])
                pair = jnp.stack([jnp.where(core == 0, here, there), jnp.where(core == 0, there, here)], 1)
                ordered.append(pair.astype(F32))
            ko_other = to_core(ko)
            ko_all = jnp.stack([jnp.where(core == 0, ko, ko_other), jnp.where(core == 0, ko_other, ko)]).astype(F32)
            f_all, qv_all = ordered
            up = f_all[:, :, :, 0:2].transpose(2, 4, 0, 1, 3, 5).reshape(D, FF)
            down = f_all[:, :, :, 2:4].transpose(2, 1, 3, 4, 0, 5).reshape(FF, D)
            q, v = (qv_all[n].transpose(1, 2, 0, 3).reshape(D, D) for n in range(2))
            k, out = (ko_all[:, :, n].transpose(1, 2, 0, 3).reshape(D, D) for n in range(2))
            grads[layer] = [
                lax.psum_scatter(array, "dp", scatter_dimension=0, tiled=True)
                for array in (up, down, jnp.concatenate([q, k, v], 1), out)
            ]
        ups, downs, qkvs, outs = (jnp.stack(pair) for pair in zip(*grads))
        small = lax.psum(small, ("section", "dp")).reshape(4, 8, D)

        def mine_of(rows):
            width = rows.shape[-1] // replicas
            return lax.dynamic_slice_in_dim(rows, replica * width, width, 1)

        g_a_gain, g_a_shift, g_b_out = (mine_of(small[0:2, n]) for n in range(3))
        g_f_gain, g_f_shift, g_b_down = (mine_of(small[2:4, n]) for n in range(3))
        g_b_up = mine_of(small[2:4, 4:8].reshape(2, FF))

        def placed(keep, got):
            got = got.astype(F32)
            return jnp.stack([jnp.where(chip == 0, keep, got), jnp.where(chip == 0, got, keep)])[:, None]

        final_out, input_out = placed(final_keep, final_got), placed(input_keep, to_chip(input_send))

    return (
        final_out,
        input_out,
        g_a_gain,
        g_a_shift,
        qkvs,
        outs,
        g_b_out,
        g_f_gain,
        g_f_shift,
        ups,
        g_b_up,
        downs,
        g_b_down,
    )


def solution(mesh):
    split = P(None, "dp", None, None)
    placed = (split, P(None, "dp", None)) + (P(),) * 11 + (split,)
    rows = P(None, "dp", "section", None)
    vector, matrix = P(None, "dp"), P(None, "dp", None)
    return jax.shard_map(
        on_device,
        mesh=mesh,
        in_specs=placed,
        out_specs=(
            rows,
            rows,
            vector,
            vector,
            matrix,
            matrix,
            vector,
            vector,
            vector,
            matrix,
            vector,
            matrix,
            vector,
        ),
        check_vma=False,
    )
```

```python
from functools import partial

import jax
import jax.numpy as jnp
from jax import lax
from jax.experimental import pallas as pl
from jax.experimental.pallas import tpu as pltpu
from jax.sharding import PartitionSpec as P

BF = jnp.bfloat16
F32 = jnp.float32
EPS = 1e-05
MASKED = -1e30
D = 768
HALF = 384
PAIR = 128
HEAD_DIM = 64
FF = 3072
LENGTH = 1024
BLOCK = 256
ROWS = 512
PART = 96
GELU_A = 0.7978845608028654
GELU_B = GELU_A * 0.044715


def dot(a, b):
    return jnp.dot(a, b, preferred_element_type=F32)


def dot_nt(a, b):
    return lax.dot_general(a, b, (((1,), (1,)), ((), ())), preferred_element_type=F32)


def dot_tn(a, b):
    return lax.dot_general(a, b, (((0,), (0,)), ((), ())), preferred_element_type=F32)


def normalise(rows):
    center = rows - jnp.mean(rows, -1, keepdims=True)
    spread = lax.rsqrt(jnp.mean(center * center, -1, keepdims=True) + EPS)
    return center * spread, spread


def norm_low(rows, gain, shift):
    unit, _ = normalise(rows.astype(F32))
    return (unit * gain + shift).astype(BF)


def call(body, grid, in_specs, out_specs, out_shape, scratch, cost, deps=(), aliases=None):
    count = len(in_specs)

    def with_deps(sc, *refs):
        return body(sc, *refs[:count], *refs[count + len(deps) :])

    kernel = pl.pallas_call(
        with_deps,
        grid_spec=pltpu.PrefetchScalarGridSpec(
            num_scalar_prefetch=1,
            grid=grid,
            in_specs=list(in_specs) + [pl.BlockSpec(memory_space=pl.ANY)] * len(deps),
            out_specs=out_specs,
            scratch_shapes=scratch,
        ),
        out_shape=out_shape,
        input_output_aliases=aliases or {},
        compiler_params=pltpu.CompilerParams(vmem_limit_bytes=32 * 1024 * 1024),
        cost_estimate=pl.CostEstimate(flops=int(5 * cost[0]), bytes_accessed=int(5 * cost[1]), transcendentals=0),
    )
    return lambda *args: kernel(*args, *deps)


def shape(dims, dtype):
    return jax.ShapeDtypeStruct(dims, dtype)


def stored(dims, dtype):
    return pltpu.MemorySpace.HBM(dims, dtype)


def from_hbm(array):
    return pltpu.with_memory_space_constraint(array, pltpu.MemorySpace.HBM)


def whole(dims):
    count = len(dims)
    return pl.BlockSpec(dims, lambda i, sc: (0,) * count)


def at_layer(dims, layer):
    count = len(dims) - 1
    return pl.BlockSpec(dims, lambda i, sc: (layer,) + (0,) * count)


X, C, Y, Z = 0, 1, 2, 3


def in_order(own, other, block, core):
    return jnp.where(core == block % 2, own[block // 2], other[block // 2])


def weight_copies(layer, core, weights, sides, sems):
    return [
        pltpu.make_async_copy(
            weights.at[layer, :, pl.ds(pl.multiple_of(j * D + core * HALF, PAIR), HALF)],
            sides.at[:, j * HALF : (j + 1) * HALF],
            sems.at[j],
        )
        for j in range(3)
    ]


def episode_columns(ep_ref):
    row = jnp.broadcast_to(ep_ref[...].reshape(1, LENGTH).astype(F32), (PAIR, LENGTH))
    return row, row.T


def first_key(i):
    return max(0, i - 2) * BLOCK


def attn_fwd_body(sc, own, other, ep, gain, shift, wq, wk, wv, qkv, ctx, ctx_own, ctx_oth, lse, bias, vext, lse_cols):
    core = sc[C]
    own, other = own.at[0, :, 0], other.at[0, :, 0]
    for b in range(4):
        rows = slice(b * BLOCK, (b + 1) * BLOCK)
        normed = norm_low(in_order(own, other, b, core), gain[0], shift[0])
        qkv[rows, 0:HALF] = (dot(normed, wq[0]).astype(BF) * 0.125).astype(BF)
        qkv[rows, HALF : 2 * HALF] = dot(normed, wk[0]).astype(BF)
        qkv[rows, 2 * HALF : 3 * HALF] = dot(normed, wv[0]).astype(BF)
    ep_row, ep_col = episode_columns(ep)
    for i in range(4):
        lo, hi = first_key(i), (i + 1) * BLOCK
        key_at = lo + lax.broadcasted_iota(jnp.int32, (BLOCK, hi - lo), 1)
        row_at = i * BLOCK + lax.broadcasted_iota(jnp.int32, (BLOCK, hi - lo), 0)
        same = ep_col[i * BLOCK : hi, 0:1] == ep_row[0:1, lo:hi]
        bias[i, :, 0 : hi - lo] = jnp.where((key_at <= row_at) & same, 0.0, MASKED)
    vext[:, PAIR:] = jnp.ones((LENGTH, PAIR), BF)
    lane = lax.broadcasted_iota(jnp.int32, (BLOCK, PAIR), 1)

    @pl.loop(0, 3)
    def _(p):
        at = pl.multiple_of(p * PAIR, PAIR)
        vext[:, 0:PAIR] = qkv[:, pl.ds(2 * HALF + at, PAIR)]
        for i in range(4):
            lo, hi = first_key(i), (i + 1) * BLOCK
            rows = slice(i * BLOCK, hi)
            q = qkv[rows, pl.ds(at, PAIR)]
            k = qkv[lo:hi, pl.ds(HALF + at, PAIR)]
            outs = []
            for h in range(2):
                mine = (lane >= HEAD_DIM) if h else (lane < HEAD_DIM)
                s = dot_nt(jnp.where(mine, q, jnp.zeros_like(q)), k) + bias[i, :, 0 : hi - lo]
                top = jnp.max(s, -1, keepdims=True)
                prob = jnp.exp(s - top).astype(BF)
                o = dot(prob, vext[lo:hi, :])
                total = o[:, PAIR : PAIR + 1]
                outs.append(o[:, 0:PAIR] / total)
                lse_cols[rows, :] = jnp.where(lane == 2 * p + h, top + jnp.log(total), lse_cols[rows, :])
            ctx[rows, pl.ds(at, PAIR)] = jnp.where(lane < HEAD_DIM, outs[0], outs[1]).astype(BF)

    lse[...] = lse_cols[...].T[0:8]
    for b in range(4):
        piece = ctx[b * BLOCK : (b + 1) * BLOCK]

        @pl.when(core == b % 2)
        def _():
            ctx_own[b // 2] = piece

        @pl.when(core != b % 2)
        def _():
            ctx_oth[b // 2] = piece


def attention_forward(scalars, layer, own, own_spec, other, other_spec, episodes, ep_spec, gain, shift, w_qkv):
    columns = [pl.BlockSpec((1, D, HALF), partial(lambda j, i, sc: (layer, 0, 2 * j + sc[C]), j)) for j in range(3)]
    return call(
        attn_fwd_body,
        (1,),
        [own_spec, other_spec, ep_spec, at_layer((1, 1, D), layer), at_layer((1, 1, D), layer)] + columns,
        [
            whole((LENGTH, 3 * HALF)),
            whole((LENGTH, HALF)),
            whole((2, BLOCK, HALF)),
            whole((2, BLOCK, HALF)),
            whole((8, LENGTH)),
        ],
        [
            stored((LENGTH, 3 * HALF), BF),
            stored((LENGTH, HALF), BF),
            shape((2, BLOCK, HALF), BF),
            shape((2, BLOCK, HALF), BF),
            shape((8, LENGTH), F32),
        ],
        [
            pltpu.VMEM((4, BLOCK, 3 * BLOCK), F32),
            pltpu.VMEM((LENGTH, 2 * PAIR), BF),
            pltpu.VMEM((LENGTH, PAIR), F32),
        ],
        (1.8e9 + 2.4e9, 8e6),
    )(scalars, own, other, episodes, gain, shift, *[from_hbm(w_qkv)] * 3)


def gelu_parts(u):
    cubic = GELU_B * (u * u)
    t = jnp.tanh(u * (GELU_A + cubic))
    half = 0.5 * t + 0.5
    active = u * half
    slope = half + (active * (1.0 - half)) * (6.0 * cubic + 2.0 * GELU_A)
    return active, slope


FT = 1024


def project_body(sc, ctx_own, ctx_rcv, own, w_out, b_out, s2, ctx_full):
    core = sc[C]
    a, b = ctx_own[...].reshape(ROWS, HALF), ctx_rcv[...].reshape(ROWS, HALF)
    both = jnp.concatenate([jnp.where(core == 0, a, b), jnp.where(core == 0, b, a)], 1)
    ctx_full[...] = both
    stream = own[0, :, 0].reshape(ROWS, D).astype(F32) + dot(both, w_out[0]) + b_out[0]
    s2[...] = stream.astype(BF)


def ffn_fwd_body(last, sc, *refs):
    if last:
        s2, gain, shift, w_up, b_up, w_down, b_down, act, slope, keep, send, normed, acc = refs
    else:
        gain, shift, w_up, b_up, w_down, b_down, s2, ctx_full, act, slope, s3, normed, acc = refs[5:]
    t = pl.program_id(0)

    @pl.when(t == 0)
    def _():
        if not last:
            project_body(sc, *refs[:5], s2, ctx_full)
        low = s2[...]
        normed[...] = norm_low(low, gain[0], shift[0])
        acc[...] = low.astype(F32) + b_down[0]

    u = dot(normed[...], w_up[0]) + b_up[0]
    a, d = gelu_parts(u)
    a = a.astype(BF)
    act[...] = a
    slope[...] = d.astype(BF)
    acc[...] += dot(a, w_down[0])

    @pl.when(t == FF // FT - 1)
    def _():
        if last:
            x = sc[X]
            keep[...] = acc[pl.ds(pl.multiple_of(x * BLOCK, BLOCK), BLOCK)]
            send[...] = acc[pl.ds(pl.multiple_of((1 - x) * BLOCK, BLOCK), BLOCK)].astype(BF)
        else:
            s3[...] = acc[...].reshape(2, BLOCK, D).astype(BF)


def ffn_forward(scalars, layer, ctx_own, ctx_rcv, own, own_spec, weights, deps):
    specs, ffn_weight_specs, hidden = projection_specs(layer, own_spec), ffn_specs(layer), hidden_specs()
    w_out, b_out, gain, shift, w_up, b_up, w_down, b_down = weights
    return call(
        partial(ffn_fwd_body, False),
        (FF // FT,),
        specs + ffn_weight_specs,
        [whole((ROWS, D)), whole((ROWS, D))] + hidden + [whole((2, BLOCK, D))],
        [shape((ROWS, D), BF)] * 2 + [stored((ROWS, FF), BF)] * 2 + [shape((2, BLOCK, D), BF)],
        [pltpu.VMEM((ROWS, D), BF), pltpu.VMEM((ROWS, D), F32)],
        (5.4e9, 20e6),
        deps,
    )(scalars, ctx_own, ctx_rcv, own, from_hbm(w_out), b_out, gain, shift, from_hbm(w_up), b_up, from_hbm(w_down), b_down)


def projected(scalars, layer, ctx_own, ctx_rcv, own, own_spec, w_out, b_out, deps):
    return call(
        project_body,
        (1,),
        projection_specs(layer, own_spec),
        [whole((ROWS, D)), whole((ROWS, D))],
        [shape((ROWS, D), BF)] * 2,
        [],
        (6e8, 5e6),
        deps,
    )(scalars, ctx_own, ctx_rcv, own, from_hbm(w_out), b_out)


def last_ffn_forward(scalars, layer, s2, weights):
    gain, shift, w_up, b_up, w_down, b_down = weights
    return call(
        partial(ffn_fwd_body, True),
        (FF // FT,),
        [whole((ROWS, D))] + ffn_specs(layer),
        hidden_specs() + [whole((BLOCK, D)), whole((BLOCK, D))],
        [shape((ROWS, FF), BF)] * 2 + [shape((BLOCK, D), F32), shape((BLOCK, D), BF)],
        [pltpu.VMEM((ROWS, D), BF), pltpu.VMEM((ROWS, D), F32)],
        (4.8e9, 18e6),
    )(scalars, s2, gain, shift, from_hbm(w_up), b_up, from_hbm(w_down), b_down)


def projection_specs(layer, own_spec):
    part = whole((2, BLOCK, HALF))
    return [part, part, own_spec, at_layer((1, D, D), layer), at_layer((1, 1, D), layer)]


def ffn_specs(layer):
    vector = at_layer((1, 1, D), layer)
    return [
        vector,
        vector,
        pl.BlockSpec((1, D, FT), lambda i, sc: (layer, 0, i)),
        pl.BlockSpec((1, 1, FT), lambda i, sc: (layer, 0, i)),
        pl.BlockSpec((1, FT, D), lambda i, sc: (layer, i, 0)),
        vector,
    ]


def hidden_specs():
    return [pl.BlockSpec((ROWS, FT), lambda i, sc: (0, i))] * 2


def norm_back(d_normed, rows, gain):
    unit, spread = normalise(rows)
    d_unit = d_normed * gain
    first = jnp.mean(d_unit, -1, keepdims=True)
    second = jnp.mean(d_unit * unit, -1, keepdims=True)
    d_rows = spread * (d_unit - first - unit * second)
    return d_rows, jnp.sum(d_normed * unit, 0, keepdims=True), jnp.sum(d_normed, 0, keepdims=True)


def small_rows(*vectors):
    return jnp.concatenate(vectors + (jnp.zeros((8 - len(vectors), D), F32),))


def attn_norm_body(last, sc, grad, part, part_rcv, own, gain, *rest):
    before, outs = rest[:3] if last else (), rest[3:] if last else rest
    grad_rows = grad[...].reshape(ROWS, D).astype(F32)
    d_normed = part[...].reshape(ROWS, D) + part_rcv[...].reshape(ROWS, D).astype(F32)
    d_rows, g_gain, g_shift = norm_back(d_normed, own[0, :, 0].reshape(ROWS, D).astype(F32), gain[0])
    total = grad_rows + d_rows
    small = outs[-1]
    small[0:8] = small_rows(g_gain, g_shift, jnp.sum(grad_rows, 0, keepdims=True))
    for j, ref in enumerate(before):
        small[8 * (j + 1) : 8 * (j + 2)] = ref[...]
    if last:
        keep, send = outs[0:2]
        keep[...] = jnp.where(sc[X] == 0, total[0:BLOCK], total[BLOCK:ROWS])
        send[...] = jnp.where(sc[X] == 0, total[BLOCK:ROWS], total[0:BLOCK]).astype(BF)
    else:
        outs[0][...] = total.astype(BF).reshape(2, BLOCK, D)


def attention_norm_back(scalars, layer, grad, part, part_rcv, own, own_spec, gain, smalls=(), deps=()):
    block = whole((2, BLOCK, D))
    last = bool(smalls)
    if last:
        out_specs = [whole((BLOCK, D)), whole((BLOCK, D))]
        out_shape = [shape((BLOCK, D), F32), shape((BLOCK, D), BF)]
    else:
        out_specs, out_shape = [block], [shape((2, BLOCK, D), BF)]
    rows = 8 * (1 + len(smalls))
    return call(
        partial(attn_norm_body, last),
        (1,),
        [block, block, block, own_spec, at_layer((1, 1, D), layer)] + [whole((8, D))] * len(smalls),
        out_specs + [whole((rows, D))],
        out_shape + [shape((rows, D), F32)],
        [],
        (2e8, 5e6),
        deps,
    )(scalars, grad, part, part_rcv, own, gain, *smalls)


BT = 768
AT = 1536


def ffn_back_body(sc, grad, s2, gain, w_up, w_down, slope, dh, ds, small, acc):
    t = pl.program_id(0)
    low = grad[0, :, 0].reshape(ROWS, D)
    d_act = dot_nt(low, w_down[0])
    d_hidden = d_act * slope[...].astype(F32)
    d_low = d_hidden.astype(BF)
    dh[...] = d_low
    sums = jnp.sum(d_low.astype(F32), 0, keepdims=True)
    for j in range(2):
        small[pl.ds(4 + 2 * t + j, 1)] = sums[:, j * D : (j + 1) * D]
    part = dot_nt(d_low, w_up[0])

    @pl.when(t == 0)
    def _():
        acc[...] = part

    @pl.when(t > 0)
    def _():
        acc[...] += part

    @pl.when(t == FF // AT - 1)
    def _():
        rows = low.astype(F32)
        d_rows, g_gain, g_shift = norm_back(acc[...], s2[...].astype(F32), gain[0])
        ds[...] = (rows + d_rows).astype(BF).reshape(2, BLOCK, D)
        small[0:4] = small_rows(g_gain, g_shift, jnp.sum(rows, 0, keepdims=True))[0:4]


def ffn_backward(scalars, layer, grad, grad_spec, s2, slope, weights, deps=()):
    gain, w_up, w_down = weights
    return call(
        ffn_back_body,
        (FF // AT,),
        [
            grad_spec,
            whole((ROWS, D)),
            at_layer((1, 1, D), layer),
            pl.BlockSpec((1, D, AT), lambda i, sc: (layer, 0, i)),
            pl.BlockSpec((1, AT, D), lambda i, sc: (layer, i, 0)),
            pl.BlockSpec((ROWS, AT), lambda i, sc: (0, i)),
        ],
        [
            pl.BlockSpec((ROWS, AT), lambda i, sc: (0, i)),
            whole((2, BLOCK, D)),
            whole((8, D)),
        ],
        [shape((ROWS, FF), BF), shape((2, BLOCK, D), BF), shape((8, D), F32)],
        [pltpu.VMEM((ROWS, D), F32)],
        (4.9e9, 18e6),
        deps,
    )(scalars, grad, s2, gain, from_hbm(w_up), from_hbm(w_down), (slope if layer == 1 else from_hbm(slope)))


def place(sc, piece):
    return (piece % 2) ^ sc[Y], (piece // 2) ^ sc[Z]


def ffn_weight_body(
    sc, grad, grad_o, s2, s2_o, gain, shift, act, dh, w_up, b_up, w_down, keep, send, n_t, n_o, g_t, acts, dhs
):
    t = pl.program_id(0)
    core = sc[C]
    low, low_o = grad[0, :, 0].reshape(ROWS, D), grad_o[0, :, 0].reshape(ROWS, D)

    @pl.when(t == 0)
    def _():
        n_t[:, 0:ROWS] = norm_low(s2[...], gain[0], shift[0]).T
        other = norm_low(s2_o[...], gain[0], shift[0])
        n_o[...] = other
        n_t[:, ROWS : 2 * ROWS] = other.T
        x = sc[X]
        g_t[:, 0:ROWS] = jnp.where(x == 0, low[:, 0:HALF], low[:, HALF:D]).T
        g_t[:, ROWS : 2 * ROWS] = jnp.where(x == 0, low_o[:, 0:HALF], low_o[:, HALF:D]).T

    u = dot(n_o[...], w_up[0]) + b_up[0]
    acts[0:ROWS] = act[...]

    @pl.when(t < 2)
    def _():
        active_o, slope_o = gelu_parts(u)
        acts[ROWS : 2 * ROWS] = active_o.astype(BF)
        dhs[0:ROWS] = dh[...]
        dhs[ROWS : 2 * ROWS] = (dot_nt(low_o, w_down[0]) * slope_o).astype(BF)
        g_up = dot(n_t[...], dhs[...]).astype(BF)
        for ref, when in ((send, 0), (keep, 1)):

            @pl.when(t == when)
            def _():
                for piece in range(8):
                    py, pz = place(sc, piece)
                    for j in range(2):
                        ref[py, pz, j] = g_up[piece * PART : (piece + 1) * PART, j * HALF : (j + 1) * HALF]

    @pl.when(t >= 2)
    def _():
        acts[ROWS : 2 * ROWS] = gelu_parts(u)[0].astype(BF)

    g_down = dot(g_t[...], acts[...]).astype(BF).T
    tile = ffn_tile(t, sc)
    for half in range(2):
        py, pz = place(sc, 2 * tile + half)
        for j in range(2):
            first = g_down[half * HALF + j * PART : half * HALF + (j + 1) * PART]
            second = g_down[half * HALF + (j + 2) * PART : half * HALF + (j + 3) * PART]
            keep[py, pz, 2 + j] = jnp.where(core == 0, first, second)
            send[py, pz, 2 + j] = jnp.where(core == 0, second, first)


def ffn_tile(step, sc):
    mine = 2 * sc[X]
    rest = 2 - mine
    return jnp.where(step == 0, mine + 1 - sc[C], jnp.where(step == 1, mine + sc[C], rest + step - 2))


def ffn_weights(scalars, layer, grad, grad_spec, grad_o, grad_o_spec, s2, s2_o, act, dh, weights, deps=()):
    gain, shift, w_up, b_up, w_down = weights
    packed = (2, 4, 4, PART, HALF)
    return call(
        ffn_weight_body,
        (FF // BT,),
        [
            grad_spec,
            grad_o_spec,
            whole((ROWS, D)),
            whole((ROWS, D)),
            at_layer((1, 1, D), layer),
            at_layer((1, 1, D), layer),
            pl.BlockSpec((ROWS, BT), lambda i, sc: (0, ffn_tile(i, sc))),
            pl.BlockSpec((ROWS, BT), lambda i, sc: (0, ffn_tile(jnp.minimum(i, 1), sc))),
            pl.BlockSpec((1, D, BT), lambda i, sc: (layer, 0, ffn_tile(i, sc))),
            pl.BlockSpec((1, 1, BT), lambda i, sc: (layer, 0, ffn_tile(i, sc))),
            pl.BlockSpec((1, BT, D), lambda i, sc: (layer, ffn_tile(jnp.minimum(i, 1), sc), 0)),
        ],
        [whole(packed), whole(packed)],
        [stored(packed, BF), shape(packed, BF)],
        [
            pltpu.VMEM((D, 2 * ROWS), BF),
            pltpu.VMEM((ROWS, D), BF),
            pltpu.VMEM((HALF, 2 * ROWS), BF),
            pltpu.VMEM((2 * ROWS, BT), BF),
            pltpu.VMEM((2 * ROWS, BT), BF),
        ],
        (8.6e9, 22e6),
        deps,
    )(scalars, grad, grad_o, s2, s2_o, gain, shift, (act if layer == 1 else from_hbm(act)), dh, from_hbm(w_up), b_up, from_hbm(w_down))


def attn_back_body(
    layer, sc, gr_own, gr_rcv, qkv, ctx, lse, ep, w_out, weights, d_qkv, part_own, part_oth, bias, d_ctx, delta, d_k, d_v,
    sides, sems
):
    core = sc[C]
    copies = weight_copies(layer, core, weights, sides, sems)
    for copy in copies:
        copy.start()
    for b in range(4):
        rows = slice(b * BLOCK, (b + 1) * BLOCK)
        d_ctx[rows] = dot_nt(in_order(gr_own, gr_rcv, b, core), w_out[0]).astype(BF)
    product = d_ctx[...].astype(F32) * ctx[...].astype(F32)
    high = product.astype(BF)
    rest = (product - high.astype(F32)).astype(BF)
    picks = (
        lax.broadcasted_iota(jnp.int32, (8, HALF), 0) == lax.broadcasted_iota(jnp.int32, (8, HALF), 1) // HEAD_DIM
    ).astype(BF)
    delta[...] = dot_nt(picks, high) + dot_nt(picks, rest)
    ep_row, ep_col = episode_columns(ep)
    for i in range(4):
        lo, hi = first_key(i), (i + 1) * BLOCK
        key_at = lo + lax.broadcasted_iota(jnp.int32, (hi - lo, BLOCK), 0)
        row_at = i * BLOCK + lax.broadcasted_iota(jnp.int32, (hi - lo, BLOCK), 1)
        same = ep_col[lo:hi, 0:1] == ep_row[0:1, i * BLOCK : hi]
        bias[i, 0 : hi - lo, :] = jnp.where((key_at <= row_at) & same, 0.0, MASKED)

    @pl.loop(0, 3)
    def _(p):
        at = pl.multiple_of(p * PAIR, PAIR)
        d_k[...] = jnp.zeros_like(d_k)
        d_v[...] = jnp.zeros_like(d_v)
        for i in range(4):
            lo, hi = first_key(i), (i + 1) * BLOCK
            rows = slice(i * BLOCK, hi)
            q = qkv[rows, pl.ds(at, PAIR)]
            k = qkv[lo:hi, pl.ds(HALF + at, PAIR)]
            v = qkv[lo:hi, pl.ds(2 * HALF + at, PAIR)]
            dc = d_ctx[rows, pl.ds(at, PAIR)]
            d_q = jnp.zeros((BLOCK, PAIR), F32)
            for h in range(2):

                def only(array):
                    lane = lax.broadcasted_iota(jnp.int32, array.shape, 1)
                    mine = (lane >= HEAD_DIM) if h else (lane < HEAD_DIM)
                    return jnp.where(mine, array, jnp.zeros_like(array))

                q_h, dc_h = only(q), only(dc)
                s = dot_nt(k, q_h) + bias[i, 0 : hi - lo, :]
                prob = jnp.exp(s - lse[pl.ds(2 * p + h, 1), rows])
                d_p = dot_nt(v, dc_h)
                d_s = (prob * (d_p - delta[pl.ds(2 * p + h, 1), rows])).astype(BF)
                d_v[lo:hi] += dot(prob.astype(BF), dc_h)
                d_k[lo:hi] += dot(d_s, q_h)
                d_q += dot_tn(d_s, only(k))
            d_qkv[rows, pl.ds(at, PAIR)] = (d_q * 0.125).astype(BF)
        d_qkv[:, pl.ds(HALF + at, PAIR)] = d_k[...].astype(BF)
        d_qkv[:, pl.ds(2 * HALF + at, PAIR)] = d_v[...].astype(BF)

    for copy in copies:
        copy.wait()
    for b in range(4):
        rows = slice(b * BLOCK, (b + 1) * BLOCK)
        part = dot_nt(d_qkv[rows], sides[...])

        @pl.when(core == b % 2)
        def _():
            part_own[b // 2] = part

        @pl.when(core != b % 2)
        def _():
            part_oth[b // 2] = part.astype(BF)


def attention_backward(scalars, layer, gr_own, gr_rcv, qkv, ctx, lse, episodes, ep_spec, w_out, w_qkv, deps=()):
    block = whole((2, BLOCK, D))
    return call(
        partial(attn_back_body, layer),
        (1,),
        [
            block,
            block,
            whole((LENGTH, 3 * HALF)),
            whole((LENGTH, HALF)),
            whole((8, LENGTH)),
            ep_spec,
            pl.BlockSpec((1, HALF, D), lambda i, sc: (layer, sc[C], 0)),
            pl.BlockSpec(memory_space=pl.ANY),
        ],
        [whole((LENGTH, 3 * HALF)), block, block],
        [shape((LENGTH, 3 * HALF), BF), shape((2, BLOCK, D), F32), shape((2, BLOCK, D), BF)],
        [
            pltpu.VMEM((4, 3 * BLOCK, BLOCK), F32),
            pltpu.VMEM((LENGTH, HALF), BF),
            pltpu.VMEM((8, LENGTH), F32),
            pltpu.VMEM((LENGTH, PAIR), F32),
            pltpu.VMEM((LENGTH, PAIR), F32),
            pltpu.VMEM((D, 3 * HALF), BF),
            pltpu.SemaphoreType.DMA((3,)),
        ],
        (2.5e9 + 6e9, 12e6),
        deps,
    )(scalars, gr_own, gr_rcv, from_hbm(qkv), from_hbm(ctx), lse, episodes, from_hbm(w_out), from_hbm(w_qkv))


def attn_weight_body(
    z_first, sc, own, other, gain, shift, d_qkv, gr_own, gr_rcv, ctx_full, ctx_oth, ctx_rcv, keep, send, z_keep, z_send, n_t
):
    core, x = sc[C], sc[X]
    own, other = own.at[0, :, 0], other.at[0, :, 0]
    for b in range(4):
        rows = slice(b * BLOCK, (b + 1) * BLOCK)
        n_t[:, rows] = norm_low(in_order(own, other, b, core), gain[0], shift[0]).T

    def columns(ref):
        rows = ref[...].reshape(ROWS, D)
        return jnp.where(core == 0, rows[:, 0:HALF], rows[:, HALF:D]).T

    def grad(j):
        return dot(n_t[...], d_qkv[:, j * HALF : (j + 1) * HALF]).astype(BF)

    first, second = grad(0), grad(2)
    mine, yours = jnp.where(x == 0, first, second), jnp.where(x == 0, second, first)
    for piece in range(8):
        py, pz = place(sc, piece)
        keep[py, pz] = mine[piece * PART : (piece + 1) * PART]
        send[py, pz] = yours[piece * PART : (piece + 1) * PART]

    a, b = ctx_oth[...].reshape(ROWS, HALF), ctx_rcv[...].reshape(ROWS, HALF)
    far = jnp.concatenate([jnp.where(core == 0, a, b), jnp.where(core == 0, b, a)], 1)
    g_out = (dot(columns(gr_own), ctx_full[...]) + dot(columns(gr_rcv), far)).astype(BF).T
    for j, rows in enumerate((grad(1), g_out)):
        for piece in range(8):
            py, pz = place(sc, piece)
            value = rows[piece * PART : (piece + 1) * PART]

            far = pz % 2 if z_first else py

            @pl.when(far == 0)
            def _():
                if z_first:
                    z_keep[pz // 2, py, j] = value
                else:
                    z_keep[pz, j] = value

            @pl.when(far == 1)
            def _():
                if z_first:
                    z_send[pz // 2, py, j] = value
                else:
                    z_send[pz, j] = value


def attention_weights(
    scalars, layer, own, own_spec, other, other_spec, gain, shift, d_qkv, gr_own, gr_rcv, ctx_full, ctx_oth, ctx_rcv, deps=()
):
    z_first = layer == 1
    packed, z_packed = (2, 4, PART, HALF), ((2, 2) if z_first else (4,)) + (2, PART, HALF)
    block = whole((2, BLOCK, D))
    return call(
        partial(attn_weight_body, z_first),
        (1,),
        [
            own_spec,
            other_spec,
            at_layer((1, 1, D), layer),
            at_layer((1, 1, D), layer),
            whole((LENGTH, 3 * HALF)),
            block,
            block,
            whole((ROWS, D)),
            whole((2, BLOCK, HALF)),
            whole((2, BLOCK, HALF)),
        ],
        [whole(packed), whole(packed), whole(z_packed), whole(z_packed)],
        [stored(packed, BF), shape(packed, BF), stored(z_packed, BF), shape(z_packed, BF)],
        [pltpu.VMEM((D, LENGTH), BF)],
        (2.5e9, 12e6),
        deps,
    )(scalars, own, other, gain, shift, d_qkv, gr_own, gr_rcv, ctx_full, ctx_oth, ctx_rcv)


def to_core(value):
    return lax.ppermute(value, "section", [(0, 1), (1, 0), (2, 3), (3, 2)])


def to_chip(value):
    return lax.ppermute(value, "section", [(0, 2), (2, 0), (1, 3), (3, 1)])


def to_dp(value, distance):
    return lax.ppermute(value, "dp", [(i, i ^ distance) for i in range(8)])


def total(*terms):
    out = terms[0].astype(F32)
    for term in terms[1:]:
        out = out + term.astype(F32)
    return out.astype(BF)


class Flat(list):
    pass


def combined(scalars, outputs, deps=(), pinned=()):
    terms, dims, dtypes = [], [], []

    def block_of(term):
        array, *index = term
        if index and isinstance(index[0], slice):
            count = index[0].stop - index[0].start
            return (count,) + array.shape[1:], (index[0].start // count,) + (0,) * (array.ndim - 1)
        rest = array.shape[len(index) :]
        return (None,) * len(index) + rest, tuple(index) + (0,) * len(rest)

    def dims_of(term):
        return tuple(d for d in block_of(term)[0] if d is not None)

    def rows_of(piece):
        found = dims_of(piece[0])
        return found[0] if len(found) == 3 else 1

    for pieces in outputs:
        rest = dims_of(pieces[0][0])
        if isinstance(pieces, Flat):
            dims.append((sum(rows_of(piece) for piece in pieces),) + rest[-2:])
        else:
            dims.append(((len(pieces),) if len(pieces) > 1 else ()) + rest)
        dtypes.append(pieces[0][0][0].dtype)
        terms += [term for piece in pieces for term in piece]

    def spec(term):
        block, index = block_of(term)
        return pl.BlockSpec(block, lambda i, sc: index)

    def body(sc, *refs):
        given = iter(refs[: len(terms)])
        for out, pieces in zip(refs[len(terms) :], outputs):
            at = 0
            for n, piece in enumerate(pieces):
                value = next(given)[...].astype(F32)
                for _ in piece[1:]:
                    value = value + next(given)[...].astype(F32)
                value = value.astype(out.dtype)
                if isinstance(pieces, Flat):
                    rows = rows_of(piece)
                    if len(value.shape) == 3:
                        out[at : at + rows] = value
                    else:
                        out[at] = value
                    at += rows
                elif len(pieces) > 1:
                    out[n] = value
                else:
                    out[...] = value

    return call(
        body,
        (1,),
        [spec(term) for term in terms],
        [whole(d) for d in dims],
        [shape(d, t) for d, t in zip(dims, dtypes)],
        [],
        (1e10, 1e7),
        deps,
    )(scalars, *[from_hbm(term[0]) if any(term[0] is a for a in pinned) else term[0] for term in terms])


def in_dp_order(both):
    return jnp.moveaxis(both, 0, 1).reshape((8,) + both.shape[2:])


def gathered(share):
    far, near = to_chip(share), to_core(share)
    return share, far, near, to_core(far)


def ffn_unpacked(sc, shares, up, down):
    for n in range(4):
        x, core = sc[X] ^ (n % 2), sc[C] ^ (n // 2)
        for j in range(2):
            at = pl.multiple_of(x * 4 * HALF + core * 2 * HALF + j * HALF, PAIR)
            up[0, :, pl.ds(at, HALF)] = shares[n][j].astype(F32)
            rows = pl.ds(pl.multiple_of(core * 2 * PART + j * PART, 8), PART)
            down[0, rows, pl.ds(pl.multiple_of(x * HALF, PAIR), HALF)] = shares[n][2 + j].astype(F32)


def unpack_early_body(sc, final_keep, final_got, input_keep, input_got, *refs):
    final, inputs, up, down = refs[-4:]
    x = sc[X]
    for ref, mine, got in ((final, final_keep, final_got), (inputs, input_keep, input_got)):
        ref[x, 0] = mine[...]
        ref[1 - x, 0] = got[...].astype(F32)
    ffn_unpacked(sc, refs[:4], up, down)


def unpack_body(shares, sc, small, up_before, down_before, *refs):
    up, down, qkv, out, a_gain, a_shift, b_out, f_gain, f_shift, b_down, b_up = refs[-11:]
    ffn_unpacked(sc, refs[:4], up, down)
    for layer in range(2):
        qv, ko = shares[layer]
        for n in range(4):
            x, core = sc[X] ^ (n % 2), sc[C] ^ (n // 2)
            index, at = qv[n]
            qkv[layer, :, pl.ds(pl.multiple_of(x * 2 * D + core * HALF, PAIR), HALF)] = refs[index][at].astype(F32)
        for n in range(2):
            side = pl.multiple_of((sc[C] ^ n) * HALF, PAIR)
            qkv[layer, :, pl.ds(pl.multiple_of(D + side, PAIR), HALF)] = refs[ko[n]][0].astype(F32)
            out[layer, :, pl.ds(side, HALF)] = refs[ko[n]][1].astype(F32)
    piece = 2 * sc[Z] + sc[Y]
    mine = jnp.zeros((32, PART), F32)
    for d in range(8):
        mine = jnp.where(piece == d, small[:, d * PART : (d + 1) * PART], mine)
    for layer in range(2):
        for j, (a_ref, f_ref) in enumerate(((a_gain, f_gain), (a_shift, f_shift), (b_out, b_down))):
            a_ref[layer : layer + 1] = mine[8 * layer + j : 8 * layer + j + 1]
            f_ref[layer : layer + 1] = mine[16 + 8 * layer + j : 16 + 8 * layer + j + 1]
        row = jnp.zeros((1, 4 * PART), F32)
        for d in range(8):
            at = 16 + 8 * layer + 4 + d // 2
            row = jnp.where(piece == d, small[at : at + 1, (d % 2) * HALF : (d % 2 + 1) * HALF], row)
        b_up[layer : layer + 1] = row


FFN_GRADS = ((2, PART, FF), (2, 4 * PART, D))


def unpacked_early(scalars, rows, arrays, layer):
    moved = ((2, 1, BLOCK, D),) * 2
    return call(
        unpack_early_body,
        (1,),
        [whole((BLOCK, D))] * 4 + [whole(array.shape) for array in arrays],
        [whole(d) for d in moved] + [at_layer((1,) + d[1:], layer) for d in FFN_GRADS],
        [shape(d, F32) for d in moved] + [stored(d, F32) for d in FFN_GRADS],
        [],
        (1e6, 9e6),
    )(scalars, *rows, *arrays)


def unpacked(scalars, small, up, down, arrays, shares):
    dims = ((2, PART, 3 * D), (2, PART, D)) + ((2, PART),) * 6 + ((2, 4 * PART),)
    held = pl.BlockSpec(memory_space=pl.ANY)
    return call(
        partial(unpack_body, shares),
        (1,),
        [whole((32, D)), held, held] + [whole(array.shape) for array in arrays],
        [at_layer((1,) + d[1:], 0) for d in FFN_GRADS] + [whole(d) for d in dims],
        [stored(d, F32) for d in FFN_GRADS] + [shape(d, F32) for d in dims],
        [],
        (1e6, 11e6),
        aliases={2: 0, 3: 1},
    )(scalars, small, from_hbm(up), from_hbm(down), *arrays)


def on_device(
    tokens,
    episodes,
    attn_gain,
    attn_shift,
    qkv_weight,
    out_weight,
    out_bias,
    ffn_gain,
    ffn_shift,
    up_weight,
    up_bias,
    down_weight,
    down_bias,
    cotangent,
):
    replicas = lax.axis_size("dp")
    section = lax.axis_index("section")
    replica = lax.axis_index("dp")
    chip, core = section // 2, section % 2
    direct = replicas == 8
    y, z = (replica % 2, replica // 2) if direct else (0, 0)
    scalars = jnp.stack([jnp.asarray(v, jnp.int32) for v in (chip, core, y, z)])

    stream = tokens.reshape(2, 2, 2, BLOCK, D)
    cot = cotangent.reshape(2, 2, 2, BLOCK, D)
    eps = episodes.reshape(2, 1, LENGTH)
    ep_spec = pl.BlockSpec((1, 1, LENGTH), lambda i, sc: (sc[X], 0, 0))

    def input_spec(micro, side):
        return pl.BlockSpec((1, 2, 1, BLOCK, D), lambda i, sc: (micro(sc[X]), 0, side(sc[C]), 0, 0))

    same, flip = (lambda v: v), (lambda v: 1 - v)
    own_in, other_in, far_in = input_spec(same, same), input_spec(same, flip), input_spec(flip, same)
    local = pl.BlockSpec((1, 2, 1, BLOCK, D), lambda i, sc: (0, 0, 0, 0, 0))

    def rows5(value):
        return value.reshape(1, 2, 1, BLOCK, D)

    def vec(array):
        return array.reshape(2, 1, -1)

    a_gain, a_shift, b_out = vec(attn_gain), vec(attn_shift), vec(out_bias)
    f_gain, f_shift, b_up, b_down = vec(ffn_gain), vec(ffn_shift), vec(up_bias), vec(down_bias)

    kept = []
    own, own_spec, other, other_spec = stream, own_in, stream, other_in
    for layer in range(2):
        seen = (own, own_spec, other, other_spec)
        if layer == 0:
            seen = (from_hbm(own), own_spec, from_hbm(other), other_spec)
        qkv, ctx, ctx_own, ctx_oth, lse = attention_forward(
            scalars, layer, *seen, eps, ep_spec, a_gain, a_shift, qkv_weight
        )
        ctx_rcv = to_core(ctx_oth)
        ctx_far = to_core(ctx_own)
        ffn = (f_gain, f_shift, up_weight, b_up, down_weight, b_down)
        if layer == 0:
            s2, ctx_full, act, slope, *result = ffn_forward(
                scalars, layer, ctx_own, ctx_rcv, own, own_spec, (out_weight, b_out) + ffn, ()
            )
            s2_o = to_chip(s2)
        else:
            s2, ctx_full = projected(
                scalars, layer, ctx_own, ctx_rcv, own, own_spec, out_weight, b_out, (kept[0][7], kept[0][11])
            )
            s2_o = to_chip(s2)
            act, slope, *result = last_ffn_forward(scalars, layer, s2, ffn)
        kept.append((own, own_spec, other, other_spec, qkv, ctx, ctx_oth, ctx_far, ctx_full, lse, s2, s2_o, act, slope))
        if layer == 0:
            s3 = result[0]
            own, own_spec, other, other_spec = rows5(s3), local, rows5(to_core(s3)), local
    final_keep, final_send = result

    def ffn_back(layer, grad, grad_spec, deps=()):
        kept_now = kept[layer]
        s2, slope = kept_now[10], kept_now[13]
        return ffn_backward(scalars, layer, grad, grad_spec, s2, slope, (f_gain, up_weight, down_weight), deps)

    def ffn_grads(layer, grad, grad_spec, grad_o, grad_o_spec, dh, deps=()):
        s2, s2_o, act, slope = kept[layer][10:]
        weights = (f_gain, f_shift, up_weight, b_up, down_weight)
        return ffn_weights(
            scalars, layer, grad, grad_spec, grad_o, grad_o_spec, s2, s2_o, act, dh, weights, deps
        )

    def attn_back(layer, ds, ds_rcv, deps=()):
        own, own_spec, other, other_spec, qkv, ctx, ctx_oth, ctx_far, ctx_full, lse = kept[layer][:10]
        return attention_backward(
            scalars, layer, ds, ds_rcv, qkv, ctx, lse, eps, ep_spec, out_weight, qkv_weight, deps
        )

    def attn_grads(layer, ds, ds_rcv, d_qkv, deps=()):
        own, own_spec, other, other_spec, qkv, ctx, ctx_oth, ctx_far, ctx_full, lse = kept[layer][:10]
        return attention_weights(
            scalars, layer, own, own_spec, other, other_spec, a_gain, a_shift, d_qkv, ds, ds_rcv, ctx_full, ctx_oth,
            ctx_far, deps,
        )

    def attn_norm(layer, ds, part_own, part_rcv, smalls=(), deps=()):
        own, own_spec = kept[layer][:2]
        return attention_norm_back(scalars, layer, ds, part_own, part_rcv, own, own_spec, a_gain, smalls, deps)

    if direct:
        pinned = []

        def summed(*outputs, deps=()):
            return combined(scalars, outputs, deps, pinned)

        def y_sum(keep, got):
            return [[(keep, 1), (got, 1)]]

        def z_sum(keep, got, y_got):
            return [[(keep, 0, k), (got, 0, k), (y_got, k)] for k in (1, 3)]

        def far_sum(keep, got, y_got, z_got):
            return [[(keep, 0, 2), (got, 0, 2), (y_got, 2), (z_got, 1)]]

        def share(keep, got, y_got, z_got, far_got):
            return [[(keep, 0, 0), (got, 0, 0), (y_got, 0), (z_got, 0), (far_got,)]]

        dh1, ds1, f_small1 = ffn_back(1, cot, own_in, [kept[1][7]])
        ds1_rcv = to_core(ds1)
        fk1, send = ffn_grads(1, cot, own_in, cot, far_in, dh1)
        pinned.append(fk1)
        fg1 = to_core(send)
        d_qkv1, part1, part1_oth = attn_back(1, ds1, ds1_rcv, [from_hbm(fk1)])
        part1_rcv = to_core(part1_oth)
        value, final_low = summed(y_sum(fk1, fg1), [[(final_send,)]], deps=[part1])
        fy1 = to_dp(value, 1)
        g0, a_small1 = attn_norm(1, ds1, part1, part1_rcv, deps=[value])
        g0_o = to_chip(g0)
        dh0, ds0, f_small0 = ffn_back(0, rows5(g0), local)
        ds0_rcv = to_core(ds0)
        qk1, send, ok1, z_send = attn_grads(1, ds1, ds1_rcv, d_qkv1, [ds0])
        pinned += [qk1, ok1]
        qg1, og1 = to_chip(send), to_dp(z_send, 2)
        fk0, send = ffn_grads(0, rows5(g0), local, rows5(g0_o), local, dh0, [from_hbm(qk1)])
        pinned.append(fk0)
        fg0 = to_core(send)
        (fz1,) = summed(z_sum(fk1, fg1, fy1), deps=[from_hbm(fk0)])
        fy0, final_low = summed(y_sum(fk0, fg0), [[(final_low,)]], deps=[fz1])
        d_qkv0, part0, part0_oth = attn_back(0, ds0, ds0_rcv, [fy0])
        final_got = to_chip(final_low)
        fz1, fy0 = to_dp(fz1, 2), to_dp(fy0, 1)
        part0_rcv = to_core(part0_oth)
        far1, y1 = summed(
            far_sum(fk1, fg1, fy1, fz1),
            Flat([[(ok1, 0, 1), (og1, 0, 1)], [(ok1, 1, 1), (og1, 1, 1)]] + y_sum(qk1, qg1)),
            deps=[part0],
        )
        input_keep, input_send, small = attn_norm(
            0, ds0, part0, part0_rcv, (a_small1, f_small0, f_small1), [far1, final_got]
        )
        far1, y1 = to_dp(far1, 4), to_dp(y1, 1)
        small_got = to_core(small)
        input_got = to_chip(input_send)
        fz0, small = summed(z_sum(fk0, fg0, fy0), [[(small,), (small_got,)]], deps=[input_keep])
        qk0, send, ok0, y_send = attn_grads(0, ds0, ds0_rcv, d_qkv0, [fz0])
        fz0, small_got = to_dp(fz0, 2), to_dp(small, 4)
        pinned += [qk0, ok0]
        qg0, oy0 = to_chip(send), to_dp(y_send, 1)

        far, qz1, f1, small = summed(
            Flat(far_sum(fk0, fg0, fy0, fz0) + [[(ok1, 1, 0), (og1, 1, 0), (y1, slice(2, 4))]]),
            [[(qk1, 0, k), (qg1, 0, k), (y1, 4 + k)] for k in (1, 3)],
            share(fk1, fg1, fy1, fz1, far1),
            [[(small,), (small_got,)]],
            deps=[from_hbm(qk0)],
        )
        far, qz1, small_got = to_dp(far, 4), to_dp(qz1, 2), to_dp(small, 1)
        f1_all = gathered(f1)

        qy0, oz0, qf1, small = summed(
            y_sum(qk0, qg0),
            [[(ok0, k), (oy0, k)] for k in (1, 3)],
            [[(qk1, 0, 2), (qg1, 0, 2), (y1, 6), (qz1, 1)]],
            [[(small,), (small_got,)]],
            deps=[input_got],
        )
        qy0, oz0, qf1, small_got = to_dp(qy0, 1), to_dp(oz0, 2), to_dp(qf1, 4), to_chip(small)

        of0, qz0, f0, ox1, small = summed(
            [[(ok0, 2), (oy0, 2), (oz0, 1)]],
            z_sum(qk0, qg0, qy0),
            [[(fk0, 0, 0), (fg0, 0, 0), (fy0, 0), (fz0, 0), (far, slice(0, 4))]],
            [[(ok1, 0, 0), (og1, 0, 0), (y1, slice(0, 2)), (far, slice(4, 6))]],
            [[(small,), (small_got,)]],
            deps=f1_all[1:],
        )
        of0, qz0, ox1_got, small_got = to_dp(of0, 4), to_dp(qz0, 2), to_chip(ox1), to_dp(small, 2)
        f0_all = gathered(f0)

        qf0, ox0, o1, small = summed(
            far_sum(qk0, qg0, qy0, qz0),
            [[(ok0, 0), (oy0, 0), (oz0, 0), (of0,)]],
            [[(ox1,), (ox1_got,)]],
            [[(small,), (small_got,)]],
        )
        qf0, ox0_got = to_dp(qf0, 4), to_chip(ox0)

        final_out, input_out, ups, downs = unpacked_early(
            scalars, (final_keep, final_got, input_keep, input_got), f1_all, 1
        )
        both, o0 = summed(
            share(qk0, qg0, qy0, qz0, qf0) + [[(qk1, 0, 0), (qg1, 0, 0), (y1, 4), (qz1, 0), (qf1,)]],
            [[(ox0,), (ox0_got,)]],
            deps=f0_all[1:] + (from_hbm(ups),),
        )
        arrays = f0_all + gathered(both) + (o0, to_core(o0), o1, to_core(o1))
        shares = ((tuple((n, 0) for n in range(4, 8)), (8, 9)), (tuple((n, 1) for n in range(4, 8)), (10, 11)))
        (ups, downs, qkvs, outs, *vectors) = unpacked(scalars, small, ups, downs, arrays, shares)
        g_a_gain, g_a_shift, g_b_out, g_f_gain, g_f_shift, g_b_down, g_b_up = vectors
    else:
        final_got = to_chip(final_send)
        grads = [None, None]
        grad, grad_spec, grad_o, grad_o_spec = cot, own_in, cot, far_in
        for layer in (1, 0):
            dh, ds, f_small = ffn_back(layer, grad, grad_spec)
            ds_rcv = to_core(ds)
            f_keep, f_send = ffn_grads(layer, grad, grad_spec, grad_o, grad_o_spec, dh)
            d_qkv, part_own, part_oth = attn_back(layer, ds, ds_rcv)
            keep, send, z_keep, z_send = attn_grads(layer, ds, ds_rcv, d_qkv)
            if layer == 1:
                g0, a_small1 = attn_norm(1, ds, part_own, to_core(part_oth))
                grad, grad_spec, grad_o, grad_o_spec = rows5(g0), local, rows5(to_chip(g0)), local
                f_small1 = f_small
            else:
                input_keep, input_send, small = attn_norm(
                    0, ds, part_own, to_core(part_oth), (a_small1, f_small, f_small1)
                )
            ffn = in_dp_order(total(f_keep, to_core(f_send)))
            qv = in_dp_order(total(keep, to_chip(send)))
            ko = jnp.stack([z_keep, z_send], 1).reshape(8, 2, PART, HALF)
            ko = total(ko, to_chip(ko))
            ordered = []
            for mine, far, near, both in (gathered(ffn), gathered(qv)):
                here = jnp.stack([jnp.where(chip == 0, mine, far), jnp.where(chip == 0, far, mine)])
                there = jnp.stack([jnp.where(chip == 0, near, both), jnp.where(chip == 0, both, near)])
                pair = jnp.stack([jnp.where(core == 0, here, there), jnp.where(core == 0, there, here)], 1)
                ordered.append(pair.astype(F32))
            ko_other = to_core(ko)
            ko_all = jnp.stack([jnp.where(core == 0, ko, ko_other), jnp.where(core == 0, ko_other, ko)]).astype(F32)
            f_all, qv_all = ordered
            up = f_all[:, :, :, 0:2].transpose(2, 4, 0, 1, 3, 5).reshape(D, FF)
            down = f_all[:, :, :, 2:4].transpose(2, 1, 3, 4, 0, 5).reshape(FF, D)
            q, v = (qv_all[n].transpose(1, 2, 0, 3).reshape(D, D) for n in range(2))
            k, out = (ko_all[:, :, n].transpose(1, 2, 0, 3).reshape(D, D) for n in range(2))
            grads[layer] = [
                lax.psum_scatter(array, "dp", scatter_dimension=0, tiled=True)
                for array in (up, down, jnp.concatenate([q, k, v], 1), out)
            ]
        ups, downs, qkvs, outs = (jnp.stack(pair) for pair in zip(*grads))
        small = lax.psum(small, ("section", "dp")).reshape(4, 8, D)

        def mine_of(rows):
            width = rows.shape[-1] // replicas
            return lax.dynamic_slice_in_dim(rows, replica * width, width, 1)

        g_a_gain, g_a_shift, g_b_out = (mine_of(small[0:2, n]) for n in range(3))
        g_f_gain, g_f_shift, g_b_down = (mine_of(small[2:4, n]) for n in range(3))
        g_b_up = mine_of(small[2:4, 4:8].reshape(2, FF))

        def placed(keep, got):
            got = got.astype(F32)
            return jnp.stack([jnp.where(chip == 0, keep, got), jnp.where(chip == 0, got, keep)])[:, None]

        final_out, input_out = placed(final_keep, final_got), placed(input_keep, to_chip(input_send))

    return (
        final_out,
        input_out,
        g_a_gain,
        g_a_shift,
        qkvs,
        outs,
        g_b_out,
        g_f_gain,
        g_f_shift,
        ups,
        g_b_up,
        downs,
        g_b_down,
    )


def solution(mesh):
    split = P(None, "dp", None, None)
    placed = (split, P(None, "dp", None)) + (P(),) * 11 + (split,)
    rows = P(None, "dp", "section", None)
    vector, matrix = P(None, "dp"), P(None, "dp", None)
    return jax.shard_map(
        on_device,
        mesh=mesh,
        in_specs=placed,
        out_specs=(
            rows,
            rows,
            vector,
            vector,
            matrix,
            matrix,
            vector,
            vector,
            vector,
            matrix,
            vector,
            matrix,
            vector,
        ),
        check_vma=False,
    )
```

```python
from functools import partial

import jax
import jax.numpy as jnp
from jax import lax
from jax.experimental import pallas as pl
from jax.experimental.pallas import tpu as pltpu
from jax.sharding import PartitionSpec as P

BF = jnp.bfloat16
F32 = jnp.float32
EPS = 1e-05
MASKED = -1e30
D = 768
HALF = 384
PAIR = 128
HEAD_DIM = 64
FF = 3072
LENGTH = 1024
BLOCK = 256
ROWS = 512
PART = 96
GELU_A = 0.7978845608028654
GELU_B = GELU_A * 0.044715


def dot(a, b):
    return jnp.dot(a, b, preferred_element_type=F32)


def dot_nt(a, b):
    return lax.dot_general(a, b, (((1,), (1,)), ((), ())), preferred_element_type=F32)


def dot_tn(a, b):
    return lax.dot_general(a, b, (((0,), (0,)), ((), ())), preferred_element_type=F32)


def normalise(rows):
    center = rows - jnp.mean(rows, -1, keepdims=True)
    spread = lax.rsqrt(jnp.mean(center * center, -1, keepdims=True) + EPS)
    return center * spread, spread


def norm_low(rows, gain, shift):
    unit, _ = normalise(rows.astype(F32))
    return (unit * gain + shift).astype(BF)


def call(body, grid, in_specs, out_specs, out_shape, scratch, cost, deps=(), aliases=None):
    count = len(in_specs)

    def with_deps(sc, *refs):
        return body(sc, *refs[:count], *refs[count + len(deps) :])

    kernel = pl.pallas_call(
        with_deps,
        grid_spec=pltpu.PrefetchScalarGridSpec(
            num_scalar_prefetch=1,
            grid=grid,
            in_specs=list(in_specs) + [pl.BlockSpec(memory_space=pl.ANY)] * len(deps),
            out_specs=out_specs,
            scratch_shapes=scratch,
        ),
        out_shape=out_shape,
        input_output_aliases=aliases or {},
        compiler_params=pltpu.CompilerParams(vmem_limit_bytes=32 * 1024 * 1024),
        cost_estimate=pl.CostEstimate(flops=int(5 * cost[0]), bytes_accessed=int(5 * cost[1]), transcendentals=0),
    )
    return lambda *args: kernel(*args, *deps)


def shape(dims, dtype):
    return jax.ShapeDtypeStruct(dims, dtype)


def stored(dims, dtype):
    return pltpu.MemorySpace.HBM(dims, dtype)


def from_hbm(array):
    return pltpu.with_memory_space_constraint(array, pltpu.MemorySpace.HBM)


def whole(dims):
    count = len(dims)
    return pl.BlockSpec(dims, lambda i, sc: (0,) * count)


def at_layer(dims, layer):
    count = len(dims) - 1
    return pl.BlockSpec(dims, lambda i, sc: (layer,) + (0,) * count)


X, C, Y, Z = 0, 1, 2, 3


def in_order(own, other, block, core):
    return jnp.where(core == block % 2, own[block // 2], other[block // 2])


def weight_copies(layer, core, weights, sides, sems):
    return [
        pltpu.make_async_copy(
            weights.at[layer, :, pl.ds(pl.multiple_of(j * D + core * HALF, PAIR), HALF)],
            sides.at[:, j * HALF : (j + 1) * HALF],
            sems.at[j],
        )
        for j in range(3)
    ]


def episode_columns(ep_ref):
    row = jnp.broadcast_to(ep_ref[...].reshape(1, LENGTH).astype(F32), (PAIR, LENGTH))
    return row, row.T


def first_key(i):
    return max(0, i - 2) * BLOCK


def attn_fwd_body(sc, own, other, ep, gain, shift, wq, wk, wv, qkv, ctx, ctx_own, ctx_oth, lse, bias, vext, lse_cols):
    core = sc[C]
    own, other = own.at[0, :, 0], other.at[0, :, 0]
    for b in range(4):
        rows = slice(b * BLOCK, (b + 1) * BLOCK)
        normed = norm_low(in_order(own, other, b, core), gain[0], shift[0])
        qkv[rows, 0:HALF] = (dot(normed, wq[0]).astype(BF) * 0.125).astype(BF)
        qkv[rows, HALF : 2 * HALF] = dot(normed, wk[0]).astype(BF)
        qkv[rows, 2 * HALF : 3 * HALF] = dot(normed, wv[0]).astype(BF)
    ep_row, ep_col = episode_columns(ep)
    for i in range(4):
        lo, hi = first_key(i), (i + 1) * BLOCK
        key_at = lo + lax.broadcasted_iota(jnp.int32, (BLOCK, hi - lo), 1)
        row_at = i * BLOCK + lax.broadcasted_iota(jnp.int32, (BLOCK, hi - lo), 0)
        same = ep_col[i * BLOCK : hi, 0:1] == ep_row[0:1, lo:hi]
        bias[i, :, 0 : hi - lo] = jnp.where((key_at <= row_at) & same, 0.0, MASKED)
    vext[:, PAIR:] = jnp.ones((LENGTH, PAIR), BF)
    lane = lax.broadcasted_iota(jnp.int32, (BLOCK, PAIR), 1)

    @pl.loop(0, 3)
    def _(p):
        at = pl.multiple_of(p * PAIR, PAIR)
        vext[:, 0:PAIR] = qkv[:, pl.ds(2 * HALF + at, PAIR)]
        for i in range(4):
            lo, hi = first_key(i), (i + 1) * BLOCK
            rows = slice(i * BLOCK, hi)
            q = qkv[rows, pl.ds(at, PAIR)]
            k = qkv[lo:hi, pl.ds(HALF + at, PAIR)]
            outs = []
            for h in range(2):
                mine = (lane >= HEAD_DIM) if h else (lane < HEAD_DIM)
                s = dot_nt(jnp.where(mine, q, jnp.zeros_like(q)), k) + bias[i, :, 0 : hi - lo]
                top = jnp.max(s, -1, keepdims=True)
                prob = jnp.exp(s - top).astype(BF)
                o = dot(prob, vext[lo:hi, :])
                total = o[:, PAIR : PAIR + 1]
                outs.append(o[:, 0:PAIR] / total)
                lse_cols[rows, :] = jnp.where(lane == 2 * p + h, top + jnp.log(total), lse_cols[rows, :])
            ctx[rows, pl.ds(at, PAIR)] = jnp.where(lane < HEAD_DIM, outs[0], outs[1]).astype(BF)

    lse[...] = lse_cols[...].T[0:8]
    for b in range(4):
        piece = ctx[b * BLOCK : (b + 1) * BLOCK]

        @pl.when(core == b % 2)
        def _():
            ctx_own[b // 2] = piece

        @pl.when(core != b % 2)
        def _():
            ctx_oth[b // 2] = piece


def attention_forward(scalars, layer, own, own_spec, other, other_spec, episodes, ep_spec, gain, shift, w_qkv):
    columns = [pl.BlockSpec((1, D, HALF), partial(lambda j, i, sc: (layer, 0, 2 * j + sc[C]), j)) for j in range(3)]
    return call(
        attn_fwd_body,
        (1,),
        [own_spec, other_spec, ep_spec, at_layer((1, 1, D), layer), at_layer((1, 1, D), layer)] + columns,
        [
            whole((LENGTH, 3 * HALF)),
            whole((LENGTH, HALF)),
            whole((2, BLOCK, HALF)),
            whole((2, BLOCK, HALF)),
            whole((8, LENGTH)),
        ],
        [
            stored((LENGTH, 3 * HALF), BF),
            stored((LENGTH, HALF), BF),
            shape((2, BLOCK, HALF), BF),
            shape((2, BLOCK, HALF), BF),
            shape((8, LENGTH), F32),
        ],
        [
            pltpu.VMEM((4, BLOCK, 3 * BLOCK), F32),
            pltpu.VMEM((LENGTH, 2 * PAIR), BF),
            pltpu.VMEM((LENGTH, PAIR), F32),
        ],
        (1.8e9 + 2.4e9, 8e6),
    )(scalars, own, other, episodes, gain, shift, *[from_hbm(w_qkv)] * 3)


def gelu_parts(u):
    cubic = GELU_B * (u * u)
    t = jnp.tanh(u * (GELU_A + cubic))
    half = 0.5 * t + 0.5
    active = u * half
    slope = half + (active * (1.0 - half)) * (6.0 * cubic + 2.0 * GELU_A)
    return active, slope


FT = 1024


def project_body(sc, ctx_own, ctx_rcv, own, w_out, b_out, s2, ctx_full):
    core = sc[C]
    a, b = ctx_own[...].reshape(ROWS, HALF), ctx_rcv[...].reshape(ROWS, HALF)
    both = jnp.concatenate([jnp.where(core == 0, a, b), jnp.where(core == 0, b, a)], 1)
    ctx_full[...] = both
    stream = own[0, :, 0].reshape(ROWS, D).astype(F32) + dot(both, w_out[0]) + b_out[0]
    s2[...] = stream.astype(BF)


def ffn_fwd_body(last, sc, *refs):
    if last:
        s2, gain, shift, w_up, b_up, w_down, b_down, act, slope, keep, send, normed, acc = refs
    else:
        gain, shift, w_up, b_up, w_down, b_down, s2, ctx_full, act, slope, s3, normed, acc = refs[5:]
    t = pl.program_id(0)

    @pl.when(t == 0)
    def _():
        if not last:
            project_body(sc, *refs[:5], s2, ctx_full)
        low = s2[...]
        normed[...] = norm_low(low, gain[0], shift[0])
        acc[...] = low.astype(F32) + b_down[0]

    u = dot(normed[...], w_up[0]) + b_up[0]
    a, d = gelu_parts(u)
    a = a.astype(BF)
    act[...] = a
    slope[...] = d.astype(BF)
    acc[...] += dot(a, w_down[0])

    @pl.when(t == FF // FT - 1)
    def _():
        if last:
            x = sc[X]
            keep[...] = acc[pl.ds(pl.multiple_of(x * BLOCK, BLOCK), BLOCK)]
            send[...] = acc[pl.ds(pl.multiple_of((1 - x) * BLOCK, BLOCK), BLOCK)].astype(BF)
        else:
            s3[...] = acc[...].reshape(2, BLOCK, D).astype(BF)


def ffn_forward(scalars, layer, ctx_own, ctx_rcv, own, own_spec, weights, deps):
    specs, ffn_weight_specs, hidden = projection_specs(layer, own_spec), ffn_specs(layer), hidden_specs()
    w_out, b_out, gain, shift, w_up, b_up, w_down, b_down = weights
    return call(
        partial(ffn_fwd_body, False),
        (FF // FT,),
        specs + ffn_weight_specs,
        [whole((ROWS, D)), whole((ROWS, D))] + hidden + [whole((2, BLOCK, D))],
        [shape((ROWS, D), BF)] * 2 + [stored((ROWS, FF), BF)] * 2 + [shape((2, BLOCK, D), BF)],
        [pltpu.VMEM((ROWS, D), BF), pltpu.VMEM((ROWS, D), F32)],
        (5.4e9, 20e6),
        deps,
    )(scalars, ctx_own, ctx_rcv, own, from_hbm(w_out), b_out, gain, shift, from_hbm(w_up), b_up, from_hbm(w_down), b_down)


def projected(scalars, layer, ctx_own, ctx_rcv, own, own_spec, w_out, b_out, deps):
    return call(
        project_body,
        (1,),
        projection_specs(layer, own_spec),
        [whole((ROWS, D)), whole((ROWS, D))],
        [shape((ROWS, D), BF)] * 2,
        [],
        (6e8, 5e6),
        deps,
    )(scalars, ctx_own, ctx_rcv, own, from_hbm(w_out), b_out)


def last_ffn_forward(scalars, layer, s2, weights):
    gain, shift, w_up, b_up, w_down, b_down = weights
    return call(
        partial(ffn_fwd_body, True),
        (FF // FT,),
        [whole((ROWS, D))] + ffn_specs(layer),
        hidden_specs() + [whole((BLOCK, D)), whole((BLOCK, D))],
        [shape((ROWS, FF), BF)] * 2 + [shape((BLOCK, D), F32), shape((BLOCK, D), BF)],
        [pltpu.VMEM((ROWS, D), BF), pltpu.VMEM((ROWS, D), F32)],
        (4.8e9, 18e6),
    )(scalars, s2, gain, shift, from_hbm(w_up), b_up, from_hbm(w_down), b_down)


def projection_specs(layer, own_spec):
    part = whole((2, BLOCK, HALF))
    return [part, part, own_spec, at_layer((1, D, D), layer), at_layer((1, 1, D), layer)]


def ffn_specs(layer):
    vector = at_layer((1, 1, D), layer)
    return [
        vector,
        vector,
        pl.BlockSpec((1, D, FT), lambda i, sc: (layer, 0, i)),
        pl.BlockSpec((1, 1, FT), lambda i, sc: (layer, 0, i)),
        pl.BlockSpec((1, FT, D), lambda i, sc: (layer, i, 0)),
        vector,
    ]


def hidden_specs():
    return [pl.BlockSpec((ROWS, FT), lambda i, sc: (0, i))] * 2


def norm_back(d_normed, rows, gain):
    unit, spread = normalise(rows)
    d_unit = d_normed * gain
    first = jnp.mean(d_unit, -1, keepdims=True)
    second = jnp.mean(d_unit * unit, -1, keepdims=True)
    d_rows = spread * (d_unit - first - unit * second)
    return d_rows, jnp.sum(d_normed * unit, 0, keepdims=True), jnp.sum(d_normed, 0, keepdims=True)


def small_rows(*vectors):
    return jnp.concatenate(vectors + (jnp.zeros((8 - len(vectors), D), F32),))


def attn_norm_body(last, sc, grad, part, part_rcv, own, gain, *rest):
    before, outs = rest[:3] if last else (), rest[3:] if last else rest
    grad_rows = grad[...].reshape(ROWS, D).astype(F32)
    d_normed = part[...].reshape(ROWS, D) + part_rcv[...].reshape(ROWS, D).astype(F32)
    d_rows, g_gain, g_shift = norm_back(d_normed, own[0, :, 0].reshape(ROWS, D).astype(F32), gain[0])
    total = grad_rows + d_rows
    small = outs[-1]
    small[0:8] = small_rows(g_gain, g_shift, jnp.sum(grad_rows, 0, keepdims=True))
    for j, ref in enumerate(before):
        small[8 * (j + 1) : 8 * (j + 2)] = ref[...]
    if last:
        keep, send = outs[0:2]
        keep[...] = jnp.where(sc[X] == 0, total[0:BLOCK], total[BLOCK:ROWS])
        send[...] = jnp.where(sc[X] == 0, total[BLOCK:ROWS], total[0:BLOCK]).astype(BF)
    else:
        outs[0][...] = total.astype(BF).reshape(2, BLOCK, D)


def attention_norm_back(scalars, layer, grad, part, part_rcv, own, own_spec, gain, smalls=(), deps=()):
    block = whole((2, BLOCK, D))
    last = bool(smalls)
    if last:
        out_specs = [whole((BLOCK, D)), whole((BLOCK, D))]
        out_shape = [shape((BLOCK, D), F32), shape((BLOCK, D), BF)]
    else:
        out_specs, out_shape = [block], [shape((2, BLOCK, D), BF)]
    rows = 8 * (1 + len(smalls))
    return call(
        partial(attn_norm_body, last),
        (1,),
        [block, block, block, own_spec, at_layer((1, 1, D), layer)] + [whole((8, D))] * len(smalls),
        out_specs + [whole((rows, D))],
        out_shape + [shape((rows, D), F32)],
        [],
        (2e8, 5e6),
        deps,
    )(scalars, grad, part, part_rcv, own, gain, *smalls)


BT = 768
AT = 1536


def ffn_back_body(sc, grad, s2, gain, w_up, w_down, slope, dh, ds, small, acc):
    t = pl.program_id(0)
    low = grad[0, :, 0].reshape(ROWS, D)
    d_act = dot_nt(low, w_down[0])
    d_hidden = d_act * slope[...].astype(F32)
    d_low = d_hidden.astype(BF)
    dh[...] = d_low
    sums = jnp.sum(d_low.astype(F32), 0, keepdims=True)
    for j in range(2):
        small[pl.ds(4 + 2 * t + j, 1)] = sums[:, j * D : (j + 1) * D]
    part = dot_nt(d_low, w_up[0])

    @pl.when(t == 0)
    def _():
        acc[...] = part

    @pl.when(t > 0)
    def _():
        acc[...] += part

    @pl.when(t == FF // AT - 1)
    def _():
        rows = low.astype(F32)
        d_rows, g_gain, g_shift = norm_back(acc[...], s2[...].astype(F32), gain[0])
        ds[...] = (rows + d_rows).astype(BF).reshape(2, BLOCK, D)
        small[0:4] = small_rows(g_gain, g_shift, jnp.sum(rows, 0, keepdims=True))[0:4]


def ffn_backward(scalars, layer, grad, grad_spec, s2, slope, weights, deps=()):
    gain, w_up, w_down = weights
    return call(
        ffn_back_body,
        (FF // AT,),
        [
            grad_spec,
            whole((ROWS, D)),
            at_layer((1, 1, D), layer),
            pl.BlockSpec((1, D, AT), lambda i, sc: (layer, 0, i)),
            pl.BlockSpec((1, AT, D), lambda i, sc: (layer, i, 0)),
            pl.BlockSpec((ROWS, AT), lambda i, sc: (0, i)),
        ],
        [
            pl.BlockSpec((ROWS, AT), lambda i, sc: (0, i)),
            whole((2, BLOCK, D)),
            whole((8, D)),
        ],
        [shape((ROWS, FF), BF), shape((2, BLOCK, D), BF), shape((8, D), F32)],
        [pltpu.VMEM((ROWS, D), F32)],
        (4.9e9, 18e6),
        deps,
    )(scalars, grad, s2, gain, from_hbm(w_up), from_hbm(w_down), (slope if layer == 1 else from_hbm(slope)))


def place(sc, piece):
    return (piece % 2) ^ sc[Y], (piece // 2) ^ sc[Z]


def ffn_weight_body(
    sc, grad, grad_o, s2, s2_o, gain, shift, act, dh, w_up, b_up, w_down, keep, send, n_t, n_o, g_t, acts, dhs
):
    t = pl.program_id(0)
    core = sc[C]
    low, low_o = grad[0, :, 0].reshape(ROWS, D), grad_o[0, :, 0].reshape(ROWS, D)

    @pl.when(t == 0)
    def _():
        n_t[:, 0:ROWS] = norm_low(s2[...], gain[0], shift[0]).T
        other = norm_low(s2_o[...], gain[0], shift[0])
        n_o[...] = other
        n_t[:, ROWS : 2 * ROWS] = other.T
        x = sc[X]
        g_t[:, 0:ROWS] = jnp.where(x == 0, low[:, 0:HALF], low[:, HALF:D]).T
        g_t[:, ROWS : 2 * ROWS] = jnp.where(x == 0, low_o[:, 0:HALF], low_o[:, HALF:D]).T

    u = dot(n_o[...], w_up[0]) + b_up[0]
    acts[0:ROWS] = act[...]

    @pl.when(t < 2)
    def _():
        active_o, slope_o = gelu_parts(u)
        acts[ROWS : 2 * ROWS] = active_o.astype(BF)
        dhs[0:ROWS] = dh[...]
        dhs[ROWS : 2 * ROWS] = (dot_nt(low_o, w_down[0]) * slope_o).astype(BF)
        g_up = dot(n_t[...], dhs[...]).astype(BF)
        for ref, when in ((send, 0), (keep, 1)):

            @pl.when(t == when)
            def _():
                for piece in range(8):
                    py, pz = place(sc, piece)
                    for j in range(2):
                        ref[py, pz, j] = g_up[piece * PART : (piece + 1) * PART, j * HALF : (j + 1) * HALF]

    @pl.when(t >= 2)
    def _():
        acts[ROWS : 2 * ROWS] = gelu_parts(u)[0].astype(BF)

    g_down = dot(g_t[...], acts[...]).astype(BF).T
    tile = ffn_tile(t, sc)
    for half in range(2):
        py, pz = place(sc, 2 * tile + half)
        for j in range(2):
            first = g_down[half * HALF + j * PART : half * HALF + (j + 1) * PART]
            second = g_down[half * HALF + (j + 2) * PART : half * HALF + (j + 3) * PART]
            keep[py, pz, 2 + j] = jnp.where(core == 0, first, second)
            send[py, pz, 2 + j] = jnp.where(core == 0, second, first)


def ffn_tile(step, sc):
    mine = 2 * sc[X]
    rest = 2 - mine
    return jnp.where(step == 0, mine + 1 - sc[C], jnp.where(step == 1, mine + sc[C], rest + step - 2))


def ffn_weights(scalars, layer, grad, grad_spec, grad_o, grad_o_spec, s2, s2_o, act, dh, weights, deps=()):
    gain, shift, w_up, b_up, w_down = weights
    packed = (2, 4, 4, PART, HALF)
    return call(
        ffn_weight_body,
        (FF // BT,),
        [
            grad_spec,
            grad_o_spec,
            whole((ROWS, D)),
            whole((ROWS, D)),
            at_layer((1, 1, D), layer),
            at_layer((1, 1, D), layer),
            pl.BlockSpec((ROWS, BT), lambda i, sc: (0, ffn_tile(i, sc))),
            pl.BlockSpec((ROWS, BT), lambda i, sc: (0, ffn_tile(jnp.minimum(i, 1), sc))),
            pl.BlockSpec((1, D, BT), lambda i, sc: (layer, 0, ffn_tile(i, sc))),
            pl.BlockSpec((1, 1, BT), lambda i, sc: (layer, 0, ffn_tile(i, sc))),
            pl.BlockSpec((1, BT, D), lambda i, sc: (layer, ffn_tile(jnp.minimum(i, 1), sc), 0)),
        ],
        [whole(packed), whole(packed)],
        [stored(packed, BF), shape(packed, BF)],
        [
            pltpu.VMEM((D, 2 * ROWS), BF),
            pltpu.VMEM((ROWS, D), BF),
            pltpu.VMEM((HALF, 2 * ROWS), BF),
            pltpu.VMEM((2 * ROWS, BT), BF),
            pltpu.VMEM((2 * ROWS, BT), BF),
        ],
        (8.6e9, 22e6),
        deps,
    )(scalars, grad, grad_o, s2, s2_o, gain, shift, (act if layer == 1 else from_hbm(act)), dh, from_hbm(w_up), b_up, from_hbm(w_down))


def attn_back_body(
    layer, sc, gr_own, gr_rcv, qkv, ctx, lse, ep, w_out, weights, d_qkv, part_own, part_oth, bias, d_ctx, delta, d_k, d_v,
    sides, sems
):
    core = sc[C]
    copies = weight_copies(layer, core, weights, sides, sems)
    for copy in copies:
        copy.start()
    for b in range(4):
        rows = slice(b * BLOCK, (b + 1) * BLOCK)
        d_ctx[rows] = dot_nt(in_order(gr_own, gr_rcv, b, core), w_out[0]).astype(BF)
    product = d_ctx[...].astype(F32) * ctx[...].astype(F32)
    high = product.astype(BF)
    rest = (product - high.astype(F32)).astype(BF)
    picks = (
        lax.broadcasted_iota(jnp.int32, (8, HALF), 0) == lax.broadcasted_iota(jnp.int32, (8, HALF), 1) // HEAD_DIM
    ).astype(BF)
    delta[...] = dot_nt(picks, high) + dot_nt(picks, rest)
    ep_row, ep_col = episode_columns(ep)
    for i in range(4):
        lo, hi = first_key(i), (i + 1) * BLOCK
        key_at = lo + lax.broadcasted_iota(jnp.int32, (hi - lo, BLOCK), 0)
        row_at = i * BLOCK + lax.broadcasted_iota(jnp.int32, (hi - lo, BLOCK), 1)
        same = ep_col[lo:hi, 0:1] == ep_row[0:1, i * BLOCK : hi]
        bias[i, 0 : hi - lo, :] = jnp.where((key_at <= row_at) & same, 0.0, MASKED)

    @pl.loop(0, 3)
    def _(p):
        at = pl.multiple_of(p * PAIR, PAIR)
        d_k[...] = jnp.zeros_like(d_k)
        d_v[...] = jnp.zeros_like(d_v)
        for i in range(4):
            lo, hi = first_key(i), (i + 1) * BLOCK
            rows = slice(i * BLOCK, hi)
            q = qkv[rows, pl.ds(at, PAIR)]
            k = qkv[lo:hi, pl.ds(HALF + at, PAIR)]
            v = qkv[lo:hi, pl.ds(2 * HALF + at, PAIR)]
            dc = d_ctx[rows, pl.ds(at, PAIR)]
            d_q = jnp.zeros((BLOCK, PAIR), F32)
            for h in range(2):

                def only(array):
                    lane = lax.broadcasted_iota(jnp.int32, array.shape, 1)
                    mine = (lane >= HEAD_DIM) if h else (lane < HEAD_DIM)
                    return jnp.where(mine, array, jnp.zeros_like(array))

                q_h, dc_h = only(q), only(dc)
                s = dot_nt(k, q_h) + bias[i, 0 : hi - lo, :]
                prob = jnp.exp(s - lse[pl.ds(2 * p + h, 1), rows])
                d_p = dot_nt(v, dc_h)
                d_s = (prob * (d_p - delta[pl.ds(2 * p + h, 1), rows])).astype(BF)
                d_v[lo:hi] += dot(prob.astype(BF), dc_h)
                d_k[lo:hi] += dot(d_s, q_h)
                d_q += dot_tn(d_s, only(k))
            d_qkv[rows, pl.ds(at, PAIR)] = (d_q * 0.125).astype(BF)
        d_qkv[:, pl.ds(HALF + at, PAIR)] = d_k[...].astype(BF)
        d_qkv[:, pl.ds(2 * HALF + at, PAIR)] = d_v[...].astype(BF)

    for copy in copies:
        copy.wait()
    parts = dot_nt(d_qkv[...], sides[...])
    for b in range(4):
        part = parts[b * BLOCK : (b + 1) * BLOCK]

        @pl.when(core == b % 2)
        def _():
            part_own[b // 2] = part

        @pl.when(core != b % 2)
        def _():
            part_oth[b // 2] = part.astype(BF)


def attention_backward(scalars, layer, gr_own, gr_rcv, qkv, ctx, lse, episodes, ep_spec, w_out, w_qkv, deps=()):
    block = whole((2, BLOCK, D))
    return call(
        partial(attn_back_body, layer),
        (1,),
        [
            block,
            block,
            whole((LENGTH, 3 * HALF)),
            whole((LENGTH, HALF)),
            whole((8, LENGTH)),
            ep_spec,
            pl.BlockSpec((1, HALF, D), lambda i, sc: (layer, sc[C], 0)),
            pl.BlockSpec(memory_space=pl.ANY),
        ],
        [whole((LENGTH, 3 * HALF)), block, block],
        [shape((LENGTH, 3 * HALF), BF), shape((2, BLOCK, D), F32), shape((2, BLOCK, D), BF)],
        [
            pltpu.VMEM((4, 3 * BLOCK, BLOCK), F32),
            pltpu.VMEM((LENGTH, HALF), BF),
            pltpu.VMEM((8, LENGTH), F32),
            pltpu.VMEM((LENGTH, PAIR), F32),
            pltpu.VMEM((LENGTH, PAIR), F32),
            pltpu.VMEM((D, 3 * HALF), BF),
            pltpu.SemaphoreType.DMA((3,)),
        ],
        (2.5e9 + 6e9, 12e6),
        deps,
    )(scalars, gr_own, gr_rcv, from_hbm(qkv), from_hbm(ctx), lse, episodes, from_hbm(w_out), from_hbm(w_qkv))


def attn_weight_body(
    z_first, sc, own, other, gain, shift, d_qkv, gr_own, gr_rcv, ctx_full, ctx_oth, ctx_rcv, keep, send, z_keep, z_send, n_t
):
    core, x = sc[C], sc[X]
    own, other = own.at[0, :, 0], other.at[0, :, 0]
    for b in range(4):
        rows = slice(b * BLOCK, (b + 1) * BLOCK)
        n_t[:, rows] = norm_low(in_order(own, other, b, core), gain[0], shift[0]).T

    def columns(ref):
        rows = ref[...].reshape(ROWS, D)
        return jnp.where(core == 0, rows[:, 0:HALF], rows[:, HALF:D]).T

    def grad(j):
        return dot(n_t[...], d_qkv[:, j * HALF : (j + 1) * HALF]).astype(BF)

    first, second = grad(0), grad(2)
    mine, yours = jnp.where(x == 0, first, second), jnp.where(x == 0, second, first)
    for piece in range(8):
        py, pz = place(sc, piece)
        keep[py, pz] = mine[piece * PART : (piece + 1) * PART]
        send[py, pz] = yours[piece * PART : (piece + 1) * PART]

    a, b = ctx_oth[...].reshape(ROWS, HALF), ctx_rcv[...].reshape(ROWS, HALF)
    far = jnp.concatenate([jnp.where(core == 0, a, b), jnp.where(core == 0, b, a)], 1)
    g_out = (dot(columns(gr_own), ctx_full[...]) + dot(columns(gr_rcv), far)).astype(BF).T
    for j, rows in enumerate((grad(1), g_out)):
        for piece in range(8):
            py, pz = place(sc, piece)
            value = rows[piece * PART : (piece + 1) * PART]

            far = pz % 2 if z_first else py

            @pl.when(far == 0)
            def _():
                if z_first:
                    z_keep[pz // 2, py, j] = value
                else:
                    z_keep[pz, j] = value

            @pl.when(far == 1)
            def _():
                if z_first:
                    z_send[pz // 2, py, j] = value
                else:
                    z_send[pz, j] = value


def attention_weights(
    scalars, layer, own, own_spec, other, other_spec, gain, shift, d_qkv, gr_own, gr_rcv, ctx_full, ctx_oth, ctx_rcv, deps=()
):
    z_first = layer == 1
    packed, z_packed = (2, 4, PART, HALF), ((2, 2) if z_first else (4,)) + (2, PART, HALF)
    block = whole((2, BLOCK, D))
    return call(
        partial(attn_weight_body, z_first),
        (1,),
        [
            own_spec,
            other_spec,
            at_layer((1, 1, D), layer),
            at_layer((1, 1, D), layer),
            whole((LENGTH, 3 * HALF)),
            block,
            block,
            whole((ROWS, D)),
            whole((2, BLOCK, HALF)),
            whole((2, BLOCK, HALF)),
        ],
        [whole(packed), whole(packed), whole(z_packed), whole(z_packed)],
        [stored(packed, BF), shape(packed, BF), stored(z_packed, BF), shape(z_packed, BF)],
        [pltpu.VMEM((D, LENGTH), BF)],
        (2.5e9, 12e6),
        deps,
    )(scalars, own, other, gain, shift, d_qkv, gr_own, gr_rcv, ctx_full, ctx_oth, ctx_rcv)


def to_core(value):
    return lax.ppermute(value, "section", [(0, 1), (1, 0), (2, 3), (3, 2)])


def to_chip(value):
    return lax.ppermute(value, "section", [(0, 2), (2, 0), (1, 3), (3, 1)])


def to_dp(value, distance):
    return lax.ppermute(value, "dp", [(i, i ^ distance) for i in range(8)])


def total(*terms):
    out = terms[0].astype(F32)
    for term in terms[1:]:
        out = out + term.astype(F32)
    return out.astype(BF)


class Flat(list):
    pass


def combined(scalars, outputs, deps=(), pinned=()):
    terms, dims, dtypes = [], [], []

    def block_of(term):
        array, *index = term
        if index and isinstance(index[0], slice):
            count = index[0].stop - index[0].start
            return (count,) + array.shape[1:], (index[0].start // count,) + (0,) * (array.ndim - 1)
        rest = array.shape[len(index) :]
        return (None,) * len(index) + rest, tuple(index) + (0,) * len(rest)

    def dims_of(term):
        return tuple(d for d in block_of(term)[0] if d is not None)

    def rows_of(piece):
        found = dims_of(piece[0])
        return found[0] if len(found) == 3 else 1

    for pieces in outputs:
        rest = dims_of(pieces[0][0])
        if isinstance(pieces, Flat):
            dims.append((sum(rows_of(piece) for piece in pieces),) + rest[-2:])
        else:
            dims.append(((len(pieces),) if len(pieces) > 1 else ()) + rest)
        dtypes.append(pieces[0][0][0].dtype)
        terms += [term for piece in pieces for term in piece]

    def spec(term):
        block, index = block_of(term)
        return pl.BlockSpec(block, lambda i, sc: index)

    def body(sc, *refs):
        given = iter(refs[: len(terms)])
        for out, pieces in zip(refs[len(terms) :], outputs):
            at = 0
            for n, piece in enumerate(pieces):
                value = next(given)[...].astype(F32)
                for _ in piece[1:]:
                    value = value + next(given)[...].astype(F32)
                value = value.astype(out.dtype)
                if isinstance(pieces, Flat):
                    rows = rows_of(piece)
                    if len(value.shape) == 3:
                        out[at : at + rows] = value
                    else:
                        out[at] = value
                    at += rows
                elif len(pieces) > 1:
                    out[n] = value
                else:
                    out[...] = value

    return call(
        body,
        (1,),
        [spec(term) for term in terms],
        [whole(d) for d in dims],
        [shape(d, t) for d, t in zip(dims, dtypes)],
        [],
        (1e10, 1e7),
        deps,
    )(scalars, *[from_hbm(term[0]) if any(term[0] is a for a in pinned) else term[0] for term in terms])


def in_dp_order(both):
    return jnp.moveaxis(both, 0, 1).reshape((8,) + both.shape[2:])


def gathered(share):
    far, near = to_chip(share), to_core(share)
    return share, far, near, to_core(far)


def ffn_unpacked(sc, shares, up, down):
    for n in range(4):
        x, core = sc[X] ^ (n % 2), sc[C] ^ (n // 2)
        for j in range(2):
            at = pl.multiple_of(x * 4 * HALF + core * 2 * HALF + j * HALF, PAIR)
            up[0, :, pl.ds(at, HALF)] = shares[n][j].astype(F32)
            rows = pl.ds(pl.multiple_of(core * 2 * PART + j * PART, 8), PART)
            down[0, rows, pl.ds(pl.multiple_of(x * HALF, PAIR), HALF)] = shares[n][2 + j].astype(F32)


def unpack_early_body(sc, final_keep, final_got, input_keep, input_got, *refs):
    final, inputs, up, down = refs[-4:]
    x = sc[X]
    for ref, mine, got in ((final, final_keep, final_got), (inputs, input_keep, input_got)):
        ref[x, 0] = mine[...]
        ref[1 - x, 0] = got[...].astype(F32)
    ffn_unpacked(sc, refs[:4], up, down)


def unpack_body(shares, sc, small, up_before, down_before, *refs):
    up, down, qkv, out, a_gain, a_shift, b_out, f_gain, f_shift, b_down, b_up = refs[-11:]
    ffn_unpacked(sc, refs[:4], up, down)
    for layer in range(2):
        qv, ko = shares[layer]
        for n in range(4):
            x, core = sc[X] ^ (n % 2), sc[C] ^ (n // 2)
            index, at = qv[n]
            qkv[layer, :, pl.ds(pl.multiple_of(x * 2 * D + core * HALF, PAIR), HALF)] = refs[index][at].astype(F32)
        for n in range(2):
            side = pl.multiple_of((sc[C] ^ n) * HALF, PAIR)
            qkv[layer, :, pl.ds(pl.multiple_of(D + side, PAIR), HALF)] = refs[ko[n]][0].astype(F32)
            out[layer, :, pl.ds(side, HALF)] = refs[ko[n]][1].astype(F32)
    piece = 2 * sc[Z] + sc[Y]
    mine = jnp.zeros((32, PART), F32)
    for d in range(8):
        mine = jnp.where(piece == d, small[:, d * PART : (d + 1) * PART], mine)
    for layer in range(2):
        for j, (a_ref, f_ref) in enumerate(((a_gain, f_gain), (a_shift, f_shift), (b_out, b_down))):
            a_ref[layer : layer + 1] = mine[8 * layer + j : 8 * layer + j + 1]
            f_ref[layer : layer + 1] = mine[16 + 8 * layer + j : 16 + 8 * layer + j + 1]
        row = jnp.zeros((1, 4 * PART), F32)
        for d in range(8):
            at = 16 + 8 * layer + 4 + d // 2
            row = jnp.where(piece == d, small[at : at + 1, (d % 2) * HALF : (d % 2 + 1) * HALF], row)
        b_up[layer : layer + 1] = row


FFN_GRADS = ((2, PART, FF), (2, 4 * PART, D))


def unpacked_early(scalars, rows, arrays, layer):
    moved = ((2, 1, BLOCK, D),) * 2
    return call(
        unpack_early_body,
        (1,),
        [whole((BLOCK, D))] * 4 + [whole(array.shape) for array in arrays],
        [whole(d) for d in moved] + [at_layer((1,) + d[1:], layer) for d in FFN_GRADS],
        [shape(d, F32) for d in moved] + [stored(d, F32) for d in FFN_GRADS],
        [],
        (1e6, 9e6),
    )(scalars, *rows, *arrays)


def unpacked(scalars, small, up, down, arrays, shares):
    dims = ((2, PART, 3 * D), (2, PART, D)) + ((2, PART),) * 6 + ((2, 4 * PART),)
    held = pl.BlockSpec(memory_space=pl.ANY)
    return call(
        partial(unpack_body, shares),
        (1,),
        [whole((32, D)), held, held] + [whole(array.shape) for array in arrays],
        [at_layer((1,) + d[1:], 0) for d in FFN_GRADS] + [whole(d) for d in dims],
        [stored(d, F32) for d in FFN_GRADS] + [shape(d, F32) for d in dims],
        [],
        (1e6, 11e6),
        aliases={2: 0, 3: 1},
    )(scalars, small, from_hbm(up), from_hbm(down), *arrays)


def on_device(
    tokens,
    episodes,
    attn_gain,
    attn_shift,
    qkv_weight,
    out_weight,
    out_bias,
    ffn_gain,
    ffn_shift,
    up_weight,
    up_bias,
    down_weight,
    down_bias,
    cotangent,
):
    replicas = lax.axis_size("dp")
    section = lax.axis_index("section")
    replica = lax.axis_index("dp")
    chip, core = section // 2, section % 2
    direct = replicas == 8
    y, z = (replica % 2, replica // 2) if direct else (0, 0)
    scalars = jnp.stack([jnp.asarray(v, jnp.int32) for v in (chip, core, y, z)])

    stream = tokens.reshape(2, 2, 2, BLOCK, D)
    cot = cotangent.reshape(2, 2, 2, BLOCK, D)
    eps = episodes.reshape(2, 1, LENGTH)
    ep_spec = pl.BlockSpec((1, 1, LENGTH), lambda i, sc: (sc[X], 0, 0))

    def input_spec(micro, side):
        return pl.BlockSpec((1, 2, 1, BLOCK, D), lambda i, sc: (micro(sc[X]), 0, side(sc[C]), 0, 0))

    same, flip = (lambda v: v), (lambda v: 1 - v)
    own_in, other_in, far_in = input_spec(same, same), input_spec(same, flip), input_spec(flip, same)
    local = pl.BlockSpec((1, 2, 1, BLOCK, D), lambda i, sc: (0, 0, 0, 0, 0))

    def rows5(value):
        return value.reshape(1, 2, 1, BLOCK, D)

    def vec(array):
        return array.reshape(2, 1, -1)

    a_gain, a_shift, b_out = vec(attn_gain), vec(attn_shift), vec(out_bias)
    f_gain, f_shift, b_up, b_down = vec(ffn_gain), vec(ffn_shift), vec(up_bias), vec(down_bias)

    kept = []
    own, own_spec, other, other_spec = stream, own_in, stream, other_in
    for layer in range(2):
        seen = (own, own_spec, other, other_spec)
        if layer == 0:
            seen = (from_hbm(own), own_spec, from_hbm(other), other_spec)
        qkv, ctx, ctx_own, ctx_oth, lse = attention_forward(
            scalars, layer, *seen, eps, ep_spec, a_gain, a_shift, qkv_weight
        )
        ctx_rcv = to_core(ctx_oth)
        ctx_far = to_core(ctx_own)
        ffn = (f_gain, f_shift, up_weight, b_up, down_weight, b_down)
        if layer == 0:
            s2, ctx_full, act, slope, *result = ffn_forward(
                scalars, layer, ctx_own, ctx_rcv, own, own_spec, (out_weight, b_out) + ffn, ()
            )
            s2_o = to_chip(s2)
        else:
            s2, ctx_full = projected(
                scalars, layer, ctx_own, ctx_rcv, own, own_spec, out_weight, b_out, (kept[0][7], kept[0][11])
            )
            s2_o = to_chip(s2)
            act, slope, *result = last_ffn_forward(scalars, layer, s2, ffn)
        kept.append((own, own_spec, other, other_spec, qkv, ctx, ctx_oth, ctx_far, ctx_full, lse, s2, s2_o, act, slope))
        if layer == 0:
            s3 = result[0]
            own, own_spec, other, other_spec = rows5(s3), local, rows5(to_core(s3)), local
    final_keep, final_send = result

    def ffn_back(layer, grad, grad_spec, deps=()):
        kept_now = kept[layer]
        s2, slope = kept_now[10], kept_now[13]
        return ffn_backward(scalars, layer, grad, grad_spec, s2, slope, (f_gain, up_weight, down_weight), deps)

    def ffn_grads(layer, grad, grad_spec, grad_o, grad_o_spec, dh, deps=()):
        s2, s2_o, act, slope = kept[layer][10:]
        weights = (f_gain, f_shift, up_weight, b_up, down_weight)
        return ffn_weights(
            scalars, layer, grad, grad_spec, grad_o, grad_o_spec, s2, s2_o, act, dh, weights, deps
        )

    def attn_back(layer, ds, ds_rcv, deps=()):
        own, own_spec, other, other_spec, qkv, ctx, ctx_oth, ctx_far, ctx_full, lse = kept[layer][:10]
        return attention_backward(
            scalars, layer, ds, ds_rcv, qkv, ctx, lse, eps, ep_spec, out_weight, qkv_weight, deps
        )

    def attn_grads(layer, ds, ds_rcv, d_qkv, deps=()):
        own, own_spec, other, other_spec, qkv, ctx, ctx_oth, ctx_far, ctx_full, lse = kept[layer][:10]
        return attention_weights(
            scalars, layer, own, own_spec, other, other_spec, a_gain, a_shift, d_qkv, ds, ds_rcv, ctx_full, ctx_oth,
            ctx_far, deps,
        )

    def attn_norm(layer, ds, part_own, part_rcv, smalls=(), deps=()):
        own, own_spec = kept[layer][:2]
        return attention_norm_back(scalars, layer, ds, part_own, part_rcv, own, own_spec, a_gain, smalls, deps)

    if direct:
        pinned = []

        def summed(*outputs, deps=()):
            return combined(scalars, outputs, deps, pinned)

        def y_sum(keep, got):
            return [[(keep, 1), (got, 1)]]

        def z_sum(keep, got, y_got):
            return [[(keep, 0, k), (got, 0, k), (y_got, k)] for k in (1, 3)]

        def far_sum(keep, got, y_got, z_got):
            return [[(keep, 0, 2), (got, 0, 2), (y_got, 2), (z_got, 1)]]

        def share(keep, got, y_got, z_got, far_got):
            return [[(keep, 0, 0), (got, 0, 0), (y_got, 0), (z_got, 0), (far_got,)]]

        dh1, ds1, f_small1 = ffn_back(1, cot, own_in, [kept[1][7]])
        ds1_rcv = to_core(ds1)
        fk1, send = ffn_grads(1, cot, own_in, cot, far_in, dh1)
        pinned.append(fk1)
        fg1 = to_core(send)
        d_qkv1, part1, part1_oth = attn_back(1, ds1, ds1_rcv, [from_hbm(fk1)])
        part1_rcv = to_core(part1_oth)
        value, final_low = summed(y_sum(fk1, fg1), [[(final_send,)]], deps=[part1])
        fy1 = to_dp(value, 1)
        g0, a_small1 = attn_norm(1, ds1, part1, part1_rcv, deps=[value])
        g0_o = to_chip(g0)
        dh0, ds0, f_small0 = ffn_back(0, rows5(g0), local)
        ds0_rcv = to_core(ds0)
        qk1, send, ok1, z_send = attn_grads(1, ds1, ds1_rcv, d_qkv1, [ds0])
        pinned += [qk1, ok1]
        qg1, og1 = to_chip(send), to_dp(z_send, 2)
        fk0, send = ffn_grads(0, rows5(g0), local, rows5(g0_o), local, dh0, [from_hbm(qk1)])
        pinned.append(fk0)
        fg0 = to_core(send)
        (fz1,) = summed(z_sum(fk1, fg1, fy1), deps=[from_hbm(fk0)])
        fy0, final_low = summed(y_sum(fk0, fg0), [[(final_low,)]], deps=[fz1])
        d_qkv0, part0, part0_oth = attn_back(0, ds0, ds0_rcv, [fy0])
        final_got = to_chip(final_low)
        fz1, fy0 = to_dp(fz1, 2), to_dp(fy0, 1)
        part0_rcv = to_core(part0_oth)
        far1, y1 = summed(
            far_sum(fk1, fg1, fy1, fz1),
            Flat([[(ok1, 0, 1), (og1, 0, 1)], [(ok1, 1, 1), (og1, 1, 1)]] + y_sum(qk1, qg1)),
            deps=[part0],
        )
        input_keep, input_send, small = attn_norm(
            0, ds0, part0, part0_rcv, (a_small1, f_small0, f_small1), [far1, final_got]
        )
        far1, y1 = to_dp(far1, 4), to_dp(y1, 1)
        small_got = to_core(small)
        input_got = to_chip(input_send)
        fz0, small = summed(z_sum(fk0, fg0, fy0), [[(small,), (small_got,)]], deps=[input_keep])
        qk0, send, ok0, y_send = attn_grads(0, ds0, ds0_rcv, d_qkv0, [fz0])
        fz0, small_got = to_dp(fz0, 2), to_dp(small, 4)
        pinned += [qk0, ok0]
        qg0, oy0 = to_chip(send), to_dp(y_send, 1)

        far, qz1, f1, small = summed(
            Flat(far_sum(fk0, fg0, fy0, fz0) + [[(ok1, 1, 0), (og1, 1, 0), (y1, slice(2, 4))]]),
            [[(qk1, 0, k), (qg1, 0, k), (y1, 4 + k)] for k in (1, 3)],
            share(fk1, fg1, fy1, fz1, far1),
            [[(small,), (small_got,)]],
            deps=[from_hbm(qk0)],
        )
        far, qz1, small_got = to_dp(far, 4), to_dp(qz1, 2), to_dp(small, 1)
        f1_all = gathered(f1)

        qy0, oz0, qf1, small = summed(
            y_sum(qk0, qg0),
            [[(ok0, k), (oy0, k)] for k in (1, 3)],
            [[(qk1, 0, 2), (qg1, 0, 2), (y1, 6), (qz1, 1)]],
            [[(small,), (small_got,)]],
            deps=[input_got],
        )
        qy0, oz0, qf1, small_got = to_dp(qy0, 1), to_dp(oz0, 2), to_dp(qf1, 4), to_chip(small)

        of0, qz0, f0, ox1, small = summed(
            [[(ok0, 2), (oy0, 2), (oz0, 1)]],
            z_sum(qk0, qg0, qy0),
            [[(fk0, 0, 0), (fg0, 0, 0), (fy0, 0), (fz0, 0), (far, slice(0, 4))]],
            [[(ok1, 0, 0), (og1, 0, 0), (y1, slice(0, 2)), (far, slice(4, 6))]],
            [[(small,), (small_got,)]],
            deps=f1_all[1:],
        )
        of0, qz0, ox1_got, small_got = to_dp(of0, 4), to_dp(qz0, 2), to_chip(ox1), to_dp(small, 2)
        f0_all = gathered(f0)

        qf0, ox0, o1, small = summed(
            far_sum(qk0, qg0, qy0, qz0),
            [[(ok0, 0), (oy0, 0), (oz0, 0), (of0,)]],
            [[(ox1,), (ox1_got,)]],
            [[(small,), (small_got,)]],
        )
        qf0, ox0_got = to_dp(qf0, 4), to_chip(ox0)

        final_out, input_out, ups, downs = unpacked_early(
            scalars, (final_keep, final_got, input_keep, input_got), f1_all, 1
        )
        both, o0 = summed(
            share(qk0, qg0, qy0, qz0, qf0) + [[(qk1, 0, 0), (qg1, 0, 0), (y1, 4), (qz1, 0), (qf1,)]],
            [[(ox0,), (ox0_got,)]],
            deps=f0_all[1:] + (from_hbm(ups),),
        )
        arrays = f0_all + gathered(both) + (o0, to_core(o0), o1, to_core(o1))
        shares = ((tuple((n, 0) for n in range(4, 8)), (8, 9)), (tuple((n, 1) for n in range(4, 8)), (10, 11)))
        (ups, downs, qkvs, outs, *vectors) = unpacked(scalars, small, ups, downs, arrays, shares)
        g_a_gain, g_a_shift, g_b_out, g_f_gain, g_f_shift, g_b_down, g_b_up = vectors
    else:
        final_got = to_chip(final_send)
        grads = [None, None]
        grad, grad_spec, grad_o, grad_o_spec = cot, own_in, cot, far_in
        for layer in (1, 0):
            dh, ds, f_small = ffn_back(layer, grad, grad_spec)
            ds_rcv = to_core(ds)
            f_keep, f_send = ffn_grads(layer, grad, grad_spec, grad_o, grad_o_spec, dh)
            d_qkv, part_own, part_oth = attn_back(layer, ds, ds_rcv)
            keep, send, z_keep, z_send = attn_grads(layer, ds, ds_rcv, d_qkv)
            if layer == 1:
                g0, a_small1 = attn_norm(1, ds, part_own, to_core(part_oth))
                grad, grad_spec, grad_o, grad_o_spec = rows5(g0), local, rows5(to_chip(g0)), local
                f_small1 = f_small
            else:
                input_keep, input_send, small = attn_norm(
                    0, ds, part_own, to_core(part_oth), (a_small1, f_small, f_small1)
                )
            ffn = in_dp_order(total(f_keep, to_core(f_send)))
            qv = in_dp_order(total(keep, to_chip(send)))
            ko = jnp.stack([z_keep, z_send], 1).reshape(8, 2, PART, HALF)
            ko = total(ko, to_chip(ko))
            ordered = []
            for mine, far, near, both in (gathered(ffn), gathered(qv)):
                here = jnp.stack([jnp.where(chip == 0, mine, far), jnp.where(chip == 0, far, mine)])
                there = jnp.stack([jnp.where(chip == 0, near, both), jnp.where(chip == 0, both, near)])
                pair = jnp.stack([jnp.where(core == 0, here, there), jnp.where(core == 0, there, here)], 1)
                ordered.append(pair.astype(F32))
            ko_other = to_core(ko)
            ko_all = jnp.stack([jnp.where(core == 0, ko, ko_other), jnp.where(core == 0, ko_other, ko)]).astype(F32)
            f_all, qv_all = ordered
            up = f_all[:, :, :, 0:2].transpose(2, 4, 0, 1, 3, 5).reshape(D, FF)
            down = f_all[:, :, :, 2:4].transpose(2, 1, 3, 4, 0, 5).reshape(FF, D)
            q, v = (qv_all[n].transpose(1, 2, 0, 3).reshape(D, D) for n in range(2))
            k, out = (ko_all[:, :, n].transpose(1, 2, 0, 3).reshape(D, D) for n in range(2))
            grads[layer] = [
                lax.psum_scatter(array, "dp", scatter_dimension=0, tiled=True)
                for array in (up, down, jnp.concatenate([q, k, v], 1), out)
            ]
        ups, downs, qkvs, outs = (jnp.stack(pair) for pair in zip(*grads))
        small = lax.psum(small, ("section", "dp")).reshape(4, 8, D)

        def mine_of(rows):
            width = rows.shape[-1] // replicas
            return lax.dynamic_slice_in_dim(rows, replica * width, width, 1)

        g_a_gain, g_a_shift, g_b_out = (mine_of(small[0:2, n]) for n in range(3))
        g_f_gain, g_f_shift, g_b_down = (mine_of(small[2:4, n]) for n in range(3))
        g_b_up = mine_of(small[2:4, 4:8].reshape(2, FF))

        def placed(keep, got):
            got = got.astype(F32)
            return jnp.stack([jnp.where(chip == 0, keep, got), jnp.where(chip == 0, got, keep)])[:, None]

        final_out, input_out = placed(final_keep, final_got), placed(input_keep, to_chip(input_send))

    return (
        final_out,
        input_out,
        g_a_gain,
        g_a_shift,
        qkvs,
        outs,
        g_b_out,
        g_f_gain,
        g_f_shift,
        ups,
        g_b_up,
        downs,
        g_b_down,
    )


def solution(mesh):
    split = P(None, "dp", None, None)
    placed = (split, P(None, "dp", None)) + (P(),) * 11 + (split,)
    rows = P(None, "dp", "section", None)
    vector, matrix = P(None, "dp"), P(None, "dp", None)
    return jax.shard_map(
        on_device,
        mesh=mesh,
        in_specs=placed,
        out_specs=(
            rows,
            rows,
            vector,
            vector,
            matrix,
            matrix,
            vector,
            vector,
            vector,
            matrix,
            vector,
            matrix,
            vector,
        ),
        check_vma=False,
    )
```

```python
from functools import partial

import jax
import jax.numpy as jnp
from jax import lax
from jax.experimental import pallas as pl
from jax.experimental.pallas import tpu as pltpu
from jax.sharding import PartitionSpec as P

BF = jnp.bfloat16
F32 = jnp.float32
EPS = 1e-05
MASKED = -1e30
D = 768
HALF = 384
PAIR = 128
HEAD_DIM = 64
FF = 3072
LENGTH = 1024
BLOCK = 256
ROWS = 512
PART = 96
GELU_A = 0.7978845608028654
GELU_B = GELU_A * 0.044715


def dot(a, b):
    return jnp.dot(a, b, preferred_element_type=F32)


def dot_nt(a, b):
    return lax.dot_general(a, b, (((1,), (1,)), ((), ())), preferred_element_type=F32)


def dot_tn(a, b):
    return lax.dot_general(a, b, (((0,), (0,)), ((), ())), preferred_element_type=F32)


def normalise(rows):
    center = rows - jnp.mean(rows, -1, keepdims=True)
    spread = lax.rsqrt(jnp.mean(center * center, -1, keepdims=True) + EPS)
    return center * spread, spread


def norm_low(rows, gain, shift):
    unit, _ = normalise(rows.astype(F32))
    return (unit * gain + shift).astype(BF)


def call(body, grid, in_specs, out_specs, out_shape, scratch, cost, deps=(), aliases=None):
    count = len(in_specs)

    def with_deps(sc, *refs):
        return body(sc, *refs[:count], *refs[count + len(deps) :])

    kernel = pl.pallas_call(
        with_deps,
        grid_spec=pltpu.PrefetchScalarGridSpec(
            num_scalar_prefetch=1,
            grid=grid,
            in_specs=list(in_specs) + [pl.BlockSpec(memory_space=pl.ANY)] * len(deps),
            out_specs=out_specs,
            scratch_shapes=scratch,
        ),
        out_shape=out_shape,
        input_output_aliases=aliases or {},
        compiler_params=pltpu.CompilerParams(vmem_limit_bytes=32 * 1024 * 1024),
        cost_estimate=pl.CostEstimate(flops=int(5 * cost[0]), bytes_accessed=int(5 * cost[1]), transcendentals=0),
    )
    return lambda *args: kernel(*args, *deps)


def shape(dims, dtype):
    return jax.ShapeDtypeStruct(dims, dtype)


def stored(dims, dtype):
    return pltpu.MemorySpace.HBM(dims, dtype)


def from_hbm(array):
    return pltpu.with_memory_space_constraint(array, pltpu.MemorySpace.HBM)


def whole(dims):
    count = len(dims)
    return pl.BlockSpec(dims, lambda i, sc: (0,) * count)


def at_layer(dims, layer):
    count = len(dims) - 1
    return pl.BlockSpec(dims, lambda i, sc: (layer,) + (0,) * count)


X, C, Y, Z = 0, 1, 2, 3


def in_order(own, other, block, core):
    return jnp.where(core == block % 2, own[block // 2], other[block // 2])


def weight_copies(layer, core, weights, sides, sems):
    return [
        pltpu.make_async_copy(
            weights.at[layer, :, pl.ds(pl.multiple_of(j * D + core * HALF, PAIR), HALF)],
            sides.at[:, j * HALF : (j + 1) * HALF],
            sems.at[j],
        )
        for j in range(3)
    ]


def episode_columns(ep_ref):
    row = jnp.broadcast_to(ep_ref[...].reshape(1, LENGTH).astype(F32), (PAIR, LENGTH))
    return row, row.T


def first_key(i):
    return max(0, i - 2) * BLOCK


def attn_fwd_body(sc, own, other, ep, gain, shift, wq, wk, wv, qkv, ctx, ctx_own, ctx_oth, lse, bias, vext, lse_cols):
    core = sc[C]
    own, other = own.at[0, :, 0], other.at[0, :, 0]
    for b in range(4):
        rows = slice(b * BLOCK, (b + 1) * BLOCK)
        normed = norm_low(in_order(own, other, b, core), gain[0], shift[0])
        qkv[rows, 0:HALF] = (dot(normed, wq[0]).astype(BF) * 0.125).astype(BF)
        qkv[rows, HALF : 2 * HALF] = dot(normed, wk[0]).astype(BF)
        qkv[rows, 2 * HALF : 3 * HALF] = dot(normed, wv[0]).astype(BF)
    ep_row, ep_col = episode_columns(ep)
    for i in range(4):
        lo, hi = first_key(i), (i + 1) * BLOCK
        key_at = lo + lax.broadcasted_iota(jnp.int32, (BLOCK, hi - lo), 1)
        row_at = i * BLOCK + lax.broadcasted_iota(jnp.int32, (BLOCK, hi - lo), 0)
        same = ep_col[i * BLOCK : hi, 0:1] == ep_row[0:1, lo:hi]
        bias[i, :, 0 : hi - lo] = jnp.where((key_at <= row_at) & same, 0.0, MASKED)
    vext[:, PAIR:] = jnp.ones((LENGTH, PAIR), BF)
    lane = lax.broadcasted_iota(jnp.int32, (BLOCK, PAIR), 1)

    @pl.loop(0, 3)
    def _(p):
        at = pl.multiple_of(p * PAIR, PAIR)
        vext[:, 0:PAIR] = qkv[:, pl.ds(2 * HALF + at, PAIR)]
        for i in range(4):
            lo, hi = first_key(i), (i + 1) * BLOCK
            rows = slice(i * BLOCK, hi)
            q = qkv[rows, pl.ds(at, PAIR)]
            k = qkv[lo:hi, pl.ds(HALF + at, PAIR)]
            outs = []
            for h in range(2):
                mine = (lane >= HEAD_DIM) if h else (lane < HEAD_DIM)
                s = dot_nt(jnp.where(mine, q, jnp.zeros_like(q)), k) + bias[i, :, 0 : hi - lo]
                top = jnp.max(s, -1, keepdims=True)
                prob = jnp.exp(s - top).astype(BF)
                o = dot(prob, vext[lo:hi, :])
                total = o[:, PAIR : PAIR + 1]
                outs.append(o[:, 0:PAIR] / total)
                lse_cols[rows, :] = jnp.where(lane == 2 * p + h, top + jnp.log(total), lse_cols[rows, :])
            ctx[rows, pl.ds(at, PAIR)] = jnp.where(lane < HEAD_DIM, outs[0], outs[1]).astype(BF)

    lse[...] = lse_cols[...].T[0:8]
    for b in range(4):
        piece = ctx[b * BLOCK : (b + 1) * BLOCK]

        @pl.when(core == b % 2)
        def _():
            ctx_own[b // 2] = piece

        @pl.when(core != b % 2)
        def _():
            ctx_oth[b // 2] = piece


def attention_forward(scalars, layer, own, own_spec, other, other_spec, episodes, ep_spec, gain, shift, w_qkv):
    columns = [pl.BlockSpec((1, D, HALF), partial(lambda j, i, sc: (layer, 0, 2 * j + sc[C]), j)) for j in range(3)]
    return call(
        attn_fwd_body,
        (1,),
        [own_spec, other_spec, ep_spec, at_layer((1, 1, D), layer), at_layer((1, 1, D), layer)] + columns,
        [
            whole((LENGTH, 3 * HALF)),
            whole((LENGTH, HALF)),
            whole((2, BLOCK, HALF)),
            whole((2, BLOCK, HALF)),
            whole((8, LENGTH)),
        ],
        [
            stored((LENGTH, 3 * HALF), BF),
            stored((LENGTH, HALF), BF),
            shape((2, BLOCK, HALF), BF),
            shape((2, BLOCK, HALF), BF),
            shape((8, LENGTH), F32),
        ],
        [
            pltpu.VMEM((4, BLOCK, 3 * BLOCK), F32),
            pltpu.VMEM((LENGTH, 2 * PAIR), BF),
            pltpu.VMEM((LENGTH, PAIR), F32),
        ],
        (1.8e9 + 2.4e9, 8e6),
    )(scalars, own, other, episodes, gain, shift, *[from_hbm(w_qkv)] * 3)


def gelu_parts(u):
    cubic = GELU_B * (u * u)
    t = jnp.tanh(u * (GELU_A + cubic))
    half = 0.5 * t + 0.5
    active = u * half
    slope = half + (active * (1.0 - half)) * (6.0 * cubic + 2.0 * GELU_A)
    return active, slope


FT = 1024


def project_body(sc, ctx_own, ctx_rcv, own, w_out, b_out, s2, ctx_full):
    core = sc[C]
    a, b = ctx_own[...].reshape(ROWS, HALF), ctx_rcv[...].reshape(ROWS, HALF)
    both = jnp.concatenate([jnp.where(core == 0, a, b), jnp.where(core == 0, b, a)], 1)
    ctx_full[...] = both
    stream = own[0, :, 0].reshape(ROWS, D).astype(F32) + dot(both, w_out[0]) + b_out[0]
    s2[...] = stream.astype(BF)


def ffn_fwd_body(last, sc, *refs):
    if last:
        s2, gain, shift, w_up, b_up, w_down, b_down, act, slope, keep, send, normed, acc = refs
    else:
        gain, shift, w_up, b_up, w_down, b_down, s2, ctx_full, act, slope, s3, normed, acc = refs[5:]
    t = pl.program_id(0)

    @pl.when(t == 0)
    def _():
        if not last:
            project_body(sc, *refs[:5], s2, ctx_full)
        low = s2[...]
        normed[...] = norm_low(low, gain[0], shift[0])
        acc[...] = low.astype(F32) + b_down[0]

    u = dot(normed[...], w_up[0]) + b_up[0]
    a, d = gelu_parts(u)
    a = a.astype(BF)
    act[...] = a
    slope[...] = d.astype(BF)
    acc[...] += dot(a, w_down[0])

    @pl.when(t == FF // FT - 1)
    def _():
        if last:
            x = sc[X]
            keep[...] = acc[pl.ds(pl.multiple_of(x * BLOCK, BLOCK), BLOCK)]
            send[...] = acc[pl.ds(pl.multiple_of((1 - x) * BLOCK, BLOCK), BLOCK)].astype(BF)
        else:
            s3[...] = acc[...].reshape(2, BLOCK, D).astype(BF)


def ffn_forward(scalars, layer, ctx_own, ctx_rcv, own, own_spec, weights, deps):
    specs, ffn_weight_specs, hidden = projection_specs(layer, own_spec), ffn_specs(layer), hidden_specs()
    w_out, b_out, gain, shift, w_up, b_up, w_down, b_down = weights
    return call(
        partial(ffn_fwd_body, False),
        (FF // FT,),
        specs + ffn_weight_specs,
        [whole((ROWS, D)), whole((ROWS, D))] + hidden + [whole((2, BLOCK, D))],
        [shape((ROWS, D), BF)] * 2 + [stored((ROWS, FF), BF)] * 2 + [shape((2, BLOCK, D), BF)],
        [pltpu.VMEM((ROWS, D), BF), pltpu.VMEM((ROWS, D), F32)],
        (5.4e9, 20e6),
        deps,
    )(scalars, ctx_own, ctx_rcv, own, from_hbm(w_out), b_out, gain, shift, from_hbm(w_up), b_up, from_hbm(w_down), b_down)


def projected(scalars, layer, ctx_own, ctx_rcv, own, own_spec, w_out, b_out, deps):
    return call(
        project_body,
        (1,),
        projection_specs(layer, own_spec),
        [whole((ROWS, D)), whole((ROWS, D))],
        [shape((ROWS, D), BF)] * 2,
        [],
        (6e8, 5e6),
        deps,
    )(scalars, ctx_own, ctx_rcv, own, from_hbm(w_out), b_out)


def last_ffn_forward(scalars, layer, s2, weights):
    gain, shift, w_up, b_up, w_down, b_down = weights
    return call(
        partial(ffn_fwd_body, True),
        (FF // FT,),
        [whole((ROWS, D))] + ffn_specs(layer),
        hidden_specs() + [whole((BLOCK, D)), whole((BLOCK, D))],
        [shape((ROWS, FF), BF)] * 2 + [shape((BLOCK, D), F32), shape((BLOCK, D), BF)],
        [pltpu.VMEM((ROWS, D), BF), pltpu.VMEM((ROWS, D), F32)],
        (4.8e9, 18e6),
    )(scalars, s2, gain, shift, from_hbm(w_up), b_up, from_hbm(w_down), b_down)


def projection_specs(layer, own_spec):
    part = whole((2, BLOCK, HALF))
    return [part, part, own_spec, at_layer((1, D, D), layer), at_layer((1, 1, D), layer)]


def ffn_specs(layer):
    vector = at_layer((1, 1, D), layer)
    return [
        vector,
        vector,
        pl.BlockSpec((1, D, FT), lambda i, sc: (layer, 0, i)),
        pl.BlockSpec((1, 1, FT), lambda i, sc: (layer, 0, i)),
        pl.BlockSpec((1, FT, D), lambda i, sc: (layer, i, 0)),
        vector,
    ]


def hidden_specs():
    return [pl.BlockSpec((ROWS, FT), lambda i, sc: (0, i))] * 2


def norm_back(d_normed, rows, gain):
    unit, spread = normalise(rows)
    d_unit = d_normed * gain
    first = jnp.mean(d_unit, -1, keepdims=True)
    second = jnp.mean(d_unit * unit, -1, keepdims=True)
    d_rows = spread * (d_unit - first - unit * second)
    return d_rows, jnp.sum(d_normed * unit, 0, keepdims=True), jnp.sum(d_normed, 0, keepdims=True)


def small_rows(*vectors):
    return jnp.concatenate(vectors + (jnp.zeros((8 - len(vectors), D), F32),))


def attn_norm_body(last, sc, grad, part, part_rcv, own, gain, *rest):
    before, outs = rest[:3] if last else (), rest[3:] if last else rest
    grad_rows = grad[...].reshape(ROWS, D).astype(F32)
    d_normed = part[...].reshape(ROWS, D) + part_rcv[...].reshape(ROWS, D).astype(F32)
    d_rows, g_gain, g_shift = norm_back(d_normed, own[0, :, 0].reshape(ROWS, D).astype(F32), gain[0])
    total = grad_rows + d_rows
    small = outs[-1]
    small[0:8] = small_rows(g_gain, g_shift, jnp.sum(grad_rows, 0, keepdims=True))
    for j, ref in enumerate(before):
        small[8 * (j + 1) : 8 * (j + 2)] = ref[...]
    if last:
        keep, send = outs[0:2]
        keep[...] = jnp.where(sc[X] == 0, total[0:BLOCK], total[BLOCK:ROWS])
        send[...] = jnp.where(sc[X] == 0, total[BLOCK:ROWS], total[0:BLOCK]).astype(BF)
    else:
        outs[0][...] = total.astype(BF).reshape(2, BLOCK, D)


def attention_norm_back(scalars, layer, grad, part, part_rcv, own, own_spec, gain, smalls=(), deps=()):
    block = whole((2, BLOCK, D))
    last = bool(smalls)
    if last:
        out_specs = [whole((BLOCK, D)), whole((BLOCK, D))]
        out_shape = [shape((BLOCK, D), F32), shape((BLOCK, D), BF)]
    else:
        out_specs, out_shape = [block], [shape((2, BLOCK, D), BF)]
    rows = 8 * (1 + len(smalls))
    return call(
        partial(attn_norm_body, last),
        (1,),
        [block, block, block, own_spec, at_layer((1, 1, D), layer)] + [whole((8, D))] * len(smalls),
        out_specs + [whole((rows, D))],
        out_shape + [shape((rows, D), F32)],
        [],
        (2e8, 5e6),
        deps,
    )(scalars, grad, part, part_rcv, own, gain, *smalls)


BT = 768
AT = 1536


def ffn_back_body(sc, grad, s2, gain, w_up, w_down, slope, dh, ds, small, acc):
    t = pl.program_id(0)
    low = grad[0, :, 0].reshape(ROWS, D)
    d_act = dot_nt(low, w_down[0])
    d_hidden = d_act * slope[...].astype(F32)
    d_low = d_hidden.astype(BF)
    dh[...] = d_low
    sums = jnp.sum(d_low.astype(F32), 0, keepdims=True)
    for j in range(2):
        small[pl.ds(4 + 2 * t + j, 1)] = sums[:, j * D : (j + 1) * D]
    part = dot_nt(d_low, w_up[0])

    @pl.when(t == 0)
    def _():
        acc[...] = part

    @pl.when(t > 0)
    def _():
        acc[...] += part

    @pl.when(t == FF // AT - 1)
    def _():
        rows = low.astype(F32)
        d_rows, g_gain, g_shift = norm_back(acc[...], s2[...].astype(F32), gain[0])
        ds[...] = (rows + d_rows).astype(BF).reshape(2, BLOCK, D)
        small[0:4] = small_rows(g_gain, g_shift, jnp.sum(rows, 0, keepdims=True))[0:4]


def ffn_backward(scalars, layer, grad, grad_spec, s2, slope, weights, deps=()):
    gain, w_up, w_down = weights
    return call(
        ffn_back_body,
        (FF // AT,),
        [
            grad_spec,
            whole((ROWS, D)),
            at_layer((1, 1, D), layer),
            pl.BlockSpec((1, D, AT), lambda i, sc: (layer, 0, i)),
            pl.BlockSpec((1, AT, D), lambda i, sc: (layer, i, 0)),
            pl.BlockSpec((ROWS, AT), lambda i, sc: (0, i)),
        ],
        [
            pl.BlockSpec((ROWS, AT), lambda i, sc: (0, i)),
            whole((2, BLOCK, D)),
            whole((8, D)),
        ],
        [shape((ROWS, FF), BF), shape((2, BLOCK, D), BF), shape((8, D), F32)],
        [pltpu.VMEM((ROWS, D), F32)],
        (4.9e9, 18e6),
        deps,
    )(scalars, grad, s2, gain, from_hbm(w_up), from_hbm(w_down), (slope if layer == 1 else from_hbm(slope)))


def place(sc, piece):
    return (piece % 2) ^ sc[Y], (piece // 2) ^ sc[Z]


def ffn_weight_body(
    sc, grad, grad_o, s2, s2_o, gain, shift, act, dh, w_up, b_up, w_down, keep, send, n_t, n_o, g_t, acts, dhs
):
    t = pl.program_id(0)
    core = sc[C]
    low, low_o = grad[0, :, 0].reshape(ROWS, D), grad_o[0, :, 0].reshape(ROWS, D)

    @pl.when(t == 0)
    def _():
        n_t[:, 0:ROWS] = norm_low(s2[...], gain[0], shift[0]).T
        other = norm_low(s2_o[...], gain[0], shift[0])
        n_o[...] = other
        n_t[:, ROWS : 2 * ROWS] = other.T
        x = sc[X]
        g_t[:, 0:ROWS] = jnp.where(x == 0, low[:, 0:HALF], low[:, HALF:D]).T
        g_t[:, ROWS : 2 * ROWS] = jnp.where(x == 0, low_o[:, 0:HALF], low_o[:, HALF:D]).T

    u = dot(n_o[...], w_up[0]) + b_up[0]
    acts[0:ROWS] = act[...]

    @pl.when(t < 2)
    def _():
        active_o, slope_o = gelu_parts(u)
        acts[ROWS : 2 * ROWS] = active_o.astype(BF)
        dhs[0:ROWS] = dh[...]
        dhs[ROWS : 2 * ROWS] = (dot_nt(low_o, w_down[0]) * slope_o).astype(BF)
        g_up = dot(n_t[...], dhs[...]).astype(BF)
        for ref, when in ((send, 0), (keep, 1)):

            @pl.when(t == when)
            def _():
                for piece in range(8):
                    py, pz = place(sc, piece)
                    for j in range(2):
                        ref[py, pz, j] = g_up[piece * PART : (piece + 1) * PART, j * HALF : (j + 1) * HALF]

    @pl.when(t >= 2)
    def _():
        acts[ROWS : 2 * ROWS] = gelu_parts(u)[0].astype(BF)

    g_down = dot(g_t[...], acts[...]).astype(BF).T
    tile = ffn_tile(t, sc)
    for half in range(2):
        py, pz = place(sc, 2 * tile + half)
        for j in range(2):
            first = g_down[half * HALF + j * PART : half * HALF + (j + 1) * PART]
            second = g_down[half * HALF + (j + 2) * PART : half * HALF + (j + 3) * PART]
            keep[py, pz, 2 + j] = jnp.where(core == 0, first, second)
            send[py, pz, 2 + j] = jnp.where(core == 0, second, first)


def ffn_tile(step, sc):
    mine = 2 * sc[X]
    rest = 2 - mine
    return jnp.where(step == 0, mine + 1 - sc[C], jnp.where(step == 1, mine + sc[C], rest + step - 2))


def ffn_weights(scalars, layer, grad, grad_spec, grad_o, grad_o_spec, s2, s2_o, act, dh, weights, deps=()):
    gain, shift, w_up, b_up, w_down = weights
    packed = (2, 4, 4, PART, HALF)
    return call(
        ffn_weight_body,
        (FF // BT,),
        [
            grad_spec,
            grad_o_spec,
            whole((ROWS, D)),
            whole((ROWS, D)),
            at_layer((1, 1, D), layer),
            at_layer((1, 1, D), layer),
            pl.BlockSpec((ROWS, BT), lambda i, sc: (0, ffn_tile(i, sc))),
            pl.BlockSpec((ROWS, BT), lambda i, sc: (0, ffn_tile(jnp.minimum(i, 1), sc))),
            pl.BlockSpec((1, D, BT), lambda i, sc: (layer, 0, ffn_tile(i, sc))),
            pl.BlockSpec((1, 1, BT), lambda i, sc: (layer, 0, ffn_tile(i, sc))),
            pl.BlockSpec((1, BT, D), lambda i, sc: (layer, ffn_tile(jnp.minimum(i, 1), sc), 0)),
        ],
        [whole(packed), whole(packed)],
        [stored(packed, BF), shape(packed, BF)],
        [
            pltpu.VMEM((D, 2 * ROWS), BF),
            pltpu.VMEM((ROWS, D), BF),
            pltpu.VMEM((HALF, 2 * ROWS), BF),
            pltpu.VMEM((2 * ROWS, BT), BF),
            pltpu.VMEM((2 * ROWS, BT), BF),
        ],
        (8.6e9, 22e6),
        deps,
    )(scalars, grad, grad_o, s2, s2_o, gain, shift, (act if layer == 1 else from_hbm(act)), dh, from_hbm(w_up), b_up, from_hbm(w_down))


def attn_back_body(
    layer, sc, gr_own, gr_rcv, qkv, ctx, lse, ep, w_out, weights, d_qkv, part_own, part_oth, bias, d_ctx, delta, d_k, d_v,
    sides, sems
):
    core = sc[C]
    copies = weight_copies(layer, core, weights, sides, sems)
    for copy in copies:
        copy.start()
    grad_rows = jnp.concatenate([in_order(gr_own, gr_rcv, b, core) for b in range(4)])
    d_ctx[...] = dot_nt(grad_rows, w_out[0]).astype(BF)
    product = d_ctx[...].astype(F32) * ctx[...].astype(F32)
    high = product.astype(BF)
    rest = (product - high.astype(F32)).astype(BF)
    picks = (
        lax.broadcasted_iota(jnp.int32, (8, HALF), 0) == lax.broadcasted_iota(jnp.int32, (8, HALF), 1) // HEAD_DIM
    ).astype(BF)
    delta[...] = dot_nt(picks, high) + dot_nt(picks, rest)
    ep_row, ep_col = episode_columns(ep)
    for i in range(4):
        lo, hi = first_key(i), (i + 1) * BLOCK
        key_at = lo + lax.broadcasted_iota(jnp.int32, (hi - lo, BLOCK), 0)
        row_at = i * BLOCK + lax.broadcasted_iota(jnp.int32, (hi - lo, BLOCK), 1)
        same = ep_col[lo:hi, 0:1] == ep_row[0:1, i * BLOCK : hi]
        bias[i, 0 : hi - lo, :] = jnp.where((key_at <= row_at) & same, 0.0, MASKED)

    @pl.loop(0, 3)
    def _(p):
        at = pl.multiple_of(p * PAIR, PAIR)
        d_k[...] = jnp.zeros_like(d_k)
        d_v[...] = jnp.zeros_like(d_v)
        for i in range(4):
            lo, hi = first_key(i), (i + 1) * BLOCK
            rows = slice(i * BLOCK, hi)
            q = qkv[rows, pl.ds(at, PAIR)]
            k = qkv[lo:hi, pl.ds(HALF + at, PAIR)]
            v = qkv[lo:hi, pl.ds(2 * HALF + at, PAIR)]
            dc = d_ctx[rows, pl.ds(at, PAIR)]
            d_q = jnp.zeros((BLOCK, PAIR), F32)
            for h in range(2):

                def only(array):
                    lane = lax.broadcasted_iota(jnp.int32, array.shape, 1)
                    mine = (lane >= HEAD_DIM) if h else (lane < HEAD_DIM)
                    return jnp.where(mine, array, jnp.zeros_like(array))

                q_h, dc_h = only(q), only(dc)
                s = dot_nt(k, q_h) + bias[i, 0 : hi - lo, :]
                prob = jnp.exp(s - lse[pl.ds(2 * p + h, 1), rows])
                d_p = dot_nt(v, dc_h)
                d_s = (prob * (d_p - delta[pl.ds(2 * p + h, 1), rows])).astype(BF)
                d_v[lo:hi] += dot(prob.astype(BF), dc_h)
                d_k[lo:hi] += dot(d_s, q_h)
                d_q += dot_tn(d_s, only(k))
            d_qkv[rows, pl.ds(at, PAIR)] = (d_q * 0.125).astype(BF)
        d_qkv[:, pl.ds(HALF + at, PAIR)] = d_k[...].astype(BF)
        d_qkv[:, pl.ds(2 * HALF + at, PAIR)] = d_v[...].astype(BF)

    for copy in copies:
        copy.wait()
    parts = dot_nt(d_qkv[...], sides[...])
    for b in range(4):
        part = parts[b * BLOCK : (b + 1) * BLOCK]

        @pl.when(core == b % 2)
        def _():
            part_own[b // 2] = part

        @pl.when(core != b % 2)
        def _():
            part_oth[b // 2] = part.astype(BF)


def attention_backward(scalars, layer, gr_own, gr_rcv, qkv, ctx, lse, episodes, ep_spec, w_out, w_qkv, deps=()):
    block = whole((2, BLOCK, D))
    return call(
        partial(attn_back_body, layer),
        (1,),
        [
            block,
            block,
            whole((LENGTH, 3 * HALF)),
            whole((LENGTH, HALF)),
            whole((8, LENGTH)),
            ep_spec,
            pl.BlockSpec((1, HALF, D), lambda i, sc: (layer, sc[C], 0)),
            pl.BlockSpec(memory_space=pl.ANY),
        ],
        [whole((LENGTH, 3 * HALF)), block, block],
        [shape((LENGTH, 3 * HALF), BF), shape((2, BLOCK, D), F32), shape((2, BLOCK, D), BF)],
        [
            pltpu.VMEM((4, 3 * BLOCK, BLOCK), F32),
            pltpu.VMEM((LENGTH, HALF), BF),
            pltpu.VMEM((8, LENGTH), F32),
            pltpu.VMEM((LENGTH, PAIR), F32),
            pltpu.VMEM((LENGTH, PAIR), F32),
            pltpu.VMEM((D, 3 * HALF), BF),
            pltpu.SemaphoreType.DMA((3,)),
        ],
        (2.5e9 + 6e9, 12e6),
        deps,
    )(scalars, gr_own, gr_rcv, from_hbm(qkv), from_hbm(ctx), lse, episodes, from_hbm(w_out), from_hbm(w_qkv))


def attn_weight_body(
    z_first, sc, own, other, gain, shift, d_qkv, gr_own, gr_rcv, ctx_full, ctx_oth, ctx_rcv, keep, send, z_keep, z_send, n_t
):
    core, x = sc[C], sc[X]
    own, other = own.at[0, :, 0], other.at[0, :, 0]
    for b in range(4):
        rows = slice(b * BLOCK, (b + 1) * BLOCK)
        n_t[:, rows] = norm_low(in_order(own, other, b, core), gain[0], shift[0]).T

    def columns(ref):
        rows = ref[...].reshape(ROWS, D)
        return jnp.where(core == 0, rows[:, 0:HALF], rows[:, HALF:D]).T

    def grad(j):
        return dot(n_t[...], d_qkv[:, j * HALF : (j + 1) * HALF]).astype(BF)

    first, second = grad(0), grad(2)
    mine, yours = jnp.where(x == 0, first, second), jnp.where(x == 0, second, first)
    for piece in range(8):
        py, pz = place(sc, piece)
        keep[py, pz] = mine[piece * PART : (piece + 1) * PART]
        send[py, pz] = yours[piece * PART : (piece + 1) * PART]

    a, b = ctx_oth[...].reshape(ROWS, HALF), ctx_rcv[...].reshape(ROWS, HALF)
    far = jnp.concatenate([jnp.where(core == 0, a, b), jnp.where(core == 0, b, a)], 1)
    g_out = (dot(columns(gr_own), ctx_full[...]) + dot(columns(gr_rcv), far)).astype(BF).T
    for j, rows in enumerate((grad(1), g_out)):
        for piece in range(8):
            py, pz = place(sc, piece)
            value = rows[piece * PART : (piece + 1) * PART]

            far = pz % 2 if z_first else py

            @pl.when(far == 0)
            def _():
                if z_first:
                    z_keep[pz // 2, py, j] = value
                else:
                    z_keep[pz, j] = value

            @pl.when(far == 1)
            def _():
                if z_first:
                    z_send[pz // 2, py, j] = value
                else:
                    z_send[pz, j] = value


def attention_weights(
    scalars, layer, own, own_spec, other, other_spec, gain, shift, d_qkv, gr_own, gr_rcv, ctx_full, ctx_oth, ctx_rcv, deps=()
):
    z_first = layer == 1
    packed, z_packed = (2, 4, PART, HALF), ((2, 2) if z_first else (4,)) + (2, PART, HALF)
    block = whole((2, BLOCK, D))
    return call(
        partial(attn_weight_body, z_first),
        (1,),
        [
            own_spec,
            other_spec,
            at_layer((1, 1, D), layer),
            at_layer((1, 1, D), layer),
            whole((LENGTH, 3 * HALF)),
            block,
            block,
            whole((ROWS, D)),
            whole((2, BLOCK, HALF)),
            whole((2, BLOCK, HALF)),
        ],
        [whole(packed), whole(packed), whole(z_packed), whole(z_packed)],
        [stored(packed, BF), shape(packed, BF), stored(z_packed, BF), shape(z_packed, BF)],
        [pltpu.VMEM((D, LENGTH), BF)],
        (2.5e9, 12e6),
        deps,
    )(scalars, own, other, gain, shift, d_qkv, gr_own, gr_rcv, ctx_full, ctx_oth, ctx_rcv)


def to_core(value):
    return lax.ppermute(value, "section", [(0, 1), (1, 0), (2, 3), (3, 2)])


def to_chip(value):
    return lax.ppermute(value, "section", [(0, 2), (2, 0), (1, 3), (3, 1)])


def to_dp(value, distance):
    return lax.ppermute(value, "dp", [(i, i ^ distance) for i in range(8)])


def total(*terms):
    out = terms[0].astype(F32)
    for term in terms[1:]:
        out = out + term.astype(F32)
    return out.astype(BF)


class Flat(list):
    pass


def combined(scalars, outputs, deps=(), pinned=()):
    terms, dims, dtypes = [], [], []

    def block_of(term):
        array, *index = term
        if index and isinstance(index[0], slice):
            count = index[0].stop - index[0].start
            return (count,) + array.shape[1:], (index[0].start // count,) + (0,) * (array.ndim - 1)
        rest = array.shape[len(index) :]
        return (None,) * len(index) + rest, tuple(index) + (0,) * len(rest)

    def dims_of(term):
        return tuple(d for d in block_of(term)[0] if d is not None)

    def rows_of(piece):
        found = dims_of(piece[0])
        return found[0] if len(found) == 3 else 1

    for pieces in outputs:
        rest = dims_of(pieces[0][0])
        if isinstance(pieces, Flat):
            dims.append((sum(rows_of(piece) for piece in pieces),) + rest[-2:])
        else:
            dims.append(((len(pieces),) if len(pieces) > 1 else ()) + rest)
        dtypes.append(pieces[0][0][0].dtype)
        terms += [term for piece in pieces for term in piece]

    def spec(term):
        block, index = block_of(term)
        return pl.BlockSpec(block, lambda i, sc: index)

    def body(sc, *refs):
        given = iter(refs[: len(terms)])
        for out, pieces in zip(refs[len(terms) :], outputs):
            at = 0
            for n, piece in enumerate(pieces):
                value = next(given)[...].astype(F32)
                for _ in piece[1:]:
                    value = value + next(given)[...].astype(F32)
                value = value.astype(out.dtype)
                if isinstance(pieces, Flat):
                    rows = rows_of(piece)
                    if len(value.shape) == 3:
                        out[at : at + rows] = value
                    else:
                        out[at] = value
                    at += rows
                elif len(pieces) > 1:
                    out[n] = value
                else:
                    out[...] = value

    return call(
        body,
        (1,),
        [spec(term) for term in terms],
        [whole(d) for d in dims],
        [shape(d, t) for d, t in zip(dims, dtypes)],
        [],
        (1e10, 1e7),
        deps,
    )(scalars, *[from_hbm(term[0]) if any(term[0] is a for a in pinned) else term[0] for term in terms])


def in_dp_order(both):
    return jnp.moveaxis(both, 0, 1).reshape((8,) + both.shape[2:])


def gathered(share):
    far, near = to_chip(share), to_core(share)
    return share, far, near, to_core(far)


def ffn_unpacked(sc, shares, up, down):
    for n in range(4):
        x, core = sc[X] ^ (n % 2), sc[C] ^ (n // 2)
        for j in range(2):
            at = pl.multiple_of(x * 4 * HALF + core * 2 * HALF + j * HALF, PAIR)
            up[0, :, pl.ds(at, HALF)] = shares[n][j].astype(F32)
            rows = pl.ds(pl.multiple_of(core * 2 * PART + j * PART, 8), PART)
            down[0, rows, pl.ds(pl.multiple_of(x * HALF, PAIR), HALF)] = shares[n][2 + j].astype(F32)


def unpack_early_body(sc, final_keep, final_got, input_keep, input_got, *refs):
    final, inputs, up, down = refs[-4:]
    x = sc[X]
    for ref, mine, got in ((final, final_keep, final_got), (inputs, input_keep, input_got)):
        ref[x, 0] = mine[...]
        ref[1 - x, 0] = got[...].astype(F32)
    ffn_unpacked(sc, refs[:4], up, down)


def unpack_body(shares, sc, small, up_before, down_before, *refs):
    up, down, qkv, out, a_gain, a_shift, b_out, f_gain, f_shift, b_down, b_up = refs[-11:]
    ffn_unpacked(sc, refs[:4], up, down)
    for layer in range(2):
        qv, ko = shares[layer]
        for n in range(4):
            x, core = sc[X] ^ (n % 2), sc[C] ^ (n // 2)
            index, at = qv[n]
            qkv[layer, :, pl.ds(pl.multiple_of(x * 2 * D + core * HALF, PAIR), HALF)] = refs[index][at].astype(F32)
        for n in range(2):
            side = pl.multiple_of((sc[C] ^ n) * HALF, PAIR)
            qkv[layer, :, pl.ds(pl.multiple_of(D + side, PAIR), HALF)] = refs[ko[n]][0].astype(F32)
            out[layer, :, pl.ds(side, HALF)] = refs[ko[n]][1].astype(F32)
    piece = 2 * sc[Z] + sc[Y]
    mine = jnp.zeros((32, PART), F32)
    for d in range(8):
        mine = jnp.where(piece == d, small[:, d * PART : (d + 1) * PART], mine)
    for layer in range(2):
        for j, (a_ref, f_ref) in enumerate(((a_gain, f_gain), (a_shift, f_shift), (b_out, b_down))):
            a_ref[layer : layer + 1] = mine[8 * layer + j : 8 * layer + j + 1]
            f_ref[layer : layer + 1] = mine[16 + 8 * layer + j : 16 + 8 * layer + j + 1]
        row = jnp.zeros((1, 4 * PART), F32)
        for d in range(8):
            at = 16 + 8 * layer + 4 + d // 2
            row = jnp.where(piece == d, small[at : at + 1, (d % 2) * HALF : (d % 2 + 1) * HALF], row)
        b_up[layer : layer + 1] = row


FFN_GRADS = ((2, PART, FF), (2, 4 * PART, D))


def unpacked_early(scalars, rows, arrays, layer):
    moved = ((2, 1, BLOCK, D),) * 2
    return call(
        unpack_early_body,
        (1,),
        [whole((BLOCK, D))] * 4 + [whole(array.shape) for array in arrays],
        [whole(d) for d in moved] + [at_layer((1,) + d[1:], layer) for d in FFN_GRADS],
        [shape(d, F32) for d in moved] + [stored(d, F32) for d in FFN_GRADS],
        [],
        (1e6, 9e6),
    )(scalars, *rows, *arrays)


def unpacked(scalars, small, up, down, arrays, shares):
    dims = ((2, PART, 3 * D), (2, PART, D)) + ((2, PART),) * 6 + ((2, 4 * PART),)
    held = pl.BlockSpec(memory_space=pl.ANY)
    return call(
        partial(unpack_body, shares),
        (1,),
        [whole((32, D)), held, held] + [whole(array.shape) for array in arrays],
        [at_layer((1,) + d[1:], 0) for d in FFN_GRADS] + [whole(d) for d in dims],
        [stored(d, F32) for d in FFN_GRADS] + [shape(d, F32) for d in dims],
        [],
        (1e6, 11e6),
        aliases={2: 0, 3: 1},
    )(scalars, small, from_hbm(up), from_hbm(down), *arrays)


def on_device(
    tokens,
    episodes,
    attn_gain,
    attn_shift,
    qkv_weight,
    out_weight,
    out_bias,
    ffn_gain,
    ffn_shift,
    up_weight,
    up_bias,
    down_weight,
    down_bias,
    cotangent,
):
    replicas = lax.axis_size("dp")
    section = lax.axis_index("section")
    replica = lax.axis_index("dp")
    chip, core = section // 2, section % 2
    direct = replicas == 8
    y, z = (replica % 2, replica // 2) if direct else (0, 0)
    scalars = jnp.stack([jnp.asarray(v, jnp.int32) for v in (chip, core, y, z)])

    stream = tokens.reshape(2, 2, 2, BLOCK, D)
    cot = cotangent.reshape(2, 2, 2, BLOCK, D)
    eps = episodes.reshape(2, 1, LENGTH)
    ep_spec = pl.BlockSpec((1, 1, LENGTH), lambda i, sc: (sc[X], 0, 0))

    def input_spec(micro, side):
        return pl.BlockSpec((1, 2, 1, BLOCK, D), lambda i, sc: (micro(sc[X]), 0, side(sc[C]), 0, 0))

    same, flip = (lambda v: v), (lambda v: 1 - v)
    own_in, other_in, far_in = input_spec(same, same), input_spec(same, flip), input_spec(flip, same)
    local = pl.BlockSpec((1, 2, 1, BLOCK, D), lambda i, sc: (0, 0, 0, 0, 0))

    def rows5(value):
        return value.reshape(1, 2, 1, BLOCK, D)

    def vec(array):
        return array.reshape(2, 1, -1)

    a_gain, a_shift, b_out = vec(attn_gain), vec(attn_shift), vec(out_bias)
    f_gain, f_shift, b_up, b_down = vec(ffn_gain), vec(ffn_shift), vec(up_bias), vec(down_bias)

    kept = []
    own, own_spec, other, other_spec = stream, own_in, stream, other_in
    for layer in range(2):
        seen = (own, own_spec, other, other_spec)
        if layer == 0:
            seen = (from_hbm(own), own_spec, from_hbm(other), other_spec)
        qkv, ctx, ctx_own, ctx_oth, lse = attention_forward(
            scalars, layer, *seen, eps, ep_spec, a_gain, a_shift, qkv_weight
        )
        ctx_rcv = to_core(ctx_oth)
        ctx_far = to_core(ctx_own)
        ffn = (f_gain, f_shift, up_weight, b_up, down_weight, b_down)
        if layer == 0:
            s2, ctx_full, act, slope, *result = ffn_forward(
                scalars, layer, ctx_own, ctx_rcv, own, own_spec, (out_weight, b_out) + ffn, ()
            )
            s2_o = to_chip(s2)
        else:
            s2, ctx_full = projected(
                scalars, layer, ctx_own, ctx_rcv, own, own_spec, out_weight, b_out, (kept[0][7], kept[0][11])
            )
            s2_o = to_chip(s2)
            act, slope, *result = last_ffn_forward(scalars, layer, s2, ffn)
        kept.append((own, own_spec, other, other_spec, qkv, ctx, ctx_oth, ctx_far, ctx_full, lse, s2, s2_o, act, slope))
        if layer == 0:
            s3 = result[0]
            own, own_spec, other, other_spec = rows5(s3), local, rows5(to_core(s3)), local
    final_keep, final_send = result

    def ffn_back(layer, grad, grad_spec, deps=()):
        kept_now = kept[layer]
        s2, slope = kept_now[10], kept_now[13]
        return ffn_backward(scalars, layer, grad, grad_spec, s2, slope, (f_gain, up_weight, down_weight), deps)

    def ffn_grads(layer, grad, grad_spec, grad_o, grad_o_spec, dh, deps=()):
        s2, s2_o, act, slope = kept[layer][10:]
        weights = (f_gain, f_shift, up_weight, b_up, down_weight)
        return ffn_weights(
            scalars, layer, grad, grad_spec, grad_o, grad_o_spec, s2, s2_o, act, dh, weights, deps
        )

    def attn_back(layer, ds, ds_rcv, deps=()):
        own, own_spec, other, other_spec, qkv, ctx, ctx_oth, ctx_far, ctx_full, lse = kept[layer][:10]
        return attention_backward(
            scalars, layer, ds, ds_rcv, qkv, ctx, lse, eps, ep_spec, out_weight, qkv_weight, deps
        )

    def attn_grads(layer, ds, ds_rcv, d_qkv, deps=()):
        own, own_spec, other, other_spec, qkv, ctx, ctx_oth, ctx_far, ctx_full, lse = kept[layer][:10]
        return attention_weights(
            scalars, layer, own, own_spec, other, other_spec, a_gain, a_shift, d_qkv, ds, ds_rcv, ctx_full, ctx_oth,
            ctx_far, deps,
        )

    def attn_norm(layer, ds, part_own, part_rcv, smalls=(), deps=()):
        own, own_spec = kept[layer][:2]
        return attention_norm_back(scalars, layer, ds, part_own, part_rcv, own, own_spec, a_gain, smalls, deps)

    if direct:
        pinned = []

        def summed(*outputs, deps=()):
            return combined(scalars, outputs, deps, pinned)

        def y_sum(keep, got):
            return [[(keep, 1), (got, 1)]]

        def z_sum(keep, got, y_got):
            return [[(keep, 0, k), (got, 0, k), (y_got, k)] for k in (1, 3)]

        def far_sum(keep, got, y_got, z_got):
            return [[(keep, 0, 2), (got, 0, 2), (y_got, 2), (z_got, 1)]]

        def share(keep, got, y_got, z_got, far_got):
            return [[(keep, 0, 0), (got, 0, 0), (y_got, 0), (z_got, 0), (far_got,)]]

        dh1, ds1, f_small1 = ffn_back(1, cot, own_in, [kept[1][7]])
        ds1_rcv = to_core(ds1)
        fk1, send = ffn_grads(1, cot, own_in, cot, far_in, dh1)
        pinned.append(fk1)
        fg1 = to_core(send)
        d_qkv1, part1, part1_oth = attn_back(1, ds1, ds1_rcv, [from_hbm(fk1)])
        part1_rcv = to_core(part1_oth)
        value, final_low = summed(y_sum(fk1, fg1), [[(final_send,)]], deps=[part1])
        fy1 = to_dp(value, 1)
        g0, a_small1 = attn_norm(1, ds1, part1, part1_rcv, deps=[value])
        g0_o = to_chip(g0)
        dh0, ds0, f_small0 = ffn_back(0, rows5(g0), local)
        ds0_rcv = to_core(ds0)
        qk1, send, ok1, z_send = attn_grads(1, ds1, ds1_rcv, d_qkv1, [ds0])
        pinned += [qk1, ok1]
        qg1, og1 = to_chip(send), to_dp(z_send, 2)
        fk0, send = ffn_grads(0, rows5(g0), local, rows5(g0_o), local, dh0, [from_hbm(qk1)])
        pinned.append(fk0)
        fg0 = to_core(send)
        (fz1,) = summed(z_sum(fk1, fg1, fy1), deps=[from_hbm(fk0)])
        fy0, final_low = summed(y_sum(fk0, fg0), [[(final_low,)]], deps=[fz1])
        d_qkv0, part0, part0_oth = attn_back(0, ds0, ds0_rcv, [fy0])
        final_got = to_chip(final_low)
        fz1, fy0 = to_dp(fz1, 2), to_dp(fy0, 1)
        part0_rcv = to_core(part0_oth)
        far1, y1 = summed(
            far_sum(fk1, fg1, fy1, fz1),
            Flat([[(ok1, 0, 1), (og1, 0, 1)], [(ok1, 1, 1), (og1, 1, 1)]] + y_sum(qk1, qg1)),
            deps=[part0],
        )
        input_keep, input_send, small = attn_norm(
            0, ds0, part0, part0_rcv, (a_small1, f_small0, f_small1), [far1, final_got]
        )
        far1, y1 = to_dp(far1, 4), to_dp(y1, 1)
        small_got = to_core(small)
        input_got = to_chip(input_send)
        fz0, small = summed(z_sum(fk0, fg0, fy0), [[(small,), (small_got,)]], deps=[input_keep])
        qk0, send, ok0, y_send = attn_grads(0, ds0, ds0_rcv, d_qkv0, [fz0])
        fz0, small_got = to_dp(fz0, 2), to_dp(small, 4)
        pinned += [qk0, ok0]
        qg0, oy0 = to_chip(send), to_dp(y_send, 1)

        far, qz1, f1, small = summed(
            Flat(far_sum(fk0, fg0, fy0, fz0) + [[(ok1, 1, 0), (og1, 1, 0), (y1, slice(2, 4))]]),
            [[(qk1, 0, k), (qg1, 0, k), (y1, 4 + k)] for k in (1, 3)],
            share(fk1, fg1, fy1, fz1, far1),
            [[(small,), (small_got,)]],
            deps=[from_hbm(qk0)],
        )
        far, qz1, small_got = to_dp(far, 4), to_dp(qz1, 2), to_dp(small, 1)
        f1_all = gathered(f1)

        qy0, oz0, qf1, small = summed(
            y_sum(qk0, qg0),
            [[(ok0, k), (oy0, k)] for k in (1, 3)],
            [[(qk1, 0, 2), (qg1, 0, 2), (y1, 6), (qz1, 1)]],
            [[(small,), (small_got,)]],
            deps=[input_got],
        )
        qy0, oz0, qf1, small_got = to_dp(qy0, 1), to_dp(oz0, 2), to_dp(qf1, 4), to_chip(small)

        of0, qz0, f0, ox1, small = summed(
            [[(ok0, 2), (oy0, 2), (oz0, 1)]],
            z_sum(qk0, qg0, qy0),
            [[(fk0, 0, 0), (fg0, 0, 0), (fy0, 0), (fz0, 0), (far, slice(0, 4))]],
            [[(ok1, 0, 0), (og1, 0, 0), (y1, slice(0, 2)), (far, slice(4, 6))]],
            [[(small,), (small_got,)]],
            deps=f1_all[1:],
        )
        of0, qz0, ox1_got, small_got = to_dp(of0, 4), to_dp(qz0, 2), to_chip(ox1), to_dp(small, 2)
        f0_all = gathered(f0)

        qf0, ox0, o1, small = summed(
            far_sum(qk0, qg0, qy0, qz0),
            [[(ok0, 0), (oy0, 0), (oz0, 0), (of0,)]],
            [[(ox1,), (ox1_got,)]],
            [[(small,), (small_got,)]],
        )
        qf0, ox0_got = to_dp(qf0, 4), to_chip(ox0)

        final_out, input_out, ups, downs = unpacked_early(
            scalars, (final_keep, final_got, input_keep, input_got), f1_all, 1
        )
        both, o0 = summed(
            share(qk0, qg0, qy0, qz0, qf0) + [[(qk1, 0, 0), (qg1, 0, 0), (y1, 4), (qz1, 0), (qf1,)]],
            [[(ox0,), (ox0_got,)]],
            deps=f0_all[1:] + (from_hbm(ups),),
        )
        arrays = f0_all + gathered(both) + (o0, to_core(o0), o1, to_core(o1))
        shares = ((tuple((n, 0) for n in range(4, 8)), (8, 9)), (tuple((n, 1) for n in range(4, 8)), (10, 11)))
        (ups, downs, qkvs, outs, *vectors) = unpacked(scalars, small, ups, downs, arrays, shares)
        g_a_gain, g_a_shift, g_b_out, g_f_gain, g_f_shift, g_b_down, g_b_up = vectors
    else:
        final_got = to_chip(final_send)
        grads = [None, None]
        grad, grad_spec, grad_o, grad_o_spec = cot, own_in, cot, far_in
        for layer in (1, 0):
            dh, ds, f_small = ffn_back(layer, grad, grad_spec)
            ds_rcv = to_core(ds)
            f_keep, f_send = ffn_grads(layer, grad, grad_spec, grad_o, grad_o_spec, dh)
            d_qkv, part_own, part_oth = attn_back(layer, ds, ds_rcv)
            keep, send, z_keep, z_send = attn_grads(layer, ds, ds_rcv, d_qkv)
            if layer == 1:
                g0, a_small1 = attn_norm(1, ds, part_own, to_core(part_oth))
                grad, grad_spec, grad_o, grad_o_spec = rows5(g0), local, rows5(to_chip(g0)), local
                f_small1 = f_small
            else:
                input_keep, input_send, small = attn_norm(
                    0, ds, part_own, to_core(part_oth), (a_small1, f_small, f_small1)
                )
            ffn = in_dp_order(total(f_keep, to_core(f_send)))
            qv = in_dp_order(total(keep, to_chip(send)))
            ko = jnp.stack([z_keep, z_send], 1).reshape(8, 2, PART, HALF)
            ko = total(ko, to_chip(ko))
            ordered = []
            for mine, far, near, both in (gathered(ffn), gathered(qv)):
                here = jnp.stack([jnp.where(chip == 0, mine, far), jnp.where(chip == 0, far, mine)])
                there = jnp.stack([jnp.where(chip == 0, near, both), jnp.where(chip == 0, both, near)])
                pair = jnp.stack([jnp.where(core == 0, here, there), jnp.where(core == 0, there, here)], 1)
                ordered.append(pair.astype(F32))
            ko_other = to_core(ko)
            ko_all = jnp.stack([jnp.where(core == 0, ko, ko_other), jnp.where(core == 0, ko_other, ko)]).astype(F32)
            f_all, qv_all = ordered
            up = f_all[:, :, :, 0:2].transpose(2, 4, 0, 1, 3, 5).reshape(D, FF)
            down = f_all[:, :, :, 2:4].transpose(2, 1, 3, 4, 0, 5).reshape(FF, D)
            q, v = (qv_all[n].transpose(1, 2, 0, 3).reshape(D, D) for n in range(2))
            k, out = (ko_all[:, :, n].transpose(1, 2, 0, 3).reshape(D, D) for n in range(2))
            grads[layer] = [
                lax.psum_scatter(array, "dp", scatter_dimension=0, tiled=True)
                for array in (up, down, jnp.concatenate([q, k, v], 1), out)
            ]
        ups, downs, qkvs, outs = (jnp.stack(pair) for pair in zip(*grads))
        small = lax.psum(small, ("section", "dp")).reshape(4, 8, D)

        def mine_of(rows):
            width = rows.shape[-1] // replicas
            return lax.dynamic_slice_in_dim(rows, replica * width, width, 1)

        g_a_gain, g_a_shift, g_b_out = (mine_of(small[0:2, n]) for n in range(3))
        g_f_gain, g_f_shift, g_b_down = (mine_of(small[2:4, n]) for n in range(3))
        g_b_up = mine_of(small[2:4, 4:8].reshape(2, FF))

        def placed(keep, got):
            got = got.astype(F32)
            return jnp.stack([jnp.where(chip == 0, keep, got), jnp.where(chip == 0, got, keep)])[:, None]

        final_out, input_out = placed(final_keep, final_got), placed(input_keep, to_chip(input_send))

    return (
        final_out,
        input_out,
        g_a_gain,
        g_a_shift,
        qkvs,
        outs,
        g_b_out,
        g_f_gain,
        g_f_shift,
        ups,
        g_b_up,
        downs,
        g_b_down,
    )


def solution(mesh):
    split = P(None, "dp", None, None)
    placed = (split, P(None, "dp", None)) + (P(),) * 11 + (split,)
    rows = P(None, "dp", "section", None)
    vector, matrix = P(None, "dp"), P(None, "dp", None)
    return jax.shard_map(
        on_device,
        mesh=mesh,
        in_specs=placed,
        out_specs=(
            rows,
            rows,
            vector,
            vector,
            matrix,
            matrix,
            vector,
            vector,
            vector,
            matrix,
            vector,
            matrix,
            vector,
        ),
        check_vma=False,
    )
```
